32 devices in a mesh: dp: 4 (over z), seq: 8 (over y, x, core).
Axes of the slice: x: 2, y: 2, z: 4, core: 2. Of those that a mesh axis runs over, the one named last changes fastest.
Arguments:
- features: bfloat16 [4, 8, 128, 2560], P('dp', None, 'seq'), may hold values from -6 to 6
- frozen_query_weight: bfloat16 [4, 8, 128, 1024], P('dp', None, 'seq'), may hold values from -100 to 100
- source_keys: bfloat16 [4, 8, 128, 1024], P('dp', None, 'seq'), may hold values from -6 to 6
- source_values: bfloat16 [4, 8, 128, 1024], P('dp', None, 'seq'), may hold values from -6 to 6
- output_gradient: bfloat16 [4, 8, 128, 1024], P('dp', None, 'seq'), may hold values from -6 to 6
- adapter_down_weight: bfloat16 [2560, 64], replicated, may hold values from -0.125 to 0.125
- adapter_up_weight: bfloat16 [64, 1024], replicated, may hold values from -0.75 to 0.75
- source_block_plan: int32 [4, 8], replicated, may hold values from 0 to 31, as said below
- segments: int32 [4, 1024], P('dp'), may hold values from 0 to 1, never falling along the last dimension, each value on 1 to 640 neighbouring positions
Outputs:
- down_grad: float32 [2560, 64], P('seq')
- up_grad: float32 [64, 1024], P(None, 'seq')
- log_norm: float32 [4, 8, 1024], P('dp', 'seq')
The draws below stay inside these ranges and needn't reach their ends.
Inputs may be any that keep to these rules, and one draw needn't show every extreme that they name: `source_block_plan`: each entry names a source block as group * 8 + block; every source block is named exactly once; from one group to another group at most 2 blocks go, and some pairs of groups carry exactly 2. Within a group the segment numbers never fall and all 2 segments occur; a segment spans at most 640 positions.
All inputs are finite; a program needn't handle non-finite values.
Results may differ from the reference program's by a relative error of at most 0.0087.
Values may be sent and summed in bfloat16 or wider, within the bound.
No kernel may reach another device: no remote copies, remote signals or barrier semaphores. Data moves between devices by JAX's collectives and lax.ppermute only.
A program may use at most 64 MiB of HBM per device.

```python
import math
import jax
import jax.numpy as jnp
import numpy as np
from jax import lax

INPUT_FEATURES = 2560
HEAD_SIZE = 128
ADAPTER_RANK = 64
BLOCK = 128
CAP = 2
CLIPS = 2
HEAD_TOTAL = 8
GROUPS = 4
BLOCKS = 8
LENGTH = 1024
SEG_MOST = 640
SHIFTS = 3


def shared_keys(key):
    return jnp.clip(jax.random.normal(key, (GROUPS * BLOCKS * BLOCK, HEAD_TOTAL * HEAD_SIZE), jnp.float32), -5.0, 5.0)


def draw_source_keys(key, part):
    common = shared_keys(key)
    return common.reshape(GROUPS, BLOCKS, BLOCK, HEAD_TOTAL * HEAD_SIZE).astype(jnp.bfloat16)


def draw_frozen_query_weight(key, part):
    common = shared_keys(key)
    key = jax.random.fold_in(key, 7)
    result = jnp.clip(jax.random.normal(key, common.shape, jnp.float32), -5.0, 5.0)
    return result.reshape(GROUPS, BLOCKS, BLOCK, HEAD_TOTAL * HEAD_SIZE).astype(jnp.bfloat16)


def draw_source_block_plan(key, part):
    key = jax.random.fold_in(key, 5)
    key_shift, key_order = jax.random.split(key)
    shifts = jax.random.permutation(key_shift, GROUPS - 1)[:SHIFTS] + 1
    orders = jax.vmap(lambda subkey: jax.random.permutation(subkey, BLOCKS))(jax.random.split(key_order, GROUPS))
    moved = orders[:, :SHIFTS * CAP].reshape(GROUPS, SHIFTS, CAP)
    group_ids = jnp.arange(GROUPS, dtype=jnp.int32)
    source_group = (group_ids[:, None] - shifts[None, :]) % GROUPS
    source_block = moved[source_group, jnp.arange(SHIFTS)[None, :], :]
    plan = group_ids[:, None] * BLOCKS + jnp.arange(BLOCKS, dtype=jnp.int32)[None, :]
    row_ids = jnp.broadcast_to(group_ids[:, None, None], moved.shape)
    entries = source_group[:, :, None] * BLOCKS + source_block
    return plan.at[row_ids, moved].set(entries).astype(jnp.int32)


def level_of(key, shape, pieces, smallest, largest):
    def one(dim, blocks):
        heights = jax.random.uniform(jax.random.fold_in(jax.random.fold_in(key, 6), dim), (blocks,), jnp.float32, smallest / len(pieces), largest / len(pieces))
        return jnp.repeat(jnp.exp(heights), shape[dim] // blocks).reshape((-1,) + (1,) * (len(shape) - dim - 1))

    loudness = one(*pieces[0])
    for cut in pieces[1:]:
        loudness = loudness * one(*cut)
    return loudness


def profile(amount, total, limit, skew):
    loads = [(1 << 20) // math.isqrt(grade ** skew) + 1 for grade in range(2, amount + 1)]
    spare, given = total - limit - (amount - 1), [1] * (amount - 1)
    while spare > 0:
        candidates = [i for i in range(amount - 1) if given[i] < limit]
        mass, left = sum([loads[i] for i in candidates]), spare
        for i in candidates:
            addition = min(limit - given[i], max(1, left * loads[i] // mass), spare)
            given[i] = given[i] + addition
            spare = spare - addition
    return np.array([limit] + given)


def ragged_sizes(key, count, total, reach, lean):
    if count == 2:
        one = jax.random.randint(key, (), max(1, total - reach), min(reach, total - 1) + 1)
        return jnp.stack([one, total - one])
    sizes = jnp.asarray(profile(count, total, reach, lean), jnp.int32)
    pairs = (count - 1) // 2
    source_of, receiver = sizes[1:1 + 2 * pairs:2], sizes[2:2 + 2 * pairs:2]
    room = jnp.minimum(source_of - 1, reach - receiver)
    passed = jax.random.randint(jax.random.fold_in(key, 1), (pairs,), 0, 1 << 20) % (room + 1)
    sizes = sizes.at[1:1 + 2 * pairs:2].set(source_of - passed).at[2:2 + 2 * pairs:2].set(receiver + passed)
    return sizes[jax.random.permutation(jax.random.fold_in(key, 2), count)]


def gaussian(stream_key, shape, scale, limit, cuts=(), kind=jnp.bfloat16):
    drawn = jax.random.normal(stream_key, shape, jnp.float32) * scale
    if len(cuts) > 0:
        drawn = level_of(stream_key, shape, cuts, -0.22, 0.18) * drawn
    return jnp.clip(drawn, min=-limit, max=limit).astype(kind)


def setup_inputs(seed: int = 0) -> dict:
    keys = jax.random.split(jax.random.key(seed), 10)
    features = gaussian(keys[0], (GROUPS, BLOCKS, BLOCK, INPUT_FEATURES), 1.0, 6.0, ((0, 4), (2, 8)))
    frozen_query_weight = draw_frozen_query_weight(jax.random.fold_in(keys[9], 71), 0)
    source_keys = draw_source_keys(jax.random.fold_in(keys[9], 71), 0)
    source_values = gaussian(keys[3], (GROUPS, BLOCKS, BLOCK, HEAD_TOTAL * HEAD_SIZE), 1.0, 6.0, ((0, 4), (2, 8)))
    output_gradient = gaussian(keys[4], (GROUPS, BLOCKS, BLOCK, HEAD_TOTAL * HEAD_SIZE), 1.0, 6.0, ((0, 4), (2, 8)))
    adapter_down_weight = gaussian(keys[5], (INPUT_FEATURES, ADAPTER_RANK), INPUT_FEATURES ** -0.5, 0.125)
    adapter_up_weight = gaussian(keys[6], (ADAPTER_RANK, HEAD_TOTAL * HEAD_SIZE), ADAPTER_RANK ** -0.5, 0.75)
    source_block_plan = draw_source_block_plan(jax.random.fold_in(keys[9], 71), 0)
    segments = jax.vmap(lambda own: jnp.searchsorted(jnp.cumsum(ragged_sizes(own, CLIPS, LENGTH, SEG_MOST, 1)), jnp.arange(LENGTH), side="right"))(jax.random.split(keys[8], GROUPS)).reshape((GROUPS, LENGTH)).astype(jnp.int32)
    return {"features": features, "frozen_query_weight": frozen_query_weight, "source_keys": source_keys, "source_values": source_values, "output_gradient": output_gradient, "adapter_down_weight": adapter_down_weight, "adapter_up_weight": adapter_up_weight, "source_block_plan": source_block_plan, "segments": segments}


def attend_head(query, key_rows, value_rows, cotangent, segment, clip_count, reach_rows):
    length = query.shape[0]
    width = query.shape[1]
    piece_count = 8
    piece_rows = reach_rows // piece_count
    scaling = 1.0 / math.sqrt(width)
    query_padded = jnp.pad(query, ((0, reach_rows), (0, 0)))
    grad_padded = jnp.pad(cotangent, ((0, reach_rows), (0, 0)))
    keys_padded = jnp.pad(key_rows, ((0, reach_rows), (0, 0)))
    values_padded = jnp.pad(value_rows, ((0, reach_rows), (0, 0)))
    segment_padded = jnp.pad(segment, (0, reach_rows), constant_values=-1)
    clip_ids = jnp.arange(clip_count, dtype=jnp.int32)
    starts = lax.optimization_barrier(jnp.sum((segment[None, :] < clip_ids[:, None]).astype(jnp.int32), axis=1)).astype(jnp.int32)

    def piece_pass(piece_index):
        clip_slice = piece_index // piece_count
        start = lax.dynamic_index_in_dim(starts, clip_slice, 0, keepdims=False).astype(jnp.int32)
        query_start = (start + piece_index % piece_count * piece_rows).astype(jnp.int32)
        query_tile = lax.dynamic_slice_in_dim(query_padded, query_start, piece_rows, 0)
        grad_tile = lax.dynamic_slice_in_dim(grad_padded, query_start, piece_rows, 0)
        seg_tile = lax.dynamic_slice_in_dim(segment_padded, query_start, piece_rows, 0)
        key_tile = lax.dynamic_slice_in_dim(keys_padded, start, reach_rows, 0)
        value_tile = lax.dynamic_slice_in_dim(values_padded, start, reach_rows, 0)
        seg_cols = lax.dynamic_slice_in_dim(segment_padded, start, reach_rows, 0)
        in_clip = seg_tile == clip_slice
        allowed = in_clip[:, None] & (seg_cols == clip_slice)[None, :]
        scores = lax.dot_general(query_tile, key_tile, (((1,), (1,)), ((), ())), preferred_element_type=jnp.float32) * scaling
        scores = jnp.where(allowed, scores, -1e+30)
        maximum = lax.optimization_barrier(jnp.max(scores, axis=1, keepdims=True))
        exponent = jnp.where(allowed, jnp.exp(scores - maximum), 0.0)
        totals = jnp.where(in_clip[:, None], lax.optimization_barrier(jnp.sum(exponent, axis=1, keepdims=True)), 1.0)
        log_norm = jnp.where(in_clip, maximum[:, 0] + jnp.log(totals[:, 0]), 0.0)
        probs = exponent / totals
        weights = probs.astype(jnp.bfloat16)
        attended = jnp.dot(weights, value_tile, preferred_element_type=jnp.float32)
        delta = lax.optimization_barrier(jnp.sum(grad_tile.astype(jnp.float32) * attended, axis=1, keepdims=True))
        dprob = lax.dot_general(grad_tile, value_tile, (((1,), (1,)), ((), ())), preferred_element_type=jnp.float32)
        dscore = (probs * (dprob - delta)).astype(jnp.bfloat16)
        query_gradient = (jnp.dot(dscore, key_tile, preferred_element_type=jnp.float32) * scaling).astype(jnp.bfloat16)
        query_gradient = jnp.where(in_clip[:, None], query_gradient, jnp.zeros((), jnp.bfloat16))
        return (query_gradient, log_norm, query_start)
    total_pieces = piece_count * (clip_count - 1)
    dquery_pieces, log_pieces, piece_starts = lax.map(piece_pass, jnp.arange(total_pieces, dtype=jnp.int32))

    def place(index, carry):
        grad_total, log_total = carry
        where_at = lax.dynamic_index_in_dim(piece_starts, index, 0, keepdims=False).astype(jnp.int32)
        grad_piece = lax.dynamic_index_in_dim(dquery_pieces, index, 0, keepdims=False)
        log_piece = lax.dynamic_index_in_dim(log_pieces, index, 0, keepdims=False)
        grad_old = lax.dynamic_slice_in_dim(grad_total, where_at, piece_rows, 0)
        log_old = lax.dynamic_slice_in_dim(log_total, where_at, piece_rows, 0)
        grad_total = lax.dynamic_update_slice_in_dim(grad_total, grad_old + grad_piece, where_at, 0)
        log_total = lax.dynamic_update_slice_in_dim(log_total, log_old + log_piece, where_at, 0)
        return (grad_total, log_total)
    grad_init = jnp.zeros((length + reach_rows, width), jnp.bfloat16)
    log_init = jnp.zeros((length + reach_rows,), jnp.float32)
    grad_total, log_total = lax.fori_loop(0, total_pieces, place, (grad_init, log_init))
    return (grad_total[:length], log_total[:length])

def reorder(source, source_block_plan):
    flat = source.reshape(GROUPS * BLOCKS, BLOCK, source.shape[-1])
    moved = jnp.take(flat, source_block_plan.reshape(-1).astype(jnp.int32), axis=0)
    return moved.reshape(GROUPS * BLOCKS * BLOCK, source.shape[-1])

def reference(features, frozen_query_weight, source_keys, source_values, output_gradient, adapter_down_weight, adapter_up_weight, source_block_plan, segments):
    width = HEAD_TOTAL * HEAD_SIZE
    feature_dest = reorder(features, source_block_plan)
    base_query_dest = reorder(frozen_query_weight, source_block_plan)
    keys_dest = reorder(source_keys, source_block_plan)
    values_dest = reorder(source_values, source_block_plan)
    grads_dest = output_gradient.reshape(GROUPS * LENGTH, width)
    adapter_params = jnp.dot(feature_dest, adapter_down_weight, preferred_element_type=jnp.float32).astype(jnp.bfloat16)
    query_rows = (base_query_dest.astype(jnp.float32) + jnp.dot(adapter_params, adapter_up_weight, preferred_element_type=jnp.float32)).astype(jnp.bfloat16)

    def group_pass(group_data):
        query_group, key_group, value_group, grad_group, seg_group = group_data

        def head_pass(head_index):

            def columns(array):
                return lax.dynamic_slice_in_dim(array, head_index * HEAD_SIZE, HEAD_SIZE, 1)
            return attend_head(columns(query_group), columns(key_group), columns(value_group), columns(grad_group), seg_group, CLIPS, SEG_MOST)
        return lax.map(head_pass, jnp.arange(HEAD_TOTAL, dtype=jnp.int32))
    query_gradient, log_norm = lax.map(group_pass, (query_rows.reshape(GROUPS, LENGTH, width), keys_dest.reshape(GROUPS, LENGTH, width), values_dest.reshape(GROUPS, LENGTH, width), grads_dest.reshape(GROUPS, LENGTH, width), segments))
    query_gradient = jnp.transpose(query_gradient, (0, 2, 1, 3)).reshape(GROUPS * LENGTH, width)
    adapter_gradient = lax.dot_general(query_gradient, adapter_up_weight, (((1,), (1,)), ((), ())), preferred_element_type=jnp.float32).astype(jnp.bfloat16)
    grad_norm = 4.0 / math.sqrt(GROUPS * LENGTH)
    up_grad = grad_norm * lax.dot_general(adapter_params, query_gradient, (((0,), (0,)), ((), ())), preferred_element_type=jnp.float32)
    down_grad = grad_norm * lax.dot_general(feature_dest, adapter_gradient, (((0,), (0,)), ((), ())), preferred_element_type=jnp.float32)
    return (down_grad, up_grad, log_norm)
```

```python
import functools
import math

import jax
import jax.numpy as jnp
from jax import lax
from jax.experimental import pallas as pl
from jax.experimental.pallas import tpu as pltpu
from jax.sharding import PartitionSpec as P

CAP = 2
CLIPS = 2
LANES = 128
HALF = 64
CORES = 2
LOG2E = math.log2(math.e)
VMEM = pl.BlockSpec(memory_space=pltpu.VMEM)
SMEM = pl.BlockSpec(memory_space=pltpu.SMEM)
ANY = pl.BlockSpec(memory_space=pl.ANY)
NT = (((1,), (1,)), ((), ()))


def low_lanes(rows):
    return lax.broadcasted_iota(jnp.int32, (rows, LANES), 1) < HALF


def swap_halves(tile):
    return pltpu.roll(tile, HALF, 1)


def lane_tile(index):
    return pl.ds(pl.multiple_of(index * LANES, LANES), LANES)


def row_tile(index, rows):
    return pl.ds(pl.multiple_of(index * rows, rows), rows)


def quotient(value, size):
    return lax.shift_right_logical(value, size.bit_length() - 1)


def remainder(value, size):
    return value & (size - 1)


def each_hit(plan, me, groups, blocks, live, put):
    def over_dest(dest, _):
        def over_position(position, slot):
            source = plan[dest, position]
            hit = quotient(source, blocks) == me

            @pl.when(hit)
            def _():
                put(dest, slot, remainder(source, blocks))

            return slot + hit.astype(jnp.int32)

        lax.fori_loop(0, live, over_position, jnp.int32(0))
        return 0

    lax.fori_loop(0, groups, over_dest, 0)


def each_block(plan, me, blocks, live, take):
    def over_position(position, _):
        group = quotient(plan[me, position], blocks)
        slot = jnp.int32(0)
        for other in range(live):
            same = (quotient(plan[me, other], blocks) == group) & (other < position)
            slot = slot + same.astype(jnp.int32)
        take(position, group, slot)
        return 0

    lax.fori_loop(0, live, over_position, 0)


def each_half(slot, store):
    @pl.when(remainder(slot, 2) == 0)
    def _():
        store(slice(0, HALF))

    @pl.when(remainder(slot, 2) == 1)
    def _():
        store(slice(HALF, LANES))


def split(slot, pair):
    pair = pair.astype(jnp.float32)
    return jnp.where(remainder(slot, 2) == 0, pair, swap_halves(pair))


def pack_far_kernel(dims, plan_hbm, feat_hbm, base_hbm, keys_hbm, vals_hbm, down_hbm, up_hbm, *rest):
    groups, blocks, heads, rows, live = dims
    far_hbm, qbuf, abuf = rest[:3]
    plan, feat, base, keys, vals, down, up, far_out, sems, out_sems = rest[3:]
    me = lax.axis_index("dp")
    copies = [
        pltpu.make_async_copy(source, target, sems.at[index])
        for index, (source, target) in enumerate(
            (
                (plan_hbm, plan),
                (keys_hbm, keys),
                (vals_hbm, vals),
                (feat_hbm, feat),
                (down_hbm, down),
                (base_hbm, base),
                (up_hbm, up),
            )
        )
    ]
    for copy in copies:
        copy.start()

    def put_blocks(sources, first):
        def put(dest, slot, local):
            @pl.when(slot < CAP)
            def _():
                for head in range(heads):
                    columns = slice(head * LANES, (head + 1) * LANES)
                    for index, source in enumerate(sources):
                        far_out[head * groups + dest, (first + index) * CAP + slot] = source[
                            local, :, columns
                        ]

        each_hit(plan, me, groups, blocks, live, put)

    def send(first, count, index):
        tiles = pl.ds(first, count)
        copy = pltpu.make_async_copy(far_out.at[:, tiles], far_hbm.at[:, tiles], out_sems.at[index])
        copy.start()
        return copy

    for copy in copies[:3]:
        copy.wait()
    put_blocks((keys, vals), 0)
    early = send(0, 2 * CAP, 0)
    for copy in copies[3:]:
        copy.wait()
    rank = up.shape[0]
    twice = jnp.concatenate([down[...], down[...]], axis=0)
    adapter = lax.dot_general(feat[...], twice, NT, preferred_element_type=jnp.float32).astype(
        jnp.bfloat16
    )
    abuf[...] = adapter.reshape(abuf.shape)
    lift = jnp.dot(adapter[:, :rank], up[...], preferred_element_type=jnp.float32)
    qbuf[...] = (base[...].astype(jnp.float32) + lift.reshape(base.shape)).astype(jnp.bfloat16)

    def put_adapter(dest, slot, local):
        def store(lanes):
            for head in range(heads):
                far_out[head * groups + dest, CAP * 3, :, lanes] = abuf[local, :, lanes]

        @pl.when(slot < CAP)
        def _():
            each_half(slot, store)

    each_hit(plan, me, groups, blocks, live, put_adapter)
    put_blocks((qbuf,), 2)
    late = send(2 * CAP, CAP + 1, 1)
    early.wait()
    late.wait()


def pack_own_kernel(dims, plan, keys, vals, grad, queries, adapter, *own_outs):
    groups, blocks, heads, rows, live = dims
    extras = live - CAP
    me = lax.axis_index("dp")
    seq = lax.axis_index("seq")
    sources = (keys, vals, queries)

    def put(dest, slot, local):
        @pl.when(slot >= CAP)
        def _():
            extra = slot - CAP
            where = extras * 3 + live + quotient(extra, 2)
            for turn in range(heads):
                columns = lane_tile(seq ^ turn)
                for index, source in enumerate(sources):
                    own_outs[turn][index * extras + extra] = source[local, :, columns]

            def store(lanes):
                for turn in range(heads):
                    own_outs[turn][where, :, lanes] = adapter[local, :, lanes]

            each_half(slot, store)

    each_hit(plan, me, groups, blocks, live, put)
    for turn in range(heads):
        columns = lane_tile(seq ^ turn)
        for position in range(live):
            own_outs[turn][extras * 3 + position] = grad[position, :, columns]


def attend_kernel(dims, plan, seg, up, far_in, *rest):
    groups, blocks, heads, rows, live = dims
    own_ins = rest[:heads]
    part_out = rest[heads]
    own_parts = rest[heads + 1 : heads + 1 + heads // CORES]
    up_out, log_out, qs, ks, vs, gs, ads, dqs, parts = rest[heads + 1 + heads // CORES :]
    extras = live - CAP
    me = lax.axis_index("dp")
    seq = lax.axis_index("seq")
    rank = up.shape[0]
    length = seg.shape[1]
    reach = live * LANES
    scaling = 1.0 / math.sqrt(LANES)

    ads[...] = jnp.zeros_like(ads)

    def take(position, group, slot):
        far = (group != me) | (slot < CAP)

        @pl.when(far)
        def _():
            for part in range(heads):
                index = part * groups + group
                where = row_tile(position * heads + part, rows)
                ks[where, :] = far_in[index, slot]
                vs[where, :] = far_in[index, CAP + slot]
                qs[where, :] = far_in[index, 2 * CAP + slot]

            def store(lanes):
                for part in range(heads):
                    where = row_tile(position * heads + part, rows)
                    ads[where, lanes] = far_in[part * groups + group, CAP * 3, :, lanes]

            each_half(slot, store)

        @pl.when(jnp.logical_not(far))
        def _():
            extra = slot - CAP
            pair = extras * 3 + live + quotient(extra, 2)
            for turn in range(heads):
                where = row_tile(position * heads + (seq ^ turn), rows)
                ks[where, :] = own_ins[turn][extra]
                vs[where, :] = own_ins[turn][extras + extra]
                qs[where, :] = own_ins[turn][2 * extras + extra]

            def store(lanes):
                for turn in range(heads):
                    where = row_tile(position * heads + (seq ^ turn), rows)
                    ads[where, lanes] = own_ins[turn][pair, :, lanes]

            each_half(slot, store)

    each_block(plan, me, blocks, live, take)
    for turn in range(heads):
        for position in range(live):
            gs[row_tile(position * heads + (seq ^ turn), rows), :] = own_ins[turn][
                extras * 3 + position
            ]

    count = jnp.sum((seg[...] < CLIPS - 1).astype(jnp.float32), axis=1, keepdims=True).astype(
        jnp.int32
    )
    key_rows = ks[...]
    value_rows = vs[...]
    key_columns = key_rows.T
    key_index = lax.broadcasted_iota(jnp.int32, (reach, 1), 0)
    always = length - reach
    up_head = up[:, lane_tile(seq)]
    up_twice = jnp.concatenate([up_head, up_head], axis=0)
    for start in range(0, reach, 2 * LANES):
        count_here = min(2 * LANES, reach - start)
        span = slice(start, start + count_here)
        scores = lax.dot_general(key_rows, qs[span, :], NT, preferred_element_type=jnp.float32)
        scores = jnp.concatenate(
            [
                scores[:always],
                jnp.where(key_index[always:] < count, scores[always:], -1e30),
            ],
            axis=0,
        )
        dprob = lax.dot_general(value_rows, gs[span, :], NT, preferred_element_type=jnp.float32)
        maximum = jnp.max(scores, axis=0, keepdims=True)
        exponent = jnp.exp2((scores - maximum) * (scaling * LOG2E))
        total = jnp.sum(exponent, axis=0, keepdims=True)
        delta = jnp.sum(exponent * dprob, axis=0, keepdims=True) / total
        dscore = (exponent * (dprob - delta)).astype(jnp.bfloat16)
        dquery = jnp.dot(key_columns, dscore, preferred_element_type=jnp.float32)
        query_index = lax.broadcasted_iota(jnp.int32, (1, count_here), 1) + start
        in_clip = query_index < count
        dquery = jnp.where(in_clip, dquery * (scaling / total), 0.0).astype(jnp.bfloat16)
        dqs[:, span] = dquery
        log_out[0, :, span] = jnp.where(in_clip, maximum * scaling + jnp.log(total), 0.0)
    log_out[0, :, reach:] = jnp.zeros((1, length - reach), jnp.float32)
    dquery_all = dqs[...]
    parts[...] = lax.dot_general(
        dquery_all, up_twice, (((0,), (1,)), ((), ())), preferred_element_type=jnp.float32
    ).astype(jnp.bfloat16)

    def put(position, group, slot):
        far = (group != me) | (slot < CAP)

        @pl.when(far)
        def _():
            def store(lanes):
                for part in range(heads):
                    where = row_tile(position * heads + part, rows)
                    part_out[part * groups + group, :, lanes] = parts[where, lanes]

            each_half(slot, store)

        @pl.when(jnp.logical_not(far))
        def _():
            pair = quotient(slot - CAP, 2)

            def store(lanes):
                for turn in range(heads):
                    where = row_tile(position * heads + (seq ^ turn), rows)
                    own_parts[turn // CORES][turn % CORES, pair, :, lanes] = parts[where, lanes]

            each_half(slot, store)

    each_block(plan, me, blocks, live, put)
    up_part = jnp.dot(dquery_all, ads[...], preferred_element_type=jnp.float32)
    up_out[...] = (up_part + swap_halves(up_part)).T[:rank].astype(jnp.bfloat16)


def chip_sum_kernel(*refs):
    parts, outs = refs[:-CORES], refs[-CORES:]
    for core in range(CORES):
        total = parts[0][core].astype(jnp.float32)
        for part in parts[1:]:
            total = total + part[core].astype(jnp.float32)
        outs[core][...] = total.astype(jnp.bfloat16)


def product_kernel(dims, plan, parts, feat, own_mine, own_other, out, sums, grads):
    groups, blocks, heads, rows, live = dims
    me = lax.axis_index("dp")
    for group in range(groups):
        total = parts[group].astype(jnp.float32)
        for head in range(1, heads):
            total = total + parts[head * groups + group].astype(jnp.float32)
        sums[group] = total
    for pair in range(own_mine.shape[0]):
        sums[groups + pair] = own_mine[pair].astype(jnp.float32) + own_other[pair].astype(
            jnp.float32
        )
    grads[...] = jnp.zeros_like(grads)

    def put(dest, slot, local):
        index = jnp.where(slot < CAP, dest, groups - 1 + quotient(slot, 2))
        grads[local] = split(slot, sums[index]).astype(jnp.bfloat16)

    each_hit(plan, me, groups, blocks, live, put)
    low = low_lanes(HALF // 2)
    columns = grads[...].reshape(blocks * rows, LANES).astype(jnp.float32).T[:HALF]
    columns = columns.astype(jnp.bfloat16)
    for pair in range(heads // 2):
        tiles = jnp.dot(
            columns,
            feat[:, pair * 5 * LANES : (pair + 1) * 5 * LANES],
            preferred_element_type=jnp.float32,
        )
        shared = tiles[:, 2 * LANES : 3 * LANES]
        upper, lower = shared[: HALF // 2], shared[HALF // 2 :]
        for part in range(2):
            ahead = tiles[:, part * 3 * LANES : (part * 3 + 2) * LANES].astype(jnp.bfloat16)
            out[pair * 2 + part, :HALF] = ahead[:, :LANES]
            out[pair * 2 + part, HALF : 2 * HALF] = ahead[:, LANES:]
            if part == 0:
                rest = jnp.where(low, upper, swap_halves(lower))
            else:
                rest = jnp.where(low, swap_halves(upper), lower)
            out[pair * 2 + part, 2 * HALF :] = rest.astype(jnp.bfloat16)


def join_kernel(parts, up_part, out):
    total = parts[0].astype(jnp.float32)
    for head in range(1, parts.shape[0]):
        total = total + parts[head].astype(jnp.float32)
    out[: total.shape[0]] = total.astype(jnp.bfloat16)
    out[total.shape[0] :] = up_part[...]


def total_kernel(grad_norm, *rest):
    groups = len(rest) - 3
    down_out, up_out, held = rest[groups:]
    me = lax.axis_index("dp")
    seq = lax.axis_index("seq")
    for turn in range(groups):
        held[me ^ turn] = rest[turn][...].astype(jnp.float32)
    total = held[0]
    for group in range(1, groups):
        total = total + held[group]
    total = total * grad_norm
    first, second = total[:HALF], total[HALF : 2 * HALF]
    shared = total[2 * HALF : 2 * HALF + HALF // 2]
    up_out[...] = total[2 * HALF + HALF // 2 :]
    swapped = swap_halves(shared)
    low_half = jnp.concatenate([shared, swapped], axis=0)
    high_half = jnp.concatenate([swapped, shared], axis=0)
    even = jnp.concatenate([first, second, low_half], axis=1)
    odd = pltpu.roll(jnp.concatenate([first, second, high_half], axis=1), HALF, 1)
    down = jnp.where(remainder(seq, 2) == 0, even, odd)
    down_out[...] = down[:, : down_out.shape[1]]


def call(kernel, outs, specs, scratch, flops, moved, *args, vmem_mib=32, out_specs=None):
    shapes = [jax.ShapeDtypeStruct(shape, dtype) for shape, dtype in outs]
    return pl.pallas_call(
        kernel,
        out_shape=shapes,
        in_specs=specs,
        out_specs=out_specs or [VMEM] * len(shapes),
        scratch_shapes=scratch,
        compiler_params=pltpu.CompilerParams(vmem_limit_bytes=vmem_mib << 20),
        cost_estimate=pl.CostEstimate(flops=flops, bytes_accessed=moved, transcendentals=0),
    )(*args)


def exchange(value, axis, turn):
    peers = lax.axis_size(axis)
    return lax.ppermute(value, axis, [(peer, peer ^ turn) for peer in range(peers)])


def per_device_tiles(
    features,
    frozen_query_weight,
    source_keys,
    source_values,
    output_gradient,
    adapter_down_weight,
    adapter_up_weight,
    source_block_plan,
    segments,
):
    groups = lax.axis_size("dp")
    heads = lax.axis_size("seq")
    _, blocks, rows, width = features.shape
    length = segments.shape[1]
    live = (length // 2 + length // 8) // LANES
    reach = live * LANES
    rank = adapter_up_weight.shape[0]
    extras = live - CAP
    pairs = (extras + 1) // 2
    dims = (groups, blocks, heads, rows, live)
    bf16 = jnp.bfloat16
    f32 = jnp.float32
    peers = groups * heads
    everyone = ("seq", "dp")
    flat = features[0].reshape(blocks * rows, width)
    far_shape = (peers, CAP * 3 + 1, rows, LANES)
    own_shape = (extras * 3 + live + pairs, rows, LANES)
    rows_shape = (blocks, rows, heads * LANES)

    far_send, queries, adapter = call(
        functools.partial(pack_far_kernel, dims),
        [(far_shape, bf16), (rows_shape, bf16), ((blocks, rows, LANES), bf16)],
        [ANY] * 7,
        [
            pltpu.SMEM((groups, blocks), jnp.int32),
            pltpu.VMEM((blocks * rows, width), bf16),
            pltpu.VMEM(rows_shape, bf16),
            pltpu.VMEM(rows_shape, bf16),
            pltpu.VMEM(rows_shape, bf16),
            pltpu.VMEM((rank, width), bf16),
            pltpu.VMEM((rank, heads * LANES), bf16),
            pltpu.VMEM(far_shape, bf16),
            pltpu.SemaphoreType.DMA((7,)),
            pltpu.SemaphoreType.DMA((2,)),
        ],
        60_000_000,
        4_000_000,
        source_block_plan,
        flat,
        frozen_query_weight[0],
        source_keys[0],
        source_values[0],
        adapter_down_weight.T,
        adapter_up_weight,
        vmem_mib=60,
        out_specs=[ANY, VMEM, VMEM],
    )
    own_send = call(
        functools.partial(pack_own_kernel, dims),
        [(own_shape, bf16)] * heads,
        [SMEM] + [VMEM] * 5,
        [],
        0,
        1_600_000,
        source_block_plan,
        source_keys[0],
        source_values[0],
        output_gradient[0],
        queries,
        adapter,
    )
    own = [own_send[0]] + [exchange(own_send[turn], "seq", turn) for turn in range(1, heads)]
    far = lax.all_to_all(far_send, everyone, 0, 0, tiled=True)
    attended = call(
        functools.partial(attend_kernel, dims),
        [((peers, rows, LANES), bf16)]
        + [((CORES, pairs, rows, LANES), bf16)] * (heads // CORES)
        + [((rank, LANES), bf16), ((1, 1, length), f32)],
        [SMEM] + [VMEM] * (3 + heads),
        [pltpu.VMEM((reach, LANES), bf16)] * 5
        + [pltpu.VMEM((LANES, reach), bf16), pltpu.VMEM((reach, LANES), bf16)],
        600_000_000,
        3_000_000,
        source_block_plan,
        segments,
        adapter_up_weight,
        far,
        *own,
    )
    own_parts = [
        exchange(attended[1 + chip], "seq", chip * CORES) for chip in range(heads // CORES - 1, 0, -1)
    ]
    own_mine, own_other = call(
        chip_sum_kernel,
        [((pairs, rows, LANES), bf16)] * CORES,
        [VMEM] * (heads // CORES),
        [],
        0,
        100_000,
        *own_parts,
        attended[1],
    )
    own_other = exchange(own_other, "seq", 1)
    part = lax.all_to_all(attended[0], everyone, 0, 0, tiled=True)
    up_part, log_norm = attended[1 + heads // CORES :]
    (shares,) = call(
        functools.partial(product_kernel, dims),
        [((heads, HALF * 5 // 2, LANES), bf16)],
        [SMEM] + [VMEM] * 4,
        [
            pltpu.VMEM((groups + pairs, rows, LANES), f32),
            pltpu.VMEM((blocks, rows, LANES), bf16),
        ],
        40_000_000,
        2_000_000,
        source_block_plan,
        part,
        flat,
        own_mine,
        own_other,
    )
    shares = lax.all_to_all(shares, "seq", 0, 0, tiled=True)
    (joined,) = call(
        join_kernel,
        [((HALF * 5 // 2 + rank, LANES), bf16)],
        [VMEM] * 2,
        [],
        0,
        600_000,
        shares,
        up_part,
    )
    sums = [joined] + [exchange(joined, "dp", turn) for turn in range(1, groups)]
    down, up = call(
        functools.partial(total_kernel, 4.0 / math.sqrt(groups * length)),
        [((rank, width // heads), f32), ((rank, LANES), f32)],
        [VMEM] * groups,
        [pltpu.VMEM((groups,) + joined.shape, f32)],
        0,
        400_000,
        *sums,
    )
    return (down.T, up, log_norm)


def power_of_two(size):
    return size > 1 and size & (size - 1) == 0


def fits_tiles(mesh, features, adapter_up_weight):
    groups, heads = mesh.shape["dp"], mesh.shape["seq"]
    rows = features.shape[2] // heads
    return (
        rows % 16 == 0
        and features.shape[2] == LANES
        and features.shape[3] * 2 == heads * 5 * LANES
        and power_of_two(heads)
        and power_of_two(groups)
        and power_of_two(features.shape[1])
        and adapter_up_weight.shape == (HALF, heads * LANES)
    )


def attend_head(query, key_rows, value_rows, cotangent, segment, clip_count, reach_rows):
    length = query.shape[0]
    width = query.shape[1]
    piece_count = 8
    piece_rows = reach_rows // piece_count
    scaling = 1.0 / math.sqrt(width)
    query_padded = jnp.pad(query, ((0, reach_rows), (0, 0)))
    grad_padded = jnp.pad(cotangent, ((0, reach_rows), (0, 0)))
    keys_padded = jnp.pad(key_rows, ((0, reach_rows), (0, 0)))
    values_padded = jnp.pad(value_rows, ((0, reach_rows), (0, 0)))
    segment_padded = jnp.pad(segment, (0, reach_rows), constant_values=-1)
    clip_ids = jnp.arange(clip_count, dtype=jnp.int32)
    starts = jnp.sum((segment[None, :] < clip_ids[:, None]).astype(jnp.int32), axis=1)

    def piece_pass(piece_index):
        clip_slice = piece_index // piece_count
        start = lax.dynamic_index_in_dim(starts, clip_slice, 0, keepdims=False)
        query_start = start + piece_index % piece_count * piece_rows
        query_tile = lax.dynamic_slice_in_dim(query_padded, query_start, piece_rows, 0)
        grad_tile = lax.dynamic_slice_in_dim(grad_padded, query_start, piece_rows, 0)
        seg_tile = lax.dynamic_slice_in_dim(segment_padded, query_start, piece_rows, 0)
        key_tile = lax.dynamic_slice_in_dim(keys_padded, start, reach_rows, 0)
        value_tile = lax.dynamic_slice_in_dim(values_padded, start, reach_rows, 0)
        seg_cols = lax.dynamic_slice_in_dim(segment_padded, start, reach_rows, 0)
        in_clip = seg_tile == clip_slice
        allowed = in_clip[:, None] & (seg_cols == clip_slice)[None, :]
        scores = (
            lax.dot_general(
                query_tile, key_tile, (((1,), (1,)), ((), ())), preferred_element_type=jnp.float32
            )
            * scaling
        )
        scores = jnp.where(allowed, scores, -1e30)
        maximum = jnp.max(scores, axis=1, keepdims=True)
        exponent = jnp.where(allowed, jnp.exp(scores - maximum), 0.0)
        totals = jnp.where(in_clip[:, None], jnp.sum(exponent, axis=1, keepdims=True), 1.0)
        log_norm = jnp.where(in_clip, maximum[:, 0] + jnp.log(totals[:, 0]), 0.0)
        probs = exponent / totals
        weights = probs.astype(jnp.bfloat16)
        attended = jnp.dot(weights, value_tile, preferred_element_type=jnp.float32)
        delta = jnp.sum(grad_tile.astype(jnp.float32) * attended, axis=1, keepdims=True)
        dprob = lax.dot_general(
            grad_tile, value_tile, (((1,), (1,)), ((), ())), preferred_element_type=jnp.float32
        )
        dscore = (probs * (dprob - delta)).astype(jnp.bfloat16)
        query_gradient = (
            jnp.dot(dscore, key_tile, preferred_element_type=jnp.float32) * scaling
        ).astype(jnp.bfloat16)
        query_gradient = jnp.where(in_clip[:, None], query_gradient, jnp.zeros((), jnp.bfloat16))
        return (query_gradient, log_norm, query_start)

    total_pieces = piece_count * (clip_count - 1)
    dquery_pieces, log_pieces, piece_starts = lax.map(
        piece_pass, jnp.arange(total_pieces, dtype=jnp.int32)
    )

    def place(index, carry):
        grad_total, log_total = carry
        where_at = lax.dynamic_index_in_dim(piece_starts, index, 0, keepdims=False)
        grad_piece = lax.dynamic_index_in_dim(dquery_pieces, index, 0, keepdims=False)
        log_piece = lax.dynamic_index_in_dim(log_pieces, index, 0, keepdims=False)
        grad_old = lax.dynamic_slice_in_dim(grad_total, where_at, piece_rows, 0)
        log_old = lax.dynamic_slice_in_dim(log_total, where_at, piece_rows, 0)
        grad_total = lax.dynamic_update_slice_in_dim(grad_total, grad_old + grad_piece, where_at, 0)
        log_total = lax.dynamic_update_slice_in_dim(log_total, log_old + log_piece, where_at, 0)
        return (grad_total, log_total)

    grad_init = jnp.zeros((length + reach_rows, width), jnp.bfloat16)
    log_init = jnp.zeros((length + reach_rows,), jnp.float32)
    grad_total, log_total = lax.fori_loop(0, total_pieces, place, (grad_init, log_init))
    return (grad_total[:length], log_total[:length])


def routing_tables(source_block_plan, group_index, cap_slots):
    group_count, block_count = source_block_plan.shape
    source_group = source_block_plan // block_count
    source_local = source_block_plan % block_count
    dest_groups = jnp.arange(group_count, dtype=jnp.int32)[:, None]
    outgoing = (source_group == group_index) & (dest_groups != group_index)
    out_rank = jnp.cumsum(outgoing.astype(jnp.int32), axis=1) - 1
    slot_ids = jnp.arange(cap_slots, dtype=jnp.int32)
    chosen = outgoing[:, :, None] & (out_rank[:, :, None] == slot_ids[None, None, :])
    send_index = jnp.sum(jnp.where(chosen, source_local[:, :, None], 0), axis=1)
    send_valid = jnp.any(chosen, axis=1)
    own_group = lax.dynamic_index_in_dim(source_group, group_index, 0, keepdims=False)
    own_local = lax.dynamic_index_in_dim(source_local, group_index, 0, keepdims=False)
    incoming = own_group != group_index
    positions = jnp.arange(block_count, dtype=jnp.int32)
    earlier = (own_group[None, :] == own_group[:, None]) & (positions[None, :] < positions[:, None])
    in_rank = jnp.sum(earlier.astype(jnp.int32), axis=1)
    return (send_index, send_valid, incoming, own_group, in_rank, own_local)


def pack_blocks(local, send_index, send_valid):
    picked = jnp.take(local, send_index, axis=0)
    return jnp.where(send_valid[:, :, None, None], picked, jnp.zeros((), local.dtype))


def unpack_blocks(received, local, tables, cap_slots):
    incoming, own_group, in_rank, own_local = tables
    flat = received.reshape((-1,) + received.shape[2:])
    slot_index = jnp.where(incoming, own_group * cap_slots + in_rank, 0)
    remote = jnp.take(flat, slot_index, axis=0)
    staying = jnp.take(local, own_local, axis=0)
    return jnp.where(incoming[:, None, None], remote, staying)


def per_device(
    features,
    frozen_query_weight,
    source_keys,
    source_values,
    output_gradient,
    adapter_down_weight,
    adapter_up_weight,
    source_block_plan,
    segments,
):
    group_count = lax.axis_size("dp")
    group_index = lax.axis_index("dp")
    block_count = features.shape[1]
    feat_local = features[0]
    base_local = frozen_query_weight[0]
    keys_local = source_keys[0]
    values_local = source_values[0]
    send_index, send_valid, incoming, own_group, in_rank, own_local = routing_tables(
        source_block_plan, group_index, CAP
    )
    tables = (incoming, own_group, in_rank, own_local)
    contract_final_axis = (((2,), (0,)), ((), ()))
    shuffled = (
        lax.all_to_all(
            pack_blocks(feat_local, send_index, send_valid),
            "dp",
            split_axis=0,
            concat_axis=0,
            tiled=True,
        ),
        lax.all_to_all(
            pack_blocks(base_local, send_index, send_valid),
            "dp",
            split_axis=0,
            concat_axis=0,
            tiled=True,
        ),
        lax.all_to_all(
            pack_blocks(keys_local, send_index, send_valid),
            "dp",
            split_axis=0,
            concat_axis=0,
            tiled=True,
        ),
        lax.all_to_all(
            pack_blocks(values_local, send_index, send_valid),
            "dp",
            split_axis=0,
            concat_axis=0,
            tiled=True,
        ),
    )
    feature_dest = unpack_blocks(shuffled[0], feat_local, tables, CAP)
    base_query_dest = unpack_blocks(shuffled[1], base_local, tables, CAP)
    keys_dest = unpack_blocks(shuffled[2], keys_local, tables, CAP)
    values_dest = unpack_blocks(shuffled[3], values_local, tables, CAP)
    adapter_params = lax.dot_general(
        feature_dest, adapter_down_weight, contract_final_axis, preferred_element_type=jnp.float32
    ).astype(jnp.bfloat16)
    query_rows = (
        base_query_dest.astype(jnp.float32)
        + lax.dot_general(
            adapter_params,
            adapter_up_weight,
            contract_final_axis,
            preferred_element_type=jnp.float32,
        )
    ).astype(jnp.bfloat16)
    head_query, head_keys, head_values, head_grads = (
        lax.all_to_all(query_rows, "seq", split_axis=2, concat_axis=1, tiled=True),
        lax.all_to_all(keys_dest, "seq", split_axis=2, concat_axis=1, tiled=True),
        lax.all_to_all(values_dest, "seq", split_axis=2, concat_axis=1, tiled=True),
        lax.all_to_all(output_gradient[0], "seq", split_axis=2, concat_axis=1, tiled=True),
    )
    length = head_query.shape[0] * head_query.shape[1]
    reach_rows = length // 2 + length // 8
    head_width = head_query.shape[2]
    segment = segments[0]
    head_query = head_query.reshape(length, head_width)
    head_keys = head_keys.reshape(length, head_width)
    head_values = head_values.reshape(length, head_width)
    head_grads = head_grads.reshape(length, head_width)
    dquery_head, log_head = attend_head(
        head_query, head_keys, head_values, head_grads, segment, CLIPS, reach_rows
    )
    norm_pieces = [log_head]
    log_norm = jnp.stack(norm_pieces, axis=0)
    query_gradient = lax.all_to_all(
        dquery_head.reshape(block_count, length // block_count, head_width),
        "seq",
        split_axis=1,
        concat_axis=2,
        tiled=True,
    )
    adapter_gradient = lax.dot_general(
        query_gradient,
        adapter_up_weight,
        (((2,), (1,)), ((), ())),
        preferred_element_type=jnp.float32,
    ).astype(jnp.bfloat16)
    contract_tokens = (((0, 1), (0, 1)), ((), ()))
    down_part = lax.dot_general(
        feature_dest, adapter_gradient, contract_tokens, preferred_element_type=jnp.float32
    )
    up_part = lax.dot_general(
        adapter_params, query_gradient, contract_tokens, preferred_element_type=jnp.float32
    )
    down_share, up_share = (
        lax.psum_scatter(down_part, "seq", scatter_dimension=0, tiled=True),
        lax.psum_scatter(up_part, "seq", scatter_dimension=1, tiled=True),
    )
    down_total, up_total = lax.psum((down_share, up_share), "dp")
    grad_norm = 4.0 / math.sqrt(group_count * length)
    return (down_total * grad_norm, up_total * grad_norm, log_norm[None])


def solution(mesh):
    in_specs = (
        P("dp", None, "seq", None),
        P("dp", None, "seq", None),
        P("dp", None, "seq", None),
        P("dp", None, "seq", None),
        P("dp", None, "seq", None),
        P(),
        P(),
        P(),
        P("dp", None),
    )
    out_specs = (P("seq", None), P(None, "seq"), P("dp", "seq", None))

    def whole(features, *rest):
        fits = fits_tiles(mesh, features, rest[5])
        return jax.shard_map(
            per_device_tiles if fits else per_device,
            mesh=mesh,
            in_specs=in_specs,
            out_specs=out_specs,
            check_vma=False,
        )(features, *rest)

    return whole
```

```python
import functools
import math

import jax
import jax.numpy as jnp
from jax import lax
from jax.experimental import pallas as pl
from jax.experimental.pallas import tpu as pltpu
from jax.sharding import PartitionSpec as P

CAP = 2
CLIPS = 2
LANES = 128
HALF = 64
CORES = 2
QUERIES = 640
LOG2E = math.log2(math.e)
VMEM = pl.BlockSpec(memory_space=pltpu.VMEM)
SMEM = pl.BlockSpec(memory_space=pltpu.SMEM)
ANY = pl.BlockSpec(memory_space=pl.ANY)
NT = (((1,), (1,)), ((), ()))


def low_lanes(rows):
    return lax.broadcasted_iota(jnp.int32, (rows, LANES), 1) < HALF


def swap_halves(tile):
    return pltpu.roll(tile, HALF, 1)


def lane_tile(index):
    return pl.ds(pl.multiple_of(index * LANES, LANES), LANES)


def row_tile(index, rows):
    return pl.ds(pl.multiple_of(index * rows, rows), rows)


def quotient(value, size):
    return lax.shift_right_logical(value, size.bit_length() - 1)


def remainder(value, size):
    return value & (size - 1)


def each_hit(plan, me, groups, blocks, live, put):
    def over_dest(dest, _):
        def over_position(position, slot):
            source = plan[dest, position]
            hit = quotient(source, blocks) == me

            @pl.when(hit)
            def _():
                put(dest, slot, remainder(source, blocks))

            return slot + hit.astype(jnp.int32)

        lax.fori_loop(0, live, over_position, jnp.int32(0))
        return 0

    lax.fori_loop(0, groups, over_dest, 0)


def each_block(plan, me, blocks, live, take):
    def over_position(position, _):
        group = quotient(plan[me, position], blocks)
        slot = jnp.int32(0)
        for other in range(live):
            same = (quotient(plan[me, other], blocks) == group) & (other < position)
            slot = slot + same.astype(jnp.int32)
        take(position, group, slot)
        return 0

    lax.fori_loop(0, live, over_position, 0)


def each_half(slot, store):
    @pl.when(remainder(slot, 2) == 0)
    def _():
        store(slice(0, HALF))

    @pl.when(remainder(slot, 2) == 1)
    def _():
        store(slice(HALF, LANES))


def split(slot, pair):
    pair = pair.astype(jnp.float32)
    return jnp.where(remainder(slot, 2) == 0, pair, swap_halves(pair))


def pack_far_kernel(dims, plan_hbm, feat_hbm, base_hbm, keys_hbm, vals_hbm, down_hbm, up_hbm, *rest):
    groups, blocks, heads, rows, live = dims
    far_hbm, qbuf, abuf = rest[:3]
    plan, feat, base, keys, vals, down, up, far_out, sems, out_sems = rest[3:]
    me = lax.axis_index("dp")
    copies = [
        pltpu.make_async_copy(source, target, sems.at[index])
        for index, (source, target) in enumerate(
            (
                (plan_hbm, plan),
                (keys_hbm, keys),
                (vals_hbm, vals),
                (feat_hbm, feat),
                (down_hbm, down),
                (base_hbm, base),
                (up_hbm, up),
            )
        )
    ]
    for copy in copies:
        copy.start()

    def put_blocks(sources, first):
        def put(dest, slot, local):
            @pl.when(slot < CAP)
            def _():
                for head in range(heads):
                    columns = slice(head * LANES, (head + 1) * LANES)
                    for index, source in enumerate(sources):
                        far_out[head * groups + dest, (first + index) * CAP + slot] = source[
                            local, :, columns
                        ]

        each_hit(plan, me, groups, blocks, live, put)

    def send(first, count, index):
        tiles = pl.ds(first, count)
        copy = pltpu.make_async_copy(far_out.at[:, tiles], far_hbm.at[:, tiles], out_sems.at[index])
        copy.start()
        return copy

    for copy in copies[:3]:
        copy.wait()
    put_blocks((keys, vals), 0)
    early = send(0, 2 * CAP, 0)
    for copy in copies[3:]:
        copy.wait()
    narrow = lax.dot_general(feat[...], down[...], NT, preferred_element_type=jnp.float32)
    adapter = narrow.astype(jnp.bfloat16)
    lift = jnp.dot(adapter, up[...], preferred_element_type=jnp.float32)
    abuf[...] = jnp.concatenate([narrow, narrow], axis=1).astype(jnp.bfloat16).reshape(abuf.shape)
    qbuf[...] = (base[...].astype(jnp.float32) + lift.reshape(base.shape)).astype(jnp.bfloat16)

    def put_adapter(dest, slot, local):
        def store(lanes):
            for head in range(heads):
                far_out[head * groups + dest, CAP * 3, :, lanes] = abuf[local, :, lanes]

        @pl.when(slot < CAP)
        def _():
            each_half(slot, store)

    each_hit(plan, me, groups, blocks, live, put_adapter)
    put_blocks((qbuf,), 2)
    late = send(2 * CAP, CAP + 1, 1)
    early.wait()
    late.wait()


def pack_own_kernel(dims, plan, keys, vals, grad, queries, adapter, *own_outs):
    groups, blocks, heads, rows, live = dims
    extras = live - CAP
    me = lax.axis_index("dp")
    seq = lax.axis_index("seq")
    sources = (keys, vals, queries)

    def put(dest, slot, local):
        @pl.when(slot >= CAP)
        def _():
            extra = slot - CAP
            where = extras * 3 + live + quotient(extra, 2)
            for turn in range(heads):
                columns = lane_tile(seq ^ turn)
                for index, source in enumerate(sources):
                    own_outs[turn][index * extras + extra] = source[local, :, columns]

            def store(lanes):
                for turn in range(heads):
                    own_outs[turn][where, :, lanes] = adapter[local, :, lanes]

            each_half(slot, store)

    each_hit(plan, me, groups, blocks, live, put)
    for turn in range(heads):
        columns = lane_tile(seq ^ turn)
        for position in range(live):
            own_outs[turn][extras * 3 + position] = grad[position, :, columns]


def attend_kernel(dims, plan, seg, up, far_in, *rest):
    groups, blocks, heads, rows, live = dims
    own_ins = rest[:heads]
    part_out = rest[heads]
    own_parts = rest[heads + 1 : heads + 1 + heads // CORES]
    up_out, log_out, qs, ks, vs, gs, ads, dqs, parts = rest[heads + 1 + heads // CORES :]
    extras = live - CAP
    me = lax.axis_index("dp")
    seq = lax.axis_index("seq")
    rank = up.shape[0]
    length = seg.shape[1]
    reach = live * LANES
    scaling = 1.0 / math.sqrt(LANES)

    ads[...] = jnp.zeros_like(ads)

    def take(position, group, slot):
        far = (group != me) | (slot < CAP)

        @pl.when(far)
        def _():
            for part in range(heads):
                index = part * groups + group
                where = row_tile(position * heads + part, rows)
                ks[where, :] = far_in[index, slot]
                vs[where, :] = far_in[index, CAP + slot]
                qs[where, :] = far_in[index, 2 * CAP + slot]

            def store(lanes):
                for part in range(heads):
                    where = row_tile(position * heads + part, rows)
                    ads[where, lanes] = far_in[part * groups + group, CAP * 3, :, lanes]

            each_half(slot, store)

        @pl.when(jnp.logical_not(far))
        def _():
            extra = slot - CAP
            pair = extras * 3 + live + quotient(extra, 2)
            for turn in range(heads):
                where = row_tile(position * heads + (seq ^ turn), rows)
                ks[where, :] = own_ins[turn][extra]
                vs[where, :] = own_ins[turn][extras + extra]
                qs[where, :] = own_ins[turn][2 * extras + extra]

            def store(lanes):
                for turn in range(heads):
                    where = row_tile(position * heads + (seq ^ turn), rows)
                    ads[where, lanes] = own_ins[turn][pair, :, lanes]

            each_half(slot, store)

    each_block(plan, me, blocks, live, take)
    for turn in range(heads):
        for position in range(live):
            gs[row_tile(position * heads + (seq ^ turn), rows), :] = own_ins[turn][
                extras * 3 + position
            ]

    count = jnp.sum((seg[...] < CLIPS - 1).astype(jnp.float32), axis=1, keepdims=True).astype(
        jnp.int32
    )
    key_rows = ks[...]
    value_rows = vs[...]
    key_columns = key_rows.T
    key_index = lax.broadcasted_iota(jnp.int32, (reach, 1), 0)
    always = length - reach
    up_head = up[:, lane_tile(seq)]
    up_twice = jnp.concatenate([up_head, up_head], axis=0)
    for start in range(0, reach, QUERIES):
        count_here = min(QUERIES, reach - start)
        span = slice(start, start + count_here)
        scores = lax.dot_general(key_rows, qs[span, :], NT, preferred_element_type=jnp.float32)
        scores = jnp.concatenate(
            [
                scores[:always],
                jnp.where(key_index[always:] < count, scores[always:], -1e30),
            ],
            axis=0,
        )
        dprob = lax.dot_general(value_rows, gs[span, :], NT, preferred_element_type=jnp.float32)
        maximum = jnp.max(scores, axis=0, keepdims=True)
        exponent = jnp.exp2((scores - maximum) * (scaling * LOG2E))
        total = jnp.sum(exponent, axis=0, keepdims=True)
        delta = jnp.sum(exponent * dprob, axis=0, keepdims=True) / total
        dscore = (exponent * (dprob - delta)).astype(jnp.bfloat16)
        dquery = jnp.dot(key_columns, dscore, preferred_element_type=jnp.float32)
        query_index = lax.broadcasted_iota(jnp.int32, (1, count_here), 1) + start
        in_clip = query_index < count
        dquery = jnp.where(in_clip, dquery * (scaling / total), 0.0).astype(jnp.bfloat16)
        dqs[:, span] = dquery
        log_out[0, :, span] = jnp.where(in_clip, maximum * scaling + jnp.log(total), 0.0)
    log_out[0, :, reach:] = jnp.zeros((1, length - reach), jnp.float32)
    dquery_all = dqs[...]
    parts[...] = lax.dot_general(
        dquery_all, up_twice, (((0,), (1,)), ((), ())), preferred_element_type=jnp.float32
    ).astype(jnp.bfloat16)

    def put(position, group, slot):
        far = (group != me) | (slot < CAP)

        @pl.when(far)
        def _():
            def store(lanes):
                for part in range(heads):
                    where = row_tile(position * heads + part, rows)
                    part_out[part * groups + group, :, lanes] = parts[where, lanes]

            each_half(slot, store)

        @pl.when(jnp.logical_not(far))
        def _():
            pair = quotient(slot - CAP, 2)

            def store(lanes):
                for turn in range(heads):
                    where = row_tile(position * heads + (seq ^ turn), rows)
                    own_parts[turn // CORES][turn % CORES, pair, :, lanes] = parts[where, lanes]

            each_half(slot, store)

    each_block(plan, me, blocks, live, put)
    up_part = jnp.dot(dquery_all, ads[...], preferred_element_type=jnp.float32)
    up_out[...] = (up_part + swap_halves(up_part)).T[:rank].astype(jnp.bfloat16)


def chip_sum_kernel(*refs):
    parts, outs = refs[:-CORES], refs[-CORES:]
    for core in range(CORES):
        total = parts[0][core].astype(jnp.float32)
        for part in parts[1:]:
            total = total + part[core].astype(jnp.float32)
        outs[core][...] = total.astype(jnp.bfloat16)


def product_kernel(dims, plan, parts, feat, own_mine, own_other, out, sums, grads):
    groups, blocks, heads, rows, live = dims
    me = lax.axis_index("dp")
    for group in range(groups):
        total = parts[group].astype(jnp.float32)
        for head in range(1, heads):
            total = total + parts[head * groups + group].astype(jnp.float32)
        sums[group] = total
    for pair in range(own_mine.shape[0]):
        sums[groups + pair] = own_mine[pair].astype(jnp.float32) + own_other[pair].astype(
            jnp.float32
        )
    grads[...] = jnp.zeros_like(grads)

    def put(dest, slot, local):
        index = jnp.where(slot < CAP, dest, groups - 1 + quotient(slot, 2))
        grads[local] = split(slot, sums[index]).astype(jnp.bfloat16)

    each_hit(plan, me, groups, blocks, live, put)
    low = low_lanes(HALF // 2)
    columns = grads[...].reshape(blocks * rows, LANES).astype(jnp.float32).T[:HALF]
    columns = columns.astype(jnp.bfloat16)
    for pair in range(heads // 2):
        tiles = jnp.dot(
            columns,
            feat[:, pair * 5 * LANES : (pair + 1) * 5 * LANES],
            preferred_element_type=jnp.float32,
        )
        shared = tiles[:, 2 * LANES : 3 * LANES]
        upper, lower = shared[: HALF // 2], shared[HALF // 2 :]
        for part in range(2):
            ahead = tiles[:, part * 3 * LANES : (part * 3 + 2) * LANES].astype(jnp.bfloat16)
            out[pair * 2 + part, :HALF] = ahead[:, :LANES]
            out[pair * 2 + part, HALF : 2 * HALF] = ahead[:, LANES:]
            if part == 0:
                rest = jnp.where(low, upper, swap_halves(lower))
            else:
                rest = jnp.where(low, swap_halves(upper), lower)
            out[pair * 2 + part, 2 * HALF :] = rest.astype(jnp.bfloat16)


def join_kernel(parts, up_part, out):
    total = parts[0].astype(jnp.float32)
    for head in range(1, parts.shape[0]):
        total = total + parts[head].astype(jnp.float32)
    out[: total.shape[0]] = total.astype(jnp.bfloat16)
    out[total.shape[0] :] = up_part[...]


def total_kernel(grad_norm, *rest):
    groups = len(rest) - 3
    down_out, up_out, held = rest[groups:]
    me = lax.axis_index("dp")
    seq = lax.axis_index("seq")
    for turn in range(groups):
        held[me ^ turn] = rest[turn][...].astype(jnp.float32)
    total = held[0]
    for group in range(1, groups):
        total = total + held[group]
    total = total * grad_norm
    first, second = total[:HALF], total[HALF : 2 * HALF]
    shared = total[2 * HALF : 2 * HALF + HALF // 2]
    up_out[...] = total[2 * HALF + HALF // 2 :]
    swapped = swap_halves(shared)
    low_half = jnp.concatenate([shared, swapped], axis=0)
    high_half = jnp.concatenate([swapped, shared], axis=0)
    even = jnp.concatenate([first, second, low_half], axis=1)
    odd = pltpu.roll(jnp.concatenate([first, second, high_half], axis=1), HALF, 1)
    down = jnp.where(remainder(seq, 2) == 0, even, odd)
    down_out[...] = down[:, : down_out.shape[1]]


def call(kernel, outs, specs, scratch, flops, moved, *args, vmem_mib=32, out_specs=None):
    shapes = [jax.ShapeDtypeStruct(shape, dtype) for shape, dtype in outs]
    return pl.pallas_call(
        kernel,
        out_shape=shapes,
        in_specs=specs,
        out_specs=out_specs or [VMEM] * len(shapes),
        scratch_shapes=scratch,
        compiler_params=pltpu.CompilerParams(vmem_limit_bytes=vmem_mib << 20),
        cost_estimate=pl.CostEstimate(flops=flops, bytes_accessed=moved, transcendentals=0),
    )(*args)


def exchange(value, axis, turn):
    peers = lax.axis_size(axis)
    return lax.ppermute(value, axis, [(peer, peer ^ turn) for peer in range(peers)])


def per_device_tiles(
    features,
    frozen_query_weight,
    source_keys,
    source_values,
    output_gradient,
    adapter_down_weight,
    adapter_up_weight,
    source_block_plan,
    segments,
):
    groups = lax.axis_size("dp")
    heads = lax.axis_size("seq")
    _, blocks, rows, width = features.shape
    length = segments.shape[1]
    live = (length // 2 + length // 8) // LANES
    reach = live * LANES
    rank = adapter_up_weight.shape[0]
    extras = live - CAP
    pairs = (extras + 1) // 2
    dims = (groups, blocks, heads, rows, live)
    bf16 = jnp.bfloat16
    f32 = jnp.float32
    peers = groups * heads
    everyone = ("seq", "dp")
    flat = features[0].reshape(blocks * rows, width)
    far_shape = (peers, CAP * 3 + 1, rows, LANES)
    own_shape = (extras * 3 + live + pairs, rows, LANES)
    rows_shape = (blocks, rows, heads * LANES)

    far_send, queries, adapter = call(
        functools.partial(pack_far_kernel, dims),
        [(far_shape, bf16), (rows_shape, bf16), ((blocks, rows, LANES), bf16)],
        [ANY] * 7,
        [
            pltpu.SMEM((groups, blocks), jnp.int32),
            pltpu.VMEM((blocks * rows, width), bf16),
            pltpu.VMEM(rows_shape, bf16),
            pltpu.VMEM(rows_shape, bf16),
            pltpu.VMEM(rows_shape, bf16),
            pltpu.VMEM((rank, width), bf16),
            pltpu.VMEM((rank, heads * LANES), bf16),
            pltpu.VMEM(far_shape, bf16),
            pltpu.SemaphoreType.DMA((7,)),
            pltpu.SemaphoreType.DMA((2,)),
        ],
        60_000_000,
        4_000_000,
        source_block_plan,
        flat,
        frozen_query_weight[0],
        source_keys[0],
        source_values[0],
        adapter_down_weight.T,
        adapter_up_weight,
        vmem_mib=60,
        out_specs=[ANY, VMEM, VMEM],
    )
    own_send = call(
        functools.partial(pack_own_kernel, dims),
        [(own_shape, bf16)] * heads,
        [SMEM] + [VMEM] * 5,
        [],
        0,
        1_600_000,
        source_block_plan,
        source_keys[0],
        source_values[0],
        output_gradient[0],
        queries,
        adapter,
    )
    own = [own_send[0]] + [exchange(own_send[turn], "seq", turn) for turn in range(1, heads)]
    far = lax.all_to_all(far_send, everyone, 0, 0, tiled=True)
    attended = call(
        functools.partial(attend_kernel, dims),
        [((peers, rows, LANES), bf16)]
        + [((CORES, pairs, rows, LANES), bf16)] * (heads // CORES)
        + [((rank, LANES), bf16), ((1, 1, length), f32)],
        [SMEM] + [VMEM] * (3 + heads),
        [pltpu.VMEM((reach, LANES), bf16)] * 5
        + [pltpu.VMEM((LANES, reach), bf16), pltpu.VMEM((reach, LANES), bf16)],
        600_000_000,
        3_000_000,
        source_block_plan,
        segments,
        adapter_up_weight,
        far,
        *own,
    )
    own_parts = [
        exchange(attended[1 + chip], "seq", chip * CORES) for chip in range(heads // CORES - 1, 0, -1)
    ]
    own_mine, own_other = call(
        chip_sum_kernel,
        [((pairs, rows, LANES), bf16)] * CORES,
        [VMEM] * (heads // CORES),
        [],
        0,
        100_000,
        *own_parts,
        attended[1],
    )
    own_other = exchange(own_other, "seq", 1)
    part = lax.all_to_all(attended[0], everyone, 0, 0, tiled=True)
    up_part, log_norm = attended[1 + heads // CORES :]
    (shares,) = call(
        functools.partial(product_kernel, dims),
        [((heads, HALF * 5 // 2, LANES), bf16)],
        [SMEM] + [VMEM] * 4,
        [
            pltpu.VMEM((groups + pairs, rows, LANES), f32),
            pltpu.VMEM((blocks, rows, LANES), bf16),
        ],
        40_000_000,
        2_000_000,
        source_block_plan,
        part,
        flat,
        own_mine,
        own_other,
    )
    shares = lax.all_to_all(shares, "seq", 0, 0, tiled=True)
    (joined,) = call(
        join_kernel,
        [((HALF * 5 // 2 + rank, LANES), bf16)],
        [VMEM] * 2,
        [],
        0,
        600_000,
        shares,
        up_part,
    )
    sums = [joined] + [exchange(joined, "dp", turn) for turn in range(1, groups)]
    down, up = call(
        functools.partial(total_kernel, 4.0 / math.sqrt(groups * length)),
        [((rank, width // heads), f32), ((rank, LANES), f32)],
        [VMEM] * groups,
        [pltpu.VMEM((groups,) + joined.shape, f32)],
        0,
        400_000,
        *sums,
    )
    return (down.T, up, log_norm)


def power_of_two(size):
    return size > 1 and size & (size - 1) == 0


def fits_tiles(mesh, features, adapter_up_weight):
    groups, heads = mesh.shape["dp"], mesh.shape["seq"]
    rows = features.shape[2] // heads
    return (
        rows % 16 == 0
        and features.shape[2] == LANES
        and features.shape[3] * 2 == heads * 5 * LANES
        and power_of_two(heads)
        and power_of_two(groups)
        and power_of_two(features.shape[1])
        and adapter_up_weight.shape == (HALF, heads * LANES)
    )


def attend_head(query, key_rows, value_rows, cotangent, segment, clip_count, reach_rows):
    length = query.shape[0]
    width = query.shape[1]
    piece_count = 8
    piece_rows = reach_rows // piece_count
    scaling = 1.0 / math.sqrt(width)
    query_padded = jnp.pad(query, ((0, reach_rows), (0, 0)))
    grad_padded = jnp.pad(cotangent, ((0, reach_rows), (0, 0)))
    keys_padded = jnp.pad(key_rows, ((0, reach_rows), (0, 0)))
    values_padded = jnp.pad(value_rows, ((0, reach_rows), (0, 0)))
    segment_padded = jnp.pad(segment, (0, reach_rows), constant_values=-1)
    clip_ids = jnp.arange(clip_count, dtype=jnp.int32)
    starts = jnp.sum((segment[None, :] < clip_ids[:, None]).astype(jnp.int32), axis=1)

    def piece_pass(piece_index):
        clip_slice = piece_index // piece_count
        start = lax.dynamic_index_in_dim(starts, clip_slice, 0, keepdims=False)
        query_start = start + piece_index % piece_count * piece_rows
        query_tile = lax.dynamic_slice_in_dim(query_padded, query_start, piece_rows, 0)
        grad_tile = lax.dynamic_slice_in_dim(grad_padded, query_start, piece_rows, 0)
        seg_tile = lax.dynamic_slice_in_dim(segment_padded, query_start, piece_rows, 0)
        key_tile = lax.dynamic_slice_in_dim(keys_padded, start, reach_rows, 0)
        value_tile = lax.dynamic_slice_in_dim(values_padded, start, reach_rows, 0)
        seg_cols = lax.dynamic_slice_in_dim(segment_padded, start, reach_rows, 0)
        in_clip = seg_tile == clip_slice
        allowed = in_clip[:, None] & (seg_cols == clip_slice)[None, :]
        scores = (
            lax.dot_general(
                query_tile, key_tile, (((1,), (1,)), ((), ())), preferred_element_type=jnp.float32
            )
            * scaling
        )
        scores = jnp.where(allowed, scores, -1e30)
        maximum = jnp.max(scores, axis=1, keepdims=True)
        exponent = jnp.where(allowed, jnp.exp(scores - maximum), 0.0)
        totals = jnp.where(in_clip[:, None], jnp.sum(exponent, axis=1, keepdims=True), 1.0)
        log_norm = jnp.where(in_clip, maximum[:, 0] + jnp.log(totals[:, 0]), 0.0)
        probs = exponent / totals
        weights = probs.astype(jnp.bfloat16)
        attended = jnp.dot(weights, value_tile, preferred_element_type=jnp.float32)
        delta = jnp.sum(grad_tile.astype(jnp.float32) * attended, axis=1, keepdims=True)
        dprob = lax.dot_general(
            grad_tile, value_tile, (((1,), (1,)), ((), ())), preferred_element_type=jnp.float32
        )
        dscore = (probs * (dprob - delta)).astype(jnp.bfloat16)
        query_gradient = (
            jnp.dot(dscore, key_tile, preferred_element_type=jnp.float32) * scaling
        ).astype(jnp.bfloat16)
        query_gradient = jnp.where(in_clip[:, None], query_gradient, jnp.zeros((), jnp.bfloat16))
        return (query_gradient, log_norm, query_start)

    total_pieces = piece_count * (clip_count - 1)
    dquery_pieces, log_pieces, piece_starts = lax.map(
        piece_pass, jnp.arange(total_pieces, dtype=jnp.int32)
    )

    def place(index, carry):
        grad_total, log_total = carry
        where_at = lax.dynamic_index_in_dim(piece_starts, index, 0, keepdims=False)
        grad_piece = lax.dynamic_index_in_dim(dquery_pieces, index, 0, keepdims=False)
        log_piece = lax.dynamic_index_in_dim(log_pieces, index, 0, keepdims=False)
        grad_old = lax.dynamic_slice_in_dim(grad_total, where_at, piece_rows, 0)
        log_old = lax.dynamic_slice_in_dim(log_total, where_at, piece_rows, 0)
        grad_total = lax.dynamic_update_slice_in_dim(grad_total, grad_old + grad_piece, where_at, 0)
        log_total = lax.dynamic_update_slice_in_dim(log_total, log_old + log_piece, where_at, 0)
        return (grad_total, log_total)

    grad_init = jnp.zeros((length + reach_rows, width), jnp.bfloat16)
    log_init = jnp.zeros((length + reach_rows,), jnp.float32)
    grad_total, log_total = lax.fori_loop(0, total_pieces, place, (grad_init, log_init))
    return (grad_total[:length], log_total[:length])


def routing_tables(source_block_plan, group_index, cap_slots):
    group_count, block_count = source_block_plan.shape
    source_group = source_block_plan // block_count
    source_local = source_block_plan % block_count
    dest_groups = jnp.arange(group_count, dtype=jnp.int32)[:, None]
    outgoing = (source_group == group_index) & (dest_groups != group_index)
    out_rank = jnp.cumsum(outgoing.astype(jnp.int32), axis=1) - 1
    slot_ids = jnp.arange(cap_slots, dtype=jnp.int32)
    chosen = outgoing[:, :, None] & (out_rank[:, :, None] == slot_ids[None, None, :])
    send_index = jnp.sum(jnp.where(chosen, source_local[:, :, None], 0), axis=1)
    send_valid = jnp.any(chosen, axis=1)
    own_group = lax.dynamic_index_in_dim(source_group, group_index, 0, keepdims=False)
    own_local = lax.dynamic_index_in_dim(source_local, group_index, 0, keepdims=False)
    incoming = own_group != group_index
    positions = jnp.arange(block_count, dtype=jnp.int32)
    earlier = (own_group[None, :] == own_group[:, None]) & (positions[None, :] < positions[:, None])
    in_rank = jnp.sum(earlier.astype(jnp.int32), axis=1)
    return (send_index, send_valid, incoming, own_group, in_rank, own_local)


def pack_blocks(local, send_index, send_valid):
    picked = jnp.take(local, send_index, axis=0)
    return jnp.where(send_valid[:, :, None, None], picked, jnp.zeros((), local.dtype))


def unpack_blocks(received, local, tables, cap_slots):
    incoming, own_group, in_rank, own_local = tables
    flat = received.reshape((-1,) + received.shape[2:])
    slot_index = jnp.where(incoming, own_group * cap_slots + in_rank, 0)
    remote = jnp.take(flat, slot_index, axis=0)
    staying = jnp.take(local, own_local, axis=0)
    return jnp.where(incoming[:, None, None], remote, staying)


def per_device(
    features,
    frozen_query_weight,
    source_keys,
    source_values,
    output_gradient,
    adapter_down_weight,
    adapter_up_weight,
    source_block_plan,
    segments,
):
    group_count = lax.axis_size("dp")
    group_index = lax.axis_index("dp")
    block_count = features.shape[1]
    feat_local = features[0]
    base_local = frozen_query_weight[0]
    keys_local = source_keys[0]
    values_local = source_values[0]
    send_index, send_valid, incoming, own_group, in_rank, own_local = routing_tables(
        source_block_plan, group_index, CAP
    )
    tables = (incoming, own_group, in_rank, own_local)
    contract_final_axis = (((2,), (0,)), ((), ()))
    shuffled = (
        lax.all_to_all(
            pack_blocks(feat_local, send_index, send_valid),
            "dp",
            split_axis=0,
            concat_axis=0,
            tiled=True,
        ),
        lax.all_to_all(
            pack_blocks(base_local, send_index, send_valid),
            "dp",
            split_axis=0,
            concat_axis=0,
            tiled=True,
        ),
        lax.all_to_all(
            pack_blocks(keys_local, send_index, send_valid),
            "dp",
            split_axis=0,
            concat_axis=0,
            tiled=True,
        ),
        lax.all_to_all(
            pack_blocks(values_local, send_index, send_valid),
            "dp",
            split_axis=0,
            concat_axis=0,
            tiled=True,
        ),
    )
    feature_dest = unpack_blocks(shuffled[0], feat_local, tables, CAP)
    base_query_dest = unpack_blocks(shuffled[1], base_local, tables, CAP)
    keys_dest = unpack_blocks(shuffled[2], keys_local, tables, CAP)
    values_dest = unpack_blocks(shuffled[3], values_local, tables, CAP)
    adapter_params = lax.dot_general(
        feature_dest, adapter_down_weight, contract_final_axis, preferred_element_type=jnp.float32
    ).astype(jnp.bfloat16)
    query_rows = (
        base_query_dest.astype(jnp.float32)
        + lax.dot_general(
            adapter_params,
            adapter_up_weight,
            contract_final_axis,
            preferred_element_type=jnp.float32,
        )
    ).astype(jnp.bfloat16)
    head_query, head_keys, head_values, head_grads = (
        lax.all_to_all(query_rows, "seq", split_axis=2, concat_axis=1, tiled=True),
        lax.all_to_all(keys_dest, "seq", split_axis=2, concat_axis=1, tiled=True),
        lax.all_to_all(values_dest, "seq", split_axis=2, concat_axis=1, tiled=True),
        lax.all_to_all(output_gradient[0], "seq", split_axis=2, concat_axis=1, tiled=True),
    )
    length = head_query.shape[0] * head_query.shape[1]
    reach_rows = length // 2 + length // 8
    head_width = head_query.shape[2]
    segment = segments[0]
    head_query = head_query.reshape(length, head_width)
    head_keys = head_keys.reshape(length, head_width)
    head_values = head_values.reshape(length, head_width)
    head_grads = head_grads.reshape(length, head_width)
    dquery_head, log_head = attend_head(
        head_query, head_keys, head_values, head_grads, segment, CLIPS, reach_rows
    )
    norm_pieces = [log_head]
    log_norm = jnp.stack(norm_pieces, axis=0)
    query_gradient = lax.all_to_all(
        dquery_head.reshape(block_count, length // block_count, head_width),
        "seq",
        split_axis=1,
        concat_axis=2,
        tiled=True,
    )
    adapter_gradient = lax.dot_general(
        query_gradient,
        adapter_up_weight,
        (((2,), (1,)), ((), ())),
        preferred_element_type=jnp.float32,
    ).astype(jnp.bfloat16)
    contract_tokens = (((0, 1), (0, 1)), ((), ()))
    down_part = lax.dot_general(
        feature_dest, adapter_gradient, contract_tokens, preferred_element_type=jnp.float32
    )
    up_part = lax.dot_general(
        adapter_params, query_gradient, contract_tokens, preferred_element_type=jnp.float32
    )
    down_share, up_share = (
        lax.psum_scatter(down_part, "seq", scatter_dimension=0, tiled=True),
        lax.psum_scatter(up_part, "seq", scatter_dimension=1, tiled=True),
    )
    down_total, up_total = lax.psum((down_share, up_share), "dp")
    grad_norm = 4.0 / math.sqrt(group_count * length)
    return (down_total * grad_norm, up_total * grad_norm, log_norm[None])


def solution(mesh):
    in_specs = (
        P("dp", None, "seq", None),
        P("dp", None, "seq", None),
        P("dp", None, "seq", None),
        P("dp", None, "seq", None),
        P("dp", None, "seq", None),
        P(),
        P(),
        P(),
        P("dp", None),
    )
    out_specs = (P("seq", None), P(None, "seq"), P("dp", "seq", None))

    def whole(features, *rest):
        fits = fits_tiles(mesh, features, rest[5])
        return jax.shard_map(
            per_device_tiles if fits else per_device,
            mesh=mesh,
            in_specs=in_specs,
            out_specs=out_specs,
            check_vma=False,
        )(features, *rest)

    return whole
```

```python
import functools
import math

import jax
import jax.numpy as jnp
from jax import lax
from jax.experimental import pallas as pl
from jax.experimental.pallas import tpu as pltpu
from jax.sharding import PartitionSpec as P

CAP = 2
CLIPS = 2
LANES = 128
HALF = 64
CORES = 2
QUERIES = 640
LOG2E = math.log2(math.e)
VMEM = pl.BlockSpec(memory_space=pltpu.VMEM)
SMEM = pl.BlockSpec(memory_space=pltpu.SMEM)
ANY = pl.BlockSpec(memory_space=pl.ANY)
NT = (((1,), (1,)), ((), ()))


def low_lanes(rows):
    return lax.broadcasted_iota(jnp.int32, (rows, LANES), 1) < HALF


def swap_halves(tile):
    return pltpu.roll(tile, HALF, 1)


def lane_tile(index):
    return pl.ds(pl.multiple_of(index * LANES, LANES), LANES)


def row_tile(index, rows):
    return pl.ds(pl.multiple_of(index * rows, rows), rows)


def quotient(value, size):
    return lax.shift_right_logical(value, size.bit_length() - 1)


def remainder(value, size):
    return value & (size - 1)


def each_hit(plan, me, groups, blocks, live, put):
    def over_dest(dest, _):
        def over_position(position, slot):
            source = plan[dest, position]
            hit = quotient(source, blocks) == me

            @pl.when(hit)
            def _():
                put(dest, slot, remainder(source, blocks))

            return slot + hit.astype(jnp.int32)

        lax.fori_loop(0, live, over_position, jnp.int32(0))
        return 0

    lax.fori_loop(0, groups, over_dest, 0)


def each_block(plan, me, blocks, live, take):
    def over_position(position, _):
        group = quotient(plan[me, position], blocks)
        slot = jnp.int32(0)
        for other in range(live):
            same = (quotient(plan[me, other], blocks) == group) & (other < position)
            slot = slot + same.astype(jnp.int32)
        take(position, group, slot)
        return 0

    lax.fori_loop(0, live, over_position, 0)


def each_half(slot, store):
    @pl.when(remainder(slot, 2) == 0)
    def _():
        store(slice(0, HALF))

    @pl.when(remainder(slot, 2) == 1)
    def _():
        store(slice(HALF, LANES))


def split(slot, pair):
    pair = pair.astype(jnp.float32)
    return jnp.where(remainder(slot, 2) == 0, pair, swap_halves(pair))


def pack_far_kernel(dims, plan_hbm, feat_hbm, base_hbm, keys_hbm, vals_hbm, down_hbm, up_hbm, *rest):
    groups, blocks, heads, rows, live = dims
    far_hbm, queries_hbm, adapter_hbm = rest[:3]
    plan, feat, base, keys, vals, down, up, far_out, qbuf, abuf, sems, out_sems = rest[3:]
    me = lax.axis_index("dp")
    copies = [
        pltpu.make_async_copy(source, target, sems.at[index])
        for index, (source, target) in enumerate(
            (
                (plan_hbm, plan),
                (keys_hbm, keys),
                (vals_hbm, vals),
                (feat_hbm, feat),
                (down_hbm, down),
                (base_hbm, base),
                (up_hbm, up),
            )
        )
    ]
    for copy in copies:
        copy.start()

    def put_early(dest, slot, local):
        @pl.when(slot < CAP)
        def _():
            for head in range(heads):
                columns = slice(head * LANES, (head + 1) * LANES)
                far_out[head * groups + dest, slot] = keys[local, :, columns]
                far_out[head * groups + dest, CAP + slot] = vals[local, :, columns]

    def send(first, count, index):
        tiles = pl.ds(first, count)
        copy = pltpu.make_async_copy(far_out.at[:, tiles], far_hbm.at[:, tiles], out_sems.at[index])
        copy.start()
        return copy

    for copy in copies[:3]:
        copy.wait()
    each_hit(plan, me, groups, blocks, live, put_early)
    early = send(0, 2 * CAP, 0)
    for copy in copies[3:]:
        copy.wait()
    narrow = lax.dot_general(feat[...], down[...], NT, preferred_element_type=jnp.float32)
    adapter = narrow.astype(jnp.bfloat16)
    lift = jnp.dot(adapter, up[...], preferred_element_type=jnp.float32)
    abuf[...] = jnp.concatenate([narrow, narrow], axis=1).astype(jnp.bfloat16).reshape(abuf.shape)
    qbuf[...] = (base[...].astype(jnp.float32) + lift.reshape(base.shape)).astype(jnp.bfloat16)

    def put_late(dest, slot, local):
        def store(lanes):
            for head in range(heads):
                columns = slice(head * LANES, (head + 1) * LANES)
                far_out[head * groups + dest, 2 * CAP + slot] = qbuf[local, :, columns]
                far_out[head * groups + dest, CAP * 3, :, lanes] = abuf[local, :, lanes]

        @pl.when(slot < CAP)
        def _():
            each_half(slot, store)

    each_hit(plan, me, groups, blocks, live, put_late)
    late = send(2 * CAP, CAP + 1, 1)
    rest_out = [
        pltpu.make_async_copy(qbuf, queries_hbm, out_sems.at[2]),
        pltpu.make_async_copy(abuf, adapter_hbm, out_sems.at[3]),
    ]
    for copy in rest_out:
        copy.start()
    for copy in [early, late] + rest_out:
        copy.wait()


def pack_own_kernel(dims, plan, keys, vals, grad, queries, adapter, *own_outs):
    groups, blocks, heads, rows, live = dims
    extras = live - CAP
    me = lax.axis_index("dp")
    seq = lax.axis_index("seq")
    sources = (keys, vals, queries)

    def put(dest, slot, local):
        @pl.when(slot >= CAP)
        def _():
            extra = slot - CAP
            where = extras * 3 + live + quotient(extra, 2)
            for turn in range(heads):
                columns = lane_tile(seq ^ turn)
                for index, source in enumerate(sources):
                    own_outs[turn][index * extras + extra] = source[local, :, columns]

            def store(lanes):
                for turn in range(heads):
                    own_outs[turn][where, :, lanes] = adapter[local, :, lanes]

            each_half(slot, store)

    each_hit(plan, me, groups, blocks, live, put)
    for turn in range(heads):
        columns = lane_tile(seq ^ turn)
        for position in range(live):
            own_outs[turn][extras * 3 + position] = grad[position, :, columns]


def attend_kernel(dims, plan, seg, up, far_in, *rest):
    groups, blocks, heads, rows, live = dims
    own_ins = rest[:heads]
    part_out = rest[heads]
    own_parts = rest[heads + 1 : heads + 1 + heads // CORES]
    up_out, log_out, qs, ks, vs, gs, ads, dqs, parts = rest[heads + 1 + heads // CORES :]
    extras = live - CAP
    me = lax.axis_index("dp")
    seq = lax.axis_index("seq")
    rank = up.shape[0]
    length = seg.shape[1]
    reach = live * LANES
    scaling = 1.0 / math.sqrt(LANES)

    ads[...] = jnp.zeros_like(ads)

    def take(position, group, slot):
        far = (group != me) | (slot < CAP)

        @pl.when(far)
        def _():
            for part in range(heads):
                index = part * groups + group
                where = row_tile(position * heads + part, rows)
                ks[where, :] = far_in[index, slot]
                vs[where, :] = far_in[index, CAP + slot]
                qs[where, :] = far_in[index, 2 * CAP + slot]

            def store(lanes):
                for part in range(heads):
                    where = row_tile(position * heads + part, rows)
                    ads[where, lanes] = far_in[part * groups + group, CAP * 3, :, lanes]

            each_half(slot, store)

        @pl.when(jnp.logical_not(far))
        def _():
            extra = slot - CAP
            pair = extras * 3 + live + quotient(extra, 2)
            for turn in range(heads):
                where = row_tile(position * heads + (seq ^ turn), rows)
                ks[where, :] = own_ins[turn][extra]
                vs[where, :] = own_ins[turn][extras + extra]
                qs[where, :] = own_ins[turn][2 * extras + extra]

            def store(lanes):
                for turn in range(heads):
                    where = row_tile(position * heads + (seq ^ turn), rows)
                    ads[where, lanes] = own_ins[turn][pair, :, lanes]

            each_half(slot, store)

    each_block(plan, me, blocks, live, take)
    for turn in range(heads):
        for position in range(live):
            gs[row_tile(position * heads + (seq ^ turn), rows), :] = own_ins[turn][
                extras * 3 + position
            ]

    count = jnp.sum((seg[...] < CLIPS - 1).astype(jnp.float32), axis=1, keepdims=True).astype(
        jnp.int32
    )
    key_rows = ks[...]
    value_rows = vs[...]
    key_columns = key_rows.T
    key_index = lax.broadcasted_iota(jnp.int32, (reach, 1), 0)
    always = length - reach
    up_head = up[:, lane_tile(seq)]
    up_twice = jnp.concatenate([up_head, up_head], axis=0)
    for start in range(0, reach, QUERIES):
        count_here = min(QUERIES, reach - start)
        span = slice(start, start + count_here)
        scores = lax.dot_general(key_rows, qs[span, :], NT, preferred_element_type=jnp.float32)
        scores = jnp.concatenate(
            [
                scores[:always],
                jnp.where(key_index[always:] < count, scores[always:], -1e30),
            ],
            axis=0,
        )
        dprob = lax.dot_general(value_rows, gs[span, :], NT, preferred_element_type=jnp.float32)
        maximum = jnp.max(scores, axis=0, keepdims=True)
        exponent = jnp.exp2((scores - maximum) * (scaling * LOG2E))
        total = jnp.sum(exponent, axis=0, keepdims=True)
        delta = jnp.sum(exponent * dprob, axis=0, keepdims=True) / total
        dscore = (exponent * (dprob - delta)).astype(jnp.bfloat16)
        dquery = jnp.dot(key_columns, dscore, preferred_element_type=jnp.float32)
        query_index = lax.broadcasted_iota(jnp.int32, (1, count_here), 1) + start
        in_clip = query_index < count
        dquery = jnp.where(in_clip, dquery * (scaling / total), 0.0).astype(jnp.bfloat16)
        dqs[:, span] = dquery
        log_out[0, :, span] = jnp.where(in_clip, maximum * scaling + jnp.log(total), 0.0)
    log_out[0, :, reach:] = jnp.zeros((1, length - reach), jnp.float32)
    dquery_all = dqs[...]
    parts[...] = lax.dot_general(
        dquery_all, up_twice, (((0,), (1,)), ((), ())), preferred_element_type=jnp.float32
    ).astype(jnp.bfloat16)

    def put(position, group, slot):
        far = (group != me) | (slot < CAP)

        @pl.when(far)
        def _():
            def store(lanes):
                for part in range(heads):
                    where = row_tile(position * heads + part, rows)
                    part_out[part * groups + group, :, lanes] = parts[where, lanes]

            each_half(slot, store)

        @pl.when(jnp.logical_not(far))
        def _():
            pair = quotient(slot - CAP, 2)

            def store(lanes):
                for turn in range(heads):
                    where = row_tile(position * heads + (seq ^ turn), rows)
                    own_parts[turn // CORES][turn % CORES, pair, :, lanes] = parts[where, lanes]

            each_half(slot, store)

    each_block(plan, me, blocks, live, put)
    up_part = jnp.dot(dquery_all, ads[...], preferred_element_type=jnp.float32)
    up_out[...] = (up_part + swap_halves(up_part)).T[:rank].astype(jnp.bfloat16)


def chip_sum_kernel(*refs):
    parts, outs = refs[:-CORES], refs[-CORES:]
    for core in range(CORES):
        total = parts[0][core].astype(jnp.float32)
        for part in parts[1:]:
            total = total + part[core].astype(jnp.float32)
        outs[core][...] = total.astype(jnp.bfloat16)


def product_kernel(dims, plan, parts, feat, own_mine, own_other, out, sums, grads):
    groups, blocks, heads, rows, live = dims
    me = lax.axis_index("dp")
    for group in range(groups):
        total = parts[group].astype(jnp.float32)
        for head in range(1, heads):
            total = total + parts[head * groups + group].astype(jnp.float32)
        sums[group] = total
    for pair in range(own_mine.shape[0]):
        sums[groups + pair] = own_mine[pair].astype(jnp.float32) + own_other[pair].astype(
            jnp.float32
        )
    grads[...] = jnp.zeros_like(grads)

    def put(dest, slot, local):
        index = jnp.where(slot < CAP, dest, groups - 1 + quotient(slot, 2))
        grads[local] = split(slot, sums[index]).astype(jnp.bfloat16)

    each_hit(plan, me, groups, blocks, live, put)
    low = low_lanes(HALF // 2)
    columns = grads[...].reshape(blocks * rows, LANES).astype(jnp.float32).T[:HALF]
    columns = columns.astype(jnp.bfloat16)
    for pair in range(heads // 2):
        tiles = jnp.dot(
            columns,
            feat[:, pair * 5 * LANES : (pair + 1) * 5 * LANES],
            preferred_element_type=jnp.float32,
        )
        shared = tiles[:, 2 * LANES : 3 * LANES]
        upper, lower = shared[: HALF // 2], shared[HALF // 2 :]
        for part in range(2):
            ahead = tiles[:, part * 3 * LANES : (part * 3 + 2) * LANES].astype(jnp.bfloat16)
            out[pair * 2 + part, :HALF] = ahead[:, :LANES]
            out[pair * 2 + part, HALF : 2 * HALF] = ahead[:, LANES:]
            if part == 0:
                rest = jnp.where(low, upper, swap_halves(lower))
            else:
                rest = jnp.where(low, swap_halves(upper), lower)
            out[pair * 2 + part, 2 * HALF :] = rest.astype(jnp.bfloat16)


def join_kernel(parts, up_part, out):
    total = parts[0].astype(jnp.float32)
    for head in range(1, parts.shape[0]):
        total = total + parts[head].astype(jnp.float32)
    out[: total.shape[0]] = total.astype(jnp.bfloat16)
    out[total.shape[0] :] = up_part[...]


def total_kernel(grad_norm, *rest):
    groups = len(rest) - 3
    down_out, up_out, held = rest[groups:]
    me = lax.axis_index("dp")
    seq = lax.axis_index("seq")
    for turn in range(groups):
        held[me ^ turn] = rest[turn][...].astype(jnp.float32)
    total = held[0]
    for group in range(1, groups):
        total = total + held[group]
    total = total * grad_norm
    first, second = total[:HALF], total[HALF : 2 * HALF]
    shared = total[2 * HALF : 2 * HALF + HALF // 2]
    up_out[...] = total[2 * HALF + HALF // 2 :]
    swapped = swap_halves(shared)
    low_half = jnp.concatenate([shared, swapped], axis=0)
    high_half = jnp.concatenate([swapped, shared], axis=0)
    even = jnp.concatenate([first, second, low_half], axis=1)
    odd = pltpu.roll(jnp.concatenate([first, second, high_half], axis=1), HALF, 1)
    down = jnp.where(remainder(seq, 2) == 0, even, odd)
    down_out[...] = down[:, : down_out.shape[1]]


def call(kernel, outs, specs, scratch, flops, moved, *args, vmem_mib=32, out_specs=None):
    shapes = [jax.ShapeDtypeStruct(shape, dtype) for shape, dtype in outs]
    return pl.pallas_call(
        kernel,
        out_shape=shapes,
        in_specs=specs,
        out_specs=out_specs or [VMEM] * len(shapes),
        scratch_shapes=scratch,
        compiler_params=pltpu.CompilerParams(vmem_limit_bytes=vmem_mib << 20),
        cost_estimate=pl.CostEstimate(flops=flops, bytes_accessed=moved, transcendentals=0),
    )(*args)


def exchange(value, axis, turn):
    peers = lax.axis_size(axis)
    return lax.ppermute(value, axis, [(peer, peer ^ turn) for peer in range(peers)])


def per_device_tiles(
    features,
    frozen_query_weight,
    source_keys,
    source_values,
    output_gradient,
    adapter_down_weight,
    adapter_up_weight,
    source_block_plan,
    segments,
):
    groups = lax.axis_size("dp")
    heads = lax.axis_size("seq")
    _, blocks, rows, width = features.shape
    length = segments.shape[1]
    live = (length // 2 + length // 8) // LANES
    reach = live * LANES
    rank = adapter_up_weight.shape[0]
    extras = live - CAP
    pairs = (extras + 1) // 2
    dims = (groups, blocks, heads, rows, live)
    bf16 = jnp.bfloat16
    f32 = jnp.float32
    peers = groups * heads
    everyone = ("seq", "dp")
    flat = features[0].reshape(blocks * rows, width)
    far_shape = (peers, CAP * 3 + 1, rows, LANES)
    own_shape = (extras * 3 + live + pairs, rows, LANES)
    rows_shape = (blocks, rows, heads * LANES)

    far_send, queries, adapter = call(
        functools.partial(pack_far_kernel, dims),
        [(far_shape, bf16), (rows_shape, bf16), ((blocks, rows, LANES), bf16)],
        [ANY] * 7,
        [
            pltpu.SMEM((groups, blocks), jnp.int32),
            pltpu.VMEM((blocks * rows, width), bf16),
            pltpu.VMEM(rows_shape, bf16),
            pltpu.VMEM(rows_shape, bf16),
            pltpu.VMEM(rows_shape, bf16),
            pltpu.VMEM((rank, width), bf16),
            pltpu.VMEM((rank, heads * LANES), bf16),
            pltpu.VMEM(far_shape, bf16),
            pltpu.VMEM(rows_shape, bf16),
            pltpu.VMEM((blocks, rows, LANES), bf16),
            pltpu.SemaphoreType.DMA((7,)),
            pltpu.SemaphoreType.DMA((4,)),
        ],
        60_000_000,
        4_000_000,
        source_block_plan,
        flat,
        frozen_query_weight[0],
        source_keys[0],
        source_values[0],
        adapter_down_weight.T,
        adapter_up_weight,
        vmem_mib=60,
        out_specs=[ANY] * 3,
    )
    own_send = call(
        functools.partial(pack_own_kernel, dims),
        [(own_shape, bf16)] * heads,
        [SMEM] + [VMEM] * 5,
        [],
        0,
        1_600_000,
        source_block_plan,
        source_keys[0],
        source_values[0],
        output_gradient[0],
        queries,
        adapter,
    )
    own = [own_send[0]] + [exchange(own_send[turn], "seq", turn) for turn in range(1, heads)]
    far = lax.all_to_all(far_send, everyone, 0, 0, tiled=True)
    attended = call(
        functools.partial(attend_kernel, dims),
        [((peers, rows, LANES), bf16)]
        + [((CORES, pairs, rows, LANES), bf16)] * (heads // CORES)
        + [((rank, LANES), bf16), ((1, 1, length), f32)],
        [SMEM] + [VMEM] * (3 + heads),
        [pltpu.VMEM((reach, LANES), bf16)] * 5
        + [pltpu.VMEM((LANES, reach), bf16), pltpu.VMEM((reach, LANES), bf16)],
        600_000_000,
        3_000_000,
        source_block_plan,
        segments,
        adapter_up_weight,
        far,
        *own,
    )
    own_parts = [
        exchange(attended[1 + chip], "seq", chip * CORES) for chip in range(heads // CORES - 1, 0, -1)
    ]
    own_mine, own_other = call(
        chip_sum_kernel,
        [((pairs, rows, LANES), bf16)] * CORES,
        [VMEM] * (heads // CORES),
        [],
        0,
        100_000,
        *own_parts,
        attended[1],
    )
    own_other = exchange(own_other, "seq", 1)
    part = lax.all_to_all(attended[0], everyone, 0, 0, tiled=True)
    up_part, log_norm = attended[1 + heads // CORES :]
    (shares,) = call(
        functools.partial(product_kernel, dims),
        [((heads, HALF * 5 // 2, LANES), bf16)],
        [SMEM] + [VMEM] * 4,
        [
            pltpu.VMEM((groups + pairs, rows, LANES), f32),
            pltpu.VMEM((blocks, rows, LANES), bf16),
        ],
        40_000_000,
        2_000_000,
        source_block_plan,
        part,
        flat,
        own_mine,
        own_other,
    )
    shares = lax.all_to_all(shares, "seq", 0, 0, tiled=True)
    (joined,) = call(
        join_kernel,
        [((HALF * 5 // 2 + rank, LANES), bf16)],
        [VMEM] * 2,
        [],
        0,
        600_000,
        shares,
        up_part,
    )
    sums = [joined] + [exchange(joined, "dp", turn) for turn in range(1, groups)]
    down, up = call(
        functools.partial(total_kernel, 4.0 / math.sqrt(groups * length)),
        [((rank, width // heads), f32), ((rank, LANES), f32)],
        [VMEM] * groups,
        [pltpu.VMEM((groups,) + joined.shape, f32)],
        0,
        400_000,
        *sums,
    )
    return (down.T, up, log_norm)


def power_of_two(size):
    return size > 1 and size & (size - 1) == 0


def fits_tiles(mesh, features, adapter_up_weight):
    groups, heads = mesh.shape["dp"], mesh.shape["seq"]
    rows = features.shape[2] // heads
    return (
        rows % 16 == 0
        and features.shape[2] == LANES
        and features.shape[3] * 2 == heads * 5 * LANES
        and power_of_two(heads)
        and power_of_two(groups)
        and power_of_two(features.shape[1])
        and adapter_up_weight.shape == (HALF, heads * LANES)
    )


def attend_head(query, key_rows, value_rows, cotangent, segment, clip_count, reach_rows):
    length = query.shape[0]
    width = query.shape[1]
    piece_count = 8
    piece_rows = reach_rows // piece_count
    scaling = 1.0 / math.sqrt(width)
    query_padded = jnp.pad(query, ((0, reach_rows), (0, 0)))
    grad_padded = jnp.pad(cotangent, ((0, reach_rows), (0, 0)))
    keys_padded = jnp.pad(key_rows, ((0, reach_rows), (0, 0)))
    values_padded = jnp.pad(value_rows, ((0, reach_rows), (0, 0)))
    segment_padded = jnp.pad(segment, (0, reach_rows), constant_values=-1)
    clip_ids = jnp.arange(clip_count, dtype=jnp.int32)
    starts = jnp.sum((segment[None, :] < clip_ids[:, None]).astype(jnp.int32), axis=1)

    def piece_pass(piece_index):
        clip_slice = piece_index // piece_count
        start = lax.dynamic_index_in_dim(starts, clip_slice, 0, keepdims=False)
        query_start = start + piece_index % piece_count * piece_rows
        query_tile = lax.dynamic_slice_in_dim(query_padded, query_start, piece_rows, 0)
        grad_tile = lax.dynamic_slice_in_dim(grad_padded, query_start, piece_rows, 0)
        seg_tile = lax.dynamic_slice_in_dim(segment_padded, query_start, piece_rows, 0)
        key_tile = lax.dynamic_slice_in_dim(keys_padded, start, reach_rows, 0)
        value_tile = lax.dynamic_slice_in_dim(values_padded, start, reach_rows, 0)
        seg_cols = lax.dynamic_slice_in_dim(segment_padded, start, reach_rows, 0)
        in_clip = seg_tile == clip_slice
        allowed = in_clip[:, None] & (seg_cols == clip_slice)[None, :]
        scores = (
            lax.dot_general(
                query_tile, key_tile, (((1,), (1,)), ((), ())), preferred_element_type=jnp.float32
            )
            * scaling
        )
        scores = jnp.where(allowed, scores, -1e30)
        maximum = jnp.max(scores, axis=1, keepdims=True)
        exponent = jnp.where(allowed, jnp.exp(scores - maximum), 0.0)
        totals = jnp.where(in_clip[:, None], jnp.sum(exponent, axis=1, keepdims=True), 1.0)
        log_norm = jnp.where(in_clip, maximum[:, 0] + jnp.log(totals[:, 0]), 0.0)
        probs = exponent / totals
        weights = probs.astype(jnp.bfloat16)
        attended = jnp.dot(weights, value_tile, preferred_element_type=jnp.float32)
        delta = jnp.sum(grad_tile.astype(jnp.float32) * attended, axis=1, keepdims=True)
        dprob = lax.dot_general(
            grad_tile, value_tile, (((1,), (1,)), ((), ())), preferred_element_type=jnp.float32
        )
        dscore = (probs * (dprob - delta)).astype(jnp.bfloat16)
        query_gradient = (
            jnp.dot(dscore, key_tile, preferred_element_type=jnp.float32) * scaling
        ).astype(jnp.bfloat16)
        query_gradient = jnp.where(in_clip[:, None], query_gradient, jnp.zeros((), jnp.bfloat16))
        return (query_gradient, log_norm, query_start)

    total_pieces = piece_count * (clip_count - 1)
    dquery_pieces, log_pieces, piece_starts = lax.map(
        piece_pass, jnp.arange(total_pieces, dtype=jnp.int32)
    )

    def place(index, carry):
        grad_total, log_total = carry
        where_at = lax.dynamic_index_in_dim(piece_starts, index, 0, keepdims=False)
        grad_piece = lax.dynamic_index_in_dim(dquery_pieces, index, 0, keepdims=False)
        log_piece = lax.dynamic_index_in_dim(log_pieces, index, 0, keepdims=False)
        grad_old = lax.dynamic_slice_in_dim(grad_total, where_at, piece_rows, 0)
        log_old = lax.dynamic_slice_in_dim(log_total, where_at, piece_rows, 0)
        grad_total = lax.dynamic_update_slice_in_dim(grad_total, grad_old + grad_piece, where_at, 0)
        log_total = lax.dynamic_update_slice_in_dim(log_total, log_old + log_piece, where_at, 0)
        return (grad_total, log_total)

    grad_init = jnp.zeros((length + reach_rows, width), jnp.bfloat16)
    log_init = jnp.zeros((length + reach_rows,), jnp.float32)
    grad_total, log_total = lax.fori_loop(0, total_pieces, place, (grad_init, log_init))
    return (grad_total[:length], log_total[:length])


def routing_tables(source_block_plan, group_index, cap_slots):
    group_count, block_count = source_block_plan.shape
    source_group = source_block_plan // block_count
    source_local = source_block_plan % block_count
    dest_groups = jnp.arange(group_count, dtype=jnp.int32)[:, None]
    outgoing = (source_group == group_index) & (dest_groups != group_index)
    out_rank = jnp.cumsum(outgoing.astype(jnp.int32), axis=1) - 1
    slot_ids = jnp.arange(cap_slots, dtype=jnp.int32)
    chosen = outgoing[:, :, None] & (out_rank[:, :, None] == slot_ids[None, None, :])
    send_index = jnp.sum(jnp.where(chosen, source_local[:, :, None], 0), axis=1)
    send_valid = jnp.any(chosen, axis=1)
    own_group = lax.dynamic_index_in_dim(source_group, group_index, 0, keepdims=False)
    own_local = lax.dynamic_index_in_dim(source_local, group_index, 0, keepdims=False)
    incoming = own_group != group_index
    positions = jnp.arange(block_count, dtype=jnp.int32)
    earlier = (own_group[None, :] == own_group[:, None]) & (positions[None, :] < positions[:, None])
    in_rank = jnp.sum(earlier.astype(jnp.int32), axis=1)
    return (send_index, send_valid, incoming, own_group, in_rank, own_local)


def pack_blocks(local, send_index, send_valid):
    picked = jnp.take(local, send_index, axis=0)
    return jnp.where(send_valid[:, :, None, None], picked, jnp.zeros((), local.dtype))


def unpack_blocks(received, local, tables, cap_slots):
    incoming, own_group, in_rank, own_local = tables
    flat = received.reshape((-1,) + received.shape[2:])
    slot_index = jnp.where(incoming, own_group * cap_slots + in_rank, 0)
    remote = jnp.take(flat, slot_index, axis=0)
    staying = jnp.take(local, own_local, axis=0)
    return jnp.where(incoming[:, None, None], remote, staying)


def per_device(
    features,
    frozen_query_weight,
    source_keys,
    source_values,
    output_gradient,
    adapter_down_weight,
    adapter_up_weight,
    source_block_plan,
    segments,
):
    group_count = lax.axis_size("dp")
    group_index = lax.axis_index("dp")
    block_count = features.shape[1]
    feat_local = features[0]
    base_local = frozen_query_weight[0]
    keys_local = source_keys[0]
    values_local = source_values[0]
    send_index, send_valid, incoming, own_group, in_rank, own_local = routing_tables(
        source_block_plan, group_index, CAP
    )
    tables = (incoming, own_group, in_rank, own_local)
    contract_final_axis = (((2,), (0,)), ((), ()))
    shuffled = (
        lax.all_to_all(
            pack_blocks(feat_local, send_index, send_valid),
            "dp",
            split_axis=0,
            concat_axis=0,
            tiled=True,
        ),
        lax.all_to_all(
            pack_blocks(base_local, send_index, send_valid),
            "dp",
            split_axis=0,
            concat_axis=0,
            tiled=True,
        ),
        lax.all_to_all(
            pack_blocks(keys_local, send_index, send_valid),
            "dp",
            split_axis=0,
            concat_axis=0,
            tiled=True,
        ),
        lax.all_to_all(
            pack_blocks(values_local, send_index, send_valid),
            "dp",
            split_axis=0,
            concat_axis=0,
            tiled=True,
        ),
    )
    feature_dest = unpack_blocks(shuffled[0], feat_local, tables, CAP)
    base_query_dest = unpack_blocks(shuffled[1], base_local, tables, CAP)
    keys_dest = unpack_blocks(shuffled[2], keys_local, tables, CAP)
    values_dest = unpack_blocks(shuffled[3], values_local, tables, CAP)
    adapter_params = lax.dot_general(
        feature_dest, adapter_down_weight, contract_final_axis, preferred_element_type=jnp.float32
    ).astype(jnp.bfloat16)
    query_rows = (
        base_query_dest.astype(jnp.float32)
        + lax.dot_general(
            adapter_params,
            adapter_up_weight,
            contract_final_axis,
            preferred_element_type=jnp.float32,
        )
    ).astype(jnp.bfloat16)
    head_query, head_keys, head_values, head_grads = (
        lax.all_to_all(query_rows, "seq", split_axis=2, concat_axis=1, tiled=True),
        lax.all_to_all(keys_dest, "seq", split_axis=2, concat_axis=1, tiled=True),
        lax.all_to_all(values_dest, "seq", split_axis=2, concat_axis=1, tiled=True),
        lax.all_to_all(output_gradient[0], "seq", split_axis=2, concat_axis=1, tiled=True),
    )
    length = head_query.shape[0] * head_query.shape[1]
    reach_rows = length // 2 + length // 8
    head_width = head_query.shape[2]
    segment = segments[0]
    head_query = head_query.reshape(length, head_width)
    head_keys = head_keys.reshape(length, head_width)
    head_values = head_values.reshape(length, head_width)
    head_grads = head_grads.reshape(length, head_width)
    dquery_head, log_head = attend_head(
        head_query, head_keys, head_values, head_grads, segment, CLIPS, reach_rows
    )
    norm_pieces = [log_head]
    log_norm = jnp.stack(norm_pieces, axis=0)
    query_gradient = lax.all_to_all(
        dquery_head.reshape(block_count, length // block_count, head_width),
        "seq",
        split_axis=1,
        concat_axis=2,
        tiled=True,
    )
    adapter_gradient = lax.dot_general(
        query_gradient,
        adapter_up_weight,
        (((2,), (1,)), ((), ())),
        preferred_element_type=jnp.float32,
    ).astype(jnp.bfloat16)
    contract_tokens = (((0, 1), (0, 1)), ((), ()))
    down_part = lax.dot_general(
        feature_dest, adapter_gradient, contract_tokens, preferred_element_type=jnp.float32
    )
    up_part = lax.dot_general(
        adapter_params, query_gradient, contract_tokens, preferred_element_type=jnp.float32
    )
    down_share, up_share = (
        lax.psum_scatter(down_part, "seq", scatter_dimension=0, tiled=True),
        lax.psum_scatter(up_part, "seq", scatter_dimension=1, tiled=True),
    )
    down_total, up_total = lax.psum((down_share, up_share), "dp")
    grad_norm = 4.0 / math.sqrt(group_count * length)
    return (down_total * grad_norm, up_total * grad_norm, log_norm[None])


def solution(mesh):
    in_specs = (
        P("dp", None, "seq", None),
        P("dp", None, "seq", None),
        P("dp", None, "seq", None),
        P("dp", None, "seq", None),
        P("dp", None, "seq", None),
        P(),
        P(),
        P(),
        P("dp", None),
    )
    out_specs = (P("seq", None), P(None, "seq"), P("dp", "seq", None))

    def whole(features, *rest):
        fits = fits_tiles(mesh, features, rest[5])
        return jax.shard_map(
            per_device_tiles if fits else per_device,
            mesh=mesh,
            in_specs=in_specs,
            out_specs=out_specs,
            check_vma=False,
        )(features, *rest)

    return whole
```

```python
import functools
import math

import jax
import jax.numpy as jnp
import numpy as np
from jax import lax
from jax.experimental import pallas as pl
from jax.experimental.pallas import tpu as pltpu
from jax.sharding import Mesh
from jax.sharding import PartitionSpec as P

CAP = 2
CLIPS = 2
LANES = 128
HALF = 64
CORES = 2
SEQ = ("chip", "core")
QUERIES = 640
LOG2E = math.log2(math.e)
VMEM = pl.BlockSpec(memory_space=pltpu.VMEM)
SMEM = pl.BlockSpec(memory_space=pltpu.SMEM)
ANY = pl.BlockSpec(memory_space=pl.ANY)
NT = (((1,), (1,)), ((), ()))


def low_lanes(rows):
    return lax.broadcasted_iota(jnp.int32, (rows, LANES), 1) < HALF


def swap_halves(tile):
    return pltpu.roll(tile, HALF, 1)


def lane_tile(index):
    return pl.ds(pl.multiple_of(index * LANES, LANES), LANES)


def row_tile(index, rows):
    return pl.ds(pl.multiple_of(index * rows, rows), rows)


def quotient(value, size):
    return lax.shift_right_logical(value, size.bit_length() - 1)


def remainder(value, size):
    return value & (size - 1)


def seq_index():
    return lax.axis_index("chip") * CORES + lax.axis_index("core")


def each_hit(plan, me, groups, blocks, live, put):
    def over_dest(dest, _):
        def over_position(position, slot):
            source = plan[dest, position]
            hit = quotient(source, blocks) == me

            @pl.when(hit)
            def _():
                put(dest, slot, remainder(source, blocks))

            return slot + hit.astype(jnp.int32)

        lax.fori_loop(0, live, over_position, jnp.int32(0))
        return 0

    lax.fori_loop(0, groups, over_dest, 0)


def each_block(plan, me, blocks, live, take):
    def over_position(position, _):
        group = quotient(plan[me, position], blocks)
        slot = jnp.int32(0)
        for other in range(live):
            same = (quotient(plan[me, other], blocks) == group) & (other < position)
            slot = slot + same.astype(jnp.int32)
        take(position, group, slot)
        return 0

    lax.fori_loop(0, live, over_position, 0)


def each_half(slot, store):
    @pl.when(remainder(slot, 2) == 0)
    def _():
        store(slice(0, HALF))

    @pl.when(remainder(slot, 2) == 1)
    def _():
        store(slice(HALF, LANES))


def split(slot, pair):
    pair = pair.astype(jnp.float32)
    return jnp.where(remainder(slot, 2) == 0, pair, swap_halves(pair))


def pack_far_kernel(dims, plan_hbm, feat_hbm, base_hbm, keys_hbm, vals_hbm, down_hbm, up_hbm, *rest):
    groups, blocks, heads, rows, live = dims
    far_hbm, queries_hbm, adapter_hbm = rest[:3]
    plan, routes, feat, base, keys, vals, down, up, far_out, qbuf, abuf, sems, out_sems = rest[3:]
    me = lax.axis_index("dp")
    copies = [
        pltpu.make_async_copy(source, target, sems.at[index])
        for index, (source, target) in enumerate(
            (
                (plan_hbm, plan),
                (keys_hbm, keys),
                (vals_hbm, vals),
                (feat_hbm, feat),
                (down_hbm, down),
                (base_hbm, base),
                (up_hbm, up),
            )
        )
    ]
    for copy in copies:
        copy.start()

    def put_early(dest, slot, local):
        @pl.when(slot < CAP)
        def _():
            index = routes[0, 0]
            routes[0, 0] = index + 1
            for row, value in enumerate((dest, slot, local)):
                routes[row + 1, index] = value
            for head in range(heads):
                columns = slice(head * LANES, (head + 1) * LANES)
                far_out[head * groups + dest, slot] = keys[local, :, columns]
                far_out[head * groups + dest, CAP + slot] = vals[local, :, columns]

    def send(first, count, index):
        tiles = pl.ds(first, count)
        copy = pltpu.make_async_copy(far_out.at[:, tiles], far_hbm.at[:, tiles], out_sems.at[index])
        copy.start()
        return copy

    for copy in copies[:3]:
        copy.wait()
    routes[0, 0] = 0
    each_hit(plan, me, groups, blocks, live, put_early)
    early = send(0, 2 * CAP, 0)
    for copy in copies[3:]:
        copy.wait()
    narrow = lax.dot_general(feat[...], down[...], NT, preferred_element_type=jnp.float32)
    adapter = narrow.astype(jnp.bfloat16)
    lift = jnp.dot(adapter, up[...], preferred_element_type=jnp.float32)
    abuf[...] = jnp.concatenate([narrow, narrow], axis=1).astype(jnp.bfloat16).reshape(abuf.shape)
    qbuf[...] = (base[...].astype(jnp.float32) + lift.reshape(base.shape)).astype(jnp.bfloat16)

    def put_late(index, _):
        dest, slot, local = routes[1, index], routes[2, index], routes[3, index]

        def store(lanes):
            for head in range(heads):
                columns = slice(head * LANES, (head + 1) * LANES)
                far_out[head * groups + dest, 2 * CAP + slot] = qbuf[local, :, columns]
                far_out[head * groups + dest, CAP * 3, :, lanes] = abuf[local, :, lanes]

        each_half(slot, store)
        return 0

    lax.fori_loop(0, routes[0, 0], put_late, 0)
    late = send(2 * CAP, CAP + 1, 1)
    rest_out = [
        pltpu.make_async_copy(qbuf, queries_hbm, out_sems.at[2]),
        pltpu.make_async_copy(abuf, adapter_hbm, out_sems.at[3]),
    ]
    for copy in rest_out:
        copy.start()
    for copy in [early, late] + rest_out:
        copy.wait()


def pack_own_kernel(dims, plan, keys, vals, grad, queries, adapter, *own_outs):
    groups, blocks, heads, rows, live = dims
    extras = live - CAP
    me = lax.axis_index("dp")
    seq = seq_index()
    sources = (keys, vals, queries)

    def put(dest, slot, local):
        @pl.when(slot >= CAP)
        def _():
            extra = slot - CAP
            where = extras * 3 + live + quotient(extra, 2)
            for turn in range(heads):
                columns = lane_tile(seq ^ turn)
                for index, source in enumerate(sources):
                    own_outs[turn][index * extras + extra] = source[local, :, columns]

            def store(lanes):
                for turn in range(heads):
                    own_outs[turn][where, :, lanes] = adapter[local, :, lanes]

            each_half(slot, store)

    each_hit(plan, me, groups, blocks, live, put)
    for turn in range(heads):
        columns = lane_tile(seq ^ turn)
        for position in range(live):
            own_outs[turn][extras * 3 + position] = grad[position, :, columns]


def attend_kernel(dims, plan, seg, up, far_in, *rest):
    groups, blocks, heads, rows, live = dims
    own_ins = rest[:heads]
    part_hbm = rest[heads]
    own_parts = rest[heads + 1 : heads + 1 + heads // CORES]
    up_out, log_hbm, part_out, log_out, routes, sems, qs, ks, vs, gs, ads, dqs, parts = rest[
        heads + 1 + heads // CORES :
    ]
    extras = live - CAP
    me = lax.axis_index("dp")
    seq = seq_index()
    rank = up.shape[0]
    length = seg.shape[1]
    reach = live * LANES
    scaling = 1.0 / math.sqrt(LANES)

    ads[...] = jnp.zeros_like(ads)

    def take(position, group, slot):
        routes[0, position] = group
        routes[1, position] = slot
        far = (group != me) | (slot < CAP)

        @pl.when(far)
        def _():
            for part in range(heads):
                index = part * groups + group
                where = row_tile(position * heads + part, rows)
                ks[where, :] = far_in[index, slot]
                vs[where, :] = far_in[index, CAP + slot]
                qs[where, :] = far_in[index, 2 * CAP + slot]

            def store(lanes):
                for part in range(heads):
                    where = row_tile(position * heads + part, rows)
                    ads[where, lanes] = far_in[part * groups + group, CAP * 3, :, lanes]

            each_half(slot, store)

        @pl.when(jnp.logical_not(far))
        def _():
            extra = slot - CAP
            pair = extras * 3 + live + quotient(extra, 2)
            for turn in range(heads):
                where = row_tile(position * heads + (seq ^ turn), rows)
                ks[where, :] = own_ins[turn][extra]
                vs[where, :] = own_ins[turn][extras + extra]
                qs[where, :] = own_ins[turn][2 * extras + extra]

            def store(lanes):
                for turn in range(heads):
                    where = row_tile(position * heads + (seq ^ turn), rows)
                    ads[where, lanes] = own_ins[turn][pair, :, lanes]

            each_half(slot, store)

    each_block(plan, me, blocks, live, take)
    for turn in range(heads):
        for position in range(live):
            gs[row_tile(position * heads + (seq ^ turn), rows), :] = own_ins[turn][
                extras * 3 + position
            ]

    count = jnp.sum((seg[...] < CLIPS - 1).astype(jnp.float32), axis=1, keepdims=True).astype(
        jnp.int32
    )
    key_rows = ks[...]
    value_rows = vs[...]
    key_columns = key_rows.T
    key_index = lax.broadcasted_iota(jnp.int32, (reach, 1), 0)
    always = length - reach
    up_head = up[:, lane_tile(seq)]
    up_twice = jnp.concatenate([up_head, up_head], axis=0)
    for start in range(0, reach, QUERIES):
        count_here = min(QUERIES, reach - start)
        span = slice(start, start + count_here)
        scores = lax.dot_general(key_rows, qs[span, :], NT, preferred_element_type=jnp.float32)
        scores = jnp.concatenate(
            [
                scores[:always],
                jnp.where(key_index[always:] < count, scores[always:], -1e30),
            ],
            axis=0,
        )
        dprob = lax.dot_general(value_rows, gs[span, :], NT, preferred_element_type=jnp.float32)
        maximum = jnp.max(scores, axis=0, keepdims=True)
        exponent = jnp.exp2((scores - maximum) * (scaling * LOG2E))
        total = jnp.sum(exponent, axis=0, keepdims=True)
        delta = jnp.sum(exponent * dprob, axis=0, keepdims=True) / total
        dscore = (exponent * (dprob - delta)).astype(jnp.bfloat16)
        dquery = jnp.dot(key_columns, dscore, preferred_element_type=jnp.float32)
        query_index = lax.broadcasted_iota(jnp.int32, (1, count_here), 1) + start
        in_clip = query_index < count
        dquery = jnp.where(in_clip, dquery * (scaling / total), 0.0).astype(jnp.bfloat16)
        dqs[:, span] = dquery
        log_out[0, :, span] = jnp.where(in_clip, maximum * scaling + jnp.log(total), 0.0)
    log_out[0, :, reach:] = jnp.zeros((1, length - reach), jnp.float32)
    log_copy = pltpu.make_async_copy(log_out, log_hbm, sems.at[0])
    log_copy.start()
    dquery_all = dqs[...]
    parts[...] = lax.dot_general(
        dquery_all, up_twice, (((0,), (1,)), ((), ())), preferred_element_type=jnp.float32
    ).astype(jnp.bfloat16)

    def put(position, _):
        group, slot = routes[0, position], routes[1, position]
        far = (group != me) | (slot < CAP)

        @pl.when(far)
        def _():
            def store(lanes):
                for part in range(heads):
                    where = row_tile(position * heads + part, rows)
                    part_out[part * groups + group, :, lanes] = parts[where, lanes]

            each_half(slot, store)

        @pl.when(jnp.logical_not(far))
        def _():
            pair = quotient(slot - CAP, 2)

            def store(lanes):
                for turn in range(heads):
                    where = row_tile(position * heads + (seq ^ turn), rows)
                    own_parts[turn // CORES][turn % CORES, pair, :, lanes] = parts[where, lanes]

            each_half(slot, store)

        return 0

    lax.fori_loop(0, live, put, 0)
    part_copy = pltpu.make_async_copy(part_out, part_hbm, sems.at[1])
    part_copy.start()
    up_part = jnp.dot(dquery_all, ads[...], preferred_element_type=jnp.float32)
    up_out[...] = (up_part + swap_halves(up_part)).T[:rank].astype(jnp.bfloat16)
    log_copy.wait()
    part_copy.wait()


def chip_sum_kernel(*refs):
    parts, outs = refs[:-CORES], refs[-CORES:]
    for core in range(CORES):
        total = parts[0][core].astype(jnp.float32)
        for part in parts[1:]:
            total = total + part[core].astype(jnp.float32)
        outs[core][...] = total.astype(jnp.bfloat16)


def product_kernel(dims, plan, parts, feat, own_mine, own_other, keep, send, sums, grads):
    groups, blocks, heads, rows, live = dims
    me = lax.axis_index("dp")
    for group in range(groups):
        total = parts[group].astype(jnp.float32)
        for head in range(1, heads):
            total = total + parts[head * groups + group].astype(jnp.float32)
        sums[group] = total
    for pair in range(own_mine.shape[0]):
        sums[groups + pair] = own_mine[pair].astype(jnp.float32) + own_other[pair].astype(
            jnp.float32
        )
    grads[...] = jnp.zeros_like(grads)

    def put(dest, slot, local):
        index = jnp.where(slot < CAP, dest, groups - 1 + quotient(slot, 2))
        grads[local] = split(slot, sums[index]).astype(jnp.bfloat16)

    each_hit(plan, me, groups, blocks, live, put)
    low = low_lanes(HALF // 2)
    columns = grads[...].reshape(blocks * rows, LANES).astype(jnp.float32).T[:HALF]
    columns = columns.astype(jnp.bfloat16)
    even = lax.axis_index("core") == 0
    for chip in range(heads // CORES):
        tiles = jnp.dot(
            columns,
            feat[:, chip * 5 * LANES : (chip + 1) * 5 * LANES],
            preferred_element_type=jnp.float32,
        )
        shared = tiles[:, 2 * LANES : 3 * LANES]
        upper, lower = shared[: HALF // 2], shared[HALF // 2 :]
        first = jnp.concatenate(
            [tiles[:, :LANES], tiles[:, LANES : 2 * LANES], jnp.where(low, upper, swap_halves(lower))],
            axis=0,
        )
        second = jnp.concatenate(
            [
                tiles[:, 3 * LANES : 4 * LANES],
                tiles[:, 4 * LANES :],
                jnp.where(low, swap_halves(upper), lower),
            ],
            axis=0,
        )
        keep[chip] = jnp.where(even, first, second).astype(jnp.bfloat16)
        send[chip] = jnp.where(even, second, first).astype(jnp.bfloat16)


def add_kernel(kept, received, out):
    for index in range(out.shape[0]):
        out[index] = (
            kept[index].astype(jnp.float32) + received[index].astype(jnp.float32)
        ).astype(jnp.bfloat16)


def join_kernel(parts, up_part, out):
    total = parts[0].astype(jnp.float32)
    for head in range(1, parts.shape[0]):
        total = total + parts[head].astype(jnp.float32)
    out[: total.shape[0]] = total.astype(jnp.bfloat16)
    out[total.shape[0] :] = up_part[...]


def total_kernel(grad_norm, *rest):
    groups = len(rest) - 3
    down_out, up_out, held = rest[groups:]
    me = lax.axis_index("dp")
    seq = seq_index()
    for turn in range(groups):
        held[me ^ turn] = rest[turn][...].astype(jnp.float32)
    total = held[0]
    for group in range(1, groups):
        total = total + held[group]
    total = total * grad_norm
    first, second = total[:HALF], total[HALF : 2 * HALF]
    shared = total[2 * HALF : 2 * HALF + HALF // 2]
    up_out[...] = total[2 * HALF + HALF // 2 :]
    swapped = swap_halves(shared)
    low_half = jnp.concatenate([shared, swapped], axis=0)
    high_half = jnp.concatenate([swapped, shared], axis=0)
    even = jnp.concatenate([first, second, low_half], axis=1)
    odd = pltpu.roll(jnp.concatenate([first, second, high_half], axis=1), HALF, 1)
    down = jnp.where(remainder(seq, 2) == 0, even, odd)
    down_out[...] = down[:, : down_out.shape[1]]


def call(kernel, outs, specs, scratch, flops, moved, *args, vmem_mib=32, out_specs=None):
    shapes = [jax.ShapeDtypeStruct(shape, dtype) for shape, dtype in outs]
    return pl.pallas_call(
        kernel,
        out_shape=shapes,
        in_specs=specs,
        out_specs=out_specs or [VMEM] * len(shapes),
        scratch_shapes=scratch,
        compiler_params=pltpu.CompilerParams(vmem_limit_bytes=vmem_mib << 20),
        cost_estimate=pl.CostEstimate(flops=flops, bytes_accessed=moved, transcendentals=0),
    )(*args)


def exchange(value, axis, size, turn):
    return lax.ppermute(value, axis, [(peer, peer ^ turn) for peer in range(size)])


def per_device_tiles(
    features,
    frozen_query_weight,
    source_keys,
    source_values,
    output_gradient,
    adapter_down_weight,
    adapter_up_weight,
    source_block_plan,
    segments,
):
    groups = lax.axis_size("dp")
    chips = lax.axis_size("chip")
    heads = chips * CORES
    _, blocks, rows, width = features.shape
    length = segments.shape[1]
    live = (length // 2 + length // 8) // LANES
    reach = live * LANES
    rank = adapter_up_weight.shape[0]
    extras = live - CAP
    pairs = (extras + 1) // 2
    dims = (groups, blocks, heads, rows, live)
    bf16 = jnp.bfloat16
    f32 = jnp.float32
    peers = groups * heads
    everyone = SEQ + ("dp",)
    flat = features[0].reshape(blocks * rows, width)
    far_shape = (peers, CAP * 3 + 1, rows, LANES)
    own_shape = (extras * 3 + live + pairs, rows, LANES)
    rows_shape = (blocks, rows, heads * LANES)

    far_send, queries, adapter = call(
        functools.partial(pack_far_kernel, dims),
        [(far_shape, bf16), (rows_shape, bf16), ((blocks, rows, LANES), bf16)],
        [ANY] * 7,
        [
            pltpu.SMEM((groups, blocks), jnp.int32),
            pltpu.SMEM((4, blocks), jnp.int32),
            pltpu.VMEM((blocks * rows, width), bf16),
            pltpu.VMEM(rows_shape, bf16),
            pltpu.VMEM(rows_shape, bf16),
            pltpu.VMEM(rows_shape, bf16),
            pltpu.VMEM((rank, width), bf16),
            pltpu.VMEM((rank, heads * LANES), bf16),
            pltpu.VMEM(far_shape, bf16),
            pltpu.VMEM(rows_shape, bf16),
            pltpu.VMEM((blocks, rows, LANES), bf16),
            pltpu.SemaphoreType.DMA((7,)),
            pltpu.SemaphoreType.DMA((4,)),
        ],
        60_000_000,
        4_000_000,
        source_block_plan,
        flat,
        frozen_query_weight[0],
        source_keys[0],
        source_values[0],
        adapter_down_weight.T,
        adapter_up_weight,
        vmem_mib=60,
        out_specs=[ANY] * 3,
    )
    own_send = call(
        functools.partial(pack_own_kernel, dims),
        [(own_shape, bf16)] * heads,
        [SMEM] + [VMEM] * 5,
        [],
        0,
        1_600_000,
        source_block_plan,
        source_keys[0],
        source_values[0],
        output_gradient[0],
        queries,
        adapter,
    )
    own = [own_send[0]] + [exchange(own_send[turn], SEQ, heads, turn) for turn in range(1, heads)]
    far = lax.all_to_all(far_send, everyone, 0, 0, tiled=True)
    attended = call(
        functools.partial(attend_kernel, dims),
        [((peers, rows, LANES), bf16)]
        + [((CORES, pairs, rows, LANES), bf16)] * (heads // CORES)
        + [((rank, LANES), bf16), ((1, 1, length), f32)],
        [SMEM] + [VMEM] * (3 + heads),
        [
            pltpu.VMEM((peers, rows, LANES), bf16),
            pltpu.VMEM((1, 1, length), f32),
            pltpu.SMEM((2, live), jnp.int32),
            pltpu.SemaphoreType.DMA((2,)),
        ]
        + [pltpu.VMEM((reach, LANES), bf16)] * 5
        + [pltpu.VMEM((LANES, reach), bf16), pltpu.VMEM((reach, LANES), bf16)],
        600_000_000,
        3_000_000,
        source_block_plan,
        segments,
        adapter_up_weight,
        far,
        *own,
        out_specs=[ANY] + [VMEM] * (chips + 1) + [ANY],
    )
    own_parts = [
        exchange(attended[1 + turn], "chip", chips, turn) for turn in range(chips - 1, 0, -1)
    ]
    own_mine, own_other = call(
        chip_sum_kernel,
        [((pairs, rows, LANES), bf16)] * CORES,
        [VMEM] * (heads // CORES),
        [],
        0,
        100_000,
        *own_parts,
        attended[1],
    )
    own_other = exchange(own_other, "core", CORES, 1)
    part = lax.all_to_all(attended[0], everyone, 0, 0, tiled=True)
    up_part, log_norm = attended[1 + heads // CORES :]
    keep, send = call(
        functools.partial(product_kernel, dims),
        [((chips, HALF * 5 // 2, LANES), bf16)] * 2,
        [SMEM] + [VMEM] * 4,
        [
            pltpu.VMEM((groups + pairs, rows, LANES), f32),
            pltpu.VMEM((blocks, rows, LANES), bf16),
        ],
        40_000_000,
        2_000_000,
        source_block_plan,
        part,
        flat,
        own_mine,
        own_other,
    )
    (shares,) = call(
        add_kernel,
        [((chips, HALF * 5 // 2, LANES), bf16)],
        [VMEM] * 2,
        [],
        0,
        600_000,
        keep,
        exchange(send, "core", CORES, 1),
    )
    shares = lax.all_to_all(shares, "chip", 0, 0, tiled=True)
    (joined,) = call(
        join_kernel,
        [((HALF * 5 // 2 + rank, LANES), bf16)],
        [VMEM] * 2,
        [],
        0,
        600_000,
        shares,
        up_part,
    )
    sums = [joined] + [exchange(joined, "dp", groups, turn) for turn in range(1, groups)]
    down, up = call(
        functools.partial(total_kernel, 4.0 / math.sqrt(groups * length)),
        [((rank, width // heads), f32), ((rank, LANES), f32)],
        [VMEM] * groups,
        [pltpu.VMEM((groups,) + joined.shape, f32)],
        0,
        400_000,
        *sums,
    )
    return (down.T, up, log_norm)


def power_of_two(size):
    return size > 1 and size & (size - 1) == 0


def fits_tiles(mesh, features, adapter_up_weight):
    groups, heads = mesh.shape["dp"], mesh.shape["seq"]
    rows = features.shape[2] // heads
    return (
        rows % 16 == 0
        and features.shape[2] == LANES
        and features.shape[3] * 2 == heads * 5 * LANES
        and power_of_two(heads)
        and power_of_two(groups)
        and power_of_two(features.shape[1])
        and adapter_up_weight.shape == (HALF, heads * LANES)
    )


def split_mesh(mesh):
    groups, heads = mesh.shape["dp"], mesh.shape["seq"]
    devices = np.asarray(mesh.devices).reshape(groups, heads // CORES, CORES)
    return Mesh(devices, ("dp",) + SEQ)


def tiles_solution(mesh):
    row_spec = P("dp", None, SEQ, None)
    return jax.shard_map(
        per_device_tiles,
        mesh=split_mesh(mesh),
        in_specs=(row_spec,) * 5 + (P(), P(), P(), P("dp", None)),
        out_specs=(P(SEQ, None), P(None, SEQ), P("dp", SEQ, None)),
        check_vma=False,
    )


def attend_head(query, key_rows, value_rows, cotangent, segment, clip_count, reach_rows):
    length = query.shape[0]
    width = query.shape[1]
    piece_count = 8
    piece_rows = reach_rows // piece_count
    scaling = 1.0 / math.sqrt(width)
    query_padded = jnp.pad(query, ((0, reach_rows), (0, 0)))
    grad_padded = jnp.pad(cotangent, ((0, reach_rows), (0, 0)))
    keys_padded = jnp.pad(key_rows, ((0, reach_rows), (0, 0)))
    values_padded = jnp.pad(value_rows, ((0, reach_rows), (0, 0)))
    segment_padded = jnp.pad(segment, (0, reach_rows), constant_values=-1)
    clip_ids = jnp.arange(clip_count, dtype=jnp.int32)
    starts = jnp.sum((segment[None, :] < clip_ids[:, None]).astype(jnp.int32), axis=1)

    def piece_pass(piece_index):
        clip_slice = piece_index // piece_count
        start = lax.dynamic_index_in_dim(starts, clip_slice, 0, keepdims=False)
        query_start = start + piece_index % piece_count * piece_rows
        query_tile = lax.dynamic_slice_in_dim(query_padded, query_start, piece_rows, 0)
        grad_tile = lax.dynamic_slice_in_dim(grad_padded, query_start, piece_rows, 0)
        seg_tile = lax.dynamic_slice_in_dim(segment_padded, query_start, piece_rows, 0)
        key_tile = lax.dynamic_slice_in_dim(keys_padded, start, reach_rows, 0)
        value_tile = lax.dynamic_slice_in_dim(values_padded, start, reach_rows, 0)
        seg_cols = lax.dynamic_slice_in_dim(segment_padded, start, reach_rows, 0)
        in_clip = seg_tile == clip_slice
        allowed = in_clip[:, None] & (seg_cols == clip_slice)[None, :]
        scores = (
            lax.dot_general(
                query_tile, key_tile, (((1,), (1,)), ((), ())), preferred_element_type=jnp.float32
            )
            * scaling
        )
        scores = jnp.where(allowed, scores, -1e30)
        maximum = jnp.max(scores, axis=1, keepdims=True)
        exponent = jnp.where(allowed, jnp.exp(scores - maximum), 0.0)
        totals = jnp.where(in_clip[:, None], jnp.sum(exponent, axis=1, keepdims=True), 1.0)
        log_norm = jnp.where(in_clip, maximum[:, 0] + jnp.log(totals[:, 0]), 0.0)
        probs = exponent / totals
        weights = probs.astype(jnp.bfloat16)
        attended = jnp.dot(weights, value_tile, preferred_element_type=jnp.float32)
        delta = jnp.sum(grad_tile.astype(jnp.float32) * attended, axis=1, keepdims=True)
        dprob = lax.dot_general(
            grad_tile, value_tile, (((1,), (1,)), ((), ())), preferred_element_type=jnp.float32
        )
        dscore = (probs * (dprob - delta)).astype(jnp.bfloat16)
        query_gradient = (
            jnp.dot(dscore, key_tile, preferred_element_type=jnp.float32) * scaling
        ).astype(jnp.bfloat16)
        query_gradient = jnp.where(in_clip[:, None], query_gradient, jnp.zeros((), jnp.bfloat16))
        return (query_gradient, log_norm, query_start)

    total_pieces = piece_count * (clip_count - 1)
    dquery_pieces, log_pieces, piece_starts = lax.map(
        piece_pass, jnp.arange(total_pieces, dtype=jnp.int32)
    )

    def place(index, carry):
        grad_total, log_total = carry
        where_at = lax.dynamic_index_in_dim(piece_starts, index, 0, keepdims=False)
        grad_piece = lax.dynamic_index_in_dim(dquery_pieces, index, 0, keepdims=False)
        log_piece = lax.dynamic_index_in_dim(log_pieces, index, 0, keepdims=False)
        grad_old = lax.dynamic_slice_in_dim(grad_total, where_at, piece_rows, 0)
        log_old = lax.dynamic_slice_in_dim(log_total, where_at, piece_rows, 0)
        grad_total = lax.dynamic_update_slice_in_dim(grad_total, grad_old + grad_piece, where_at, 0)
        log_total = lax.dynamic_update_slice_in_dim(log_total, log_old + log_piece, where_at, 0)
        return (grad_total, log_total)

    grad_init = jnp.zeros((length + reach_rows, width), jnp.bfloat16)
    log_init = jnp.zeros((length + reach_rows,), jnp.float32)
    grad_total, log_total = lax.fori_loop(0, total_pieces, place, (grad_init, log_init))
    return (grad_total[:length], log_total[:length])


def routing_tables(source_block_plan, group_index, cap_slots):
    group_count, block_count = source_block_plan.shape
    source_group = source_block_plan // block_count
    source_local = source_block_plan % block_count
    dest_groups = jnp.arange(group_count, dtype=jnp.int32)[:, None]
    outgoing = (source_group == group_index) & (dest_groups != group_index)
    out_rank = jnp.cumsum(outgoing.astype(jnp.int32), axis=1) - 1
    slot_ids = jnp.arange(cap_slots, dtype=jnp.int32)
    chosen = outgoing[:, :, None] & (out_rank[:, :, None] == slot_ids[None, None, :])
    send_index = jnp.sum(jnp.where(chosen, source_local[:, :, None], 0), axis=1)
    send_valid = jnp.any(chosen, axis=1)
    own_group = lax.dynamic_index_in_dim(source_group, group_index, 0, keepdims=False)
    own_local = lax.dynamic_index_in_dim(source_local, group_index, 0, keepdims=False)
    incoming = own_group != group_index
    positions = jnp.arange(block_count, dtype=jnp.int32)
    earlier = (own_group[None, :] == own_group[:, None]) & (positions[None, :] < positions[:, None])
    in_rank = jnp.sum(earlier.astype(jnp.int32), axis=1)
    return (send_index, send_valid, incoming, own_group, in_rank, own_local)


def pack_blocks(local, send_index, send_valid):
    picked = jnp.take(local, send_index, axis=0)
    return jnp.where(send_valid[:, :, None, None], picked, jnp.zeros((), local.dtype))


def unpack_blocks(received, local, tables, cap_slots):
    incoming, own_group, in_rank, own_local = tables
    flat = received.reshape((-1,) + received.shape[2:])
    slot_index = jnp.where(incoming, own_group * cap_slots + in_rank, 0)
    remote = jnp.take(flat, slot_index, axis=0)
    staying = jnp.take(local, own_local, axis=0)
    return jnp.where(incoming[:, None, None], remote, staying)


def per_device(
    features,
    frozen_query_weight,
    source_keys,
    source_values,
    output_gradient,
    adapter_down_weight,
    adapter_up_weight,
    source_block_plan,
    segments,
):
    group_count = lax.axis_size("dp")
    group_index = lax.axis_index("dp")
    block_count = features.shape[1]
    feat_local = features[0]
    base_local = frozen_query_weight[0]
    keys_local = source_keys[0]
    values_local = source_values[0]
    send_index, send_valid, incoming, own_group, in_rank, own_local = routing_tables(
        source_block_plan, group_index, CAP
    )
    tables = (incoming, own_group, in_rank, own_local)
    contract_final_axis = (((2,), (0,)), ((), ()))
    shuffled = (
        lax.all_to_all(
            pack_blocks(feat_local, send_index, send_valid),
            "dp",
            split_axis=0,
            concat_axis=0,
            tiled=True,
        ),
        lax.all_to_all(
            pack_blocks(base_local, send_index, send_valid),
            "dp",
            split_axis=0,
            concat_axis=0,
            tiled=True,
        ),
        lax.all_to_all(
            pack_blocks(keys_local, send_index, send_valid),
            "dp",
            split_axis=0,
            concat_axis=0,
            tiled=True,
        ),
        lax.all_to_all(
            pack_blocks(values_local, send_index, send_valid),
            "dp",
            split_axis=0,
            concat_axis=0,
            tiled=True,
        ),
    )
    feature_dest = unpack_blocks(shuffled[0], feat_local, tables, CAP)
    base_query_dest = unpack_blocks(shuffled[1], base_local, tables, CAP)
    keys_dest = unpack_blocks(shuffled[2], keys_local, tables, CAP)
    values_dest = unpack_blocks(shuffled[3], values_local, tables, CAP)
    adapter_params = lax.dot_general(
        feature_dest, adapter_down_weight, contract_final_axis, preferred_element_type=jnp.float32
    ).astype(jnp.bfloat16)
    query_rows = (
        base_query_dest.astype(jnp.float32)
        + lax.dot_general(
            adapter_params,
            adapter_up_weight,
            contract_final_axis,
            preferred_element_type=jnp.float32,
        )
    ).astype(jnp.bfloat16)
    head_query, head_keys, head_values, head_grads = (
        lax.all_to_all(query_rows, "seq", split_axis=2, concat_axis=1, tiled=True),
        lax.all_to_all(keys_dest, "seq", split_axis=2, concat_axis=1, tiled=True),
        lax.all_to_all(values_dest, "seq", split_axis=2, concat_axis=1, tiled=True),
        lax.all_to_all(output_gradient[0], "seq", split_axis=2, concat_axis=1, tiled=True),
    )
    length = head_query.shape[0] * head_query.shape[1]
    reach_rows = length // 2 + length // 8
    head_width = head_query.shape[2]
    segment = segments[0]
    head_query = head_query.reshape(length, head_width)
    head_keys = head_keys.reshape(length, head_width)
    head_values = head_values.reshape(length, head_width)
    head_grads = head_grads.reshape(length, head_width)
    dquery_head, log_head = attend_head(
        head_query, head_keys, head_values, head_grads, segment, CLIPS, reach_rows
    )
    norm_pieces = [log_head]
    log_norm = jnp.stack(norm_pieces, axis=0)
    query_gradient = lax.all_to_all(
        dquery_head.reshape(block_count, length // block_count, head_width),
        "seq",
        split_axis=1,
        concat_axis=2,
        tiled=True,
    )
    adapter_gradient = lax.dot_general(
        query_gradient,
        adapter_up_weight,
        (((2,), (1,)), ((), ())),
        preferred_element_type=jnp.float32,
    ).astype(jnp.bfloat16)
    contract_tokens = (((0, 1), (0, 1)), ((), ()))
    down_part = lax.dot_general(
        feature_dest, adapter_gradient, contract_tokens, preferred_element_type=jnp.float32
    )
    up_part = lax.dot_general(
        adapter_params, query_gradient, contract_tokens, preferred_element_type=jnp.float32
    )
    down_share, up_share = (
        lax.psum_scatter(down_part, "seq", scatter_dimension=0, tiled=True),
        lax.psum_scatter(up_part, "seq", scatter_dimension=1, tiled=True),
    )
    down_total, up_total = lax.psum((down_share, up_share), "dp")
    grad_norm = 4.0 / math.sqrt(group_count * length)
    return (down_total * grad_norm, up_total * grad_norm, log_norm[None])


def solution(mesh):
    in_specs = (
        P("dp", None, "seq", None),
        P("dp", None, "seq", None),
        P("dp", None, "seq", None),
        P("dp", None, "seq", None),
        P("dp", None, "seq", None),
        P(),
        P(),
        P(),
        P("dp", None),
    )
    out_specs = (P("seq", None), P(None, "seq"), P("dp", "seq", None))

    plain = jax.shard_map(
        per_device, mesh=mesh, in_specs=in_specs, out_specs=out_specs, check_vma=False
    )

    def whole(features, *rest):
        fits = fits_tiles(mesh, features, rest[5])
        return (tiles_solution(mesh) if fits else plain)(features, *rest)

    return whole
```

```python
import functools
import math

import jax
import jax.numpy as jnp
import numpy as np
from jax import lax
from jax.experimental import pallas as pl
from jax.experimental.pallas import tpu as pltpu
from jax.sharding import Mesh
from jax.sharding import PartitionSpec as P

CAP = 2
CLIPS = 2
LANES = 128
HALF = 64
CORES = 2
SEQ = ("chip", "core")
QUERIES = 640
LOG2E = math.log2(math.e)
VMEM = pl.BlockSpec(memory_space=pltpu.VMEM)
SMEM = pl.BlockSpec(memory_space=pltpu.SMEM)
ANY = pl.BlockSpec(memory_space=pl.ANY)
NT = (((1,), (1,)), ((), ()))


def low_lanes(rows):
    return lax.broadcasted_iota(jnp.int32, (rows, LANES), 1) < HALF


def swap_halves(tile):
    return pltpu.roll(tile, HALF, 1)


def lane_tile(index):
    return pl.ds(pl.multiple_of(index * LANES, LANES), LANES)


def row_tile(index, rows):
    return pl.ds(pl.multiple_of(index * rows, rows), rows)


def quotient(value, size):
    return lax.shift_right_logical(value, size.bit_length() - 1)


def remainder(value, size):
    return value & (size - 1)


def seq_index():
    return lax.axis_index("chip") * CORES + lax.axis_index("core")


def each_hit(plan, me, groups, blocks, live, put):
    def over_dest(dest, _):
        def over_position(position, slot):
            source = plan[dest, position]
            hit = quotient(source, blocks) == me

            @pl.when(hit)
            def _():
                put(dest, slot, remainder(source, blocks))

            return slot + hit.astype(jnp.int32)

        lax.fori_loop(0, live, over_position, jnp.int32(0))
        return 0

    lax.fori_loop(0, groups, over_dest, 0)


def each_block(plan, me, blocks, live, take):
    def over_position(position, _):
        group = quotient(plan[me, position], blocks)
        slot = jnp.int32(0)
        for other in range(live):
            same = (quotient(plan[me, other], blocks) == group) & (other < position)
            slot = slot + same.astype(jnp.int32)
        take(position, group, slot)
        return 0

    lax.fori_loop(0, live, over_position, 0)


def each_half(slot, store):
    @pl.when(remainder(slot, 2) == 0)
    def _():
        store(slice(0, HALF))

    @pl.when(remainder(slot, 2) == 1)
    def _():
        store(slice(HALF, LANES))


def split(slot, pair):
    pair = pair.astype(jnp.float32)
    return jnp.where(remainder(slot, 2) == 0, pair, swap_halves(pair))


def pack_far_kernel(dims, plan_hbm, feat_hbm, base_hbm, keys_hbm, vals_hbm, down_hbm, up_hbm, *rest):
    groups, blocks, heads, rows, live = dims
    far_hbm, queries_hbm, adapter_hbm = rest[:3]
    plan, routes, feat, base, keys, vals, down, up, far_out, qbuf, abuf, sems, out_sems = rest[3:]
    me = lax.axis_index("dp")
    copies = [
        pltpu.make_async_copy(source, target, sems.at[index])
        for index, (source, target) in enumerate(
            (
                (plan_hbm, plan),
                (keys_hbm, keys),
                (vals_hbm, vals),
                (feat_hbm, feat),
                (down_hbm, down),
                (base_hbm, base),
                (up_hbm, up),
            )
        )
    ]
    for copy in copies:
        copy.start()

    def put_early(dest, slot, local):
        @pl.when(slot < CAP)
        def _():
            index = routes[0, 0]
            routes[0, 0] = index + 1
            for row, value in enumerate((dest, slot, local)):
                routes[row + 1, index] = value
            for head in range(heads):
                columns = slice(head * LANES, (head + 1) * LANES)
                far_out[head * groups + dest, slot] = keys[local, :, columns]
                far_out[head * groups + dest, CAP + slot] = vals[local, :, columns]

    def send(first, count, index):
        tiles = pl.ds(first, count)
        copy = pltpu.make_async_copy(far_out.at[:, tiles], far_hbm.at[:, tiles], out_sems.at[index])
        copy.start()
        return copy

    for copy in copies[:3]:
        copy.wait()
    routes[0, 0] = 0
    each_hit(plan, me, groups, blocks, live, put_early)
    early = send(0, 2 * CAP, 0)
    for copy in copies[3:]:
        copy.wait()
    narrow = lax.dot_general(feat[...], down[...], NT, preferred_element_type=jnp.float32)
    adapter = narrow.astype(jnp.bfloat16)
    lift = jnp.dot(adapter, up[...], preferred_element_type=jnp.float32)
    abuf[...] = jnp.concatenate([narrow, narrow], axis=1).astype(jnp.bfloat16).reshape(abuf.shape)
    qbuf[...] = (base[...].astype(jnp.float32) + lift.reshape(base.shape)).astype(jnp.bfloat16)

    def put_late(index, _):
        dest, slot, local = routes[1, index], routes[2, index], routes[3, index]

        def store(lanes):
            for head in range(heads):
                columns = slice(head * LANES, (head + 1) * LANES)
                far_out[head * groups + dest, 2 * CAP + slot] = qbuf[local, :, columns]
                far_out[head * groups + dest, CAP * 3, :, lanes] = abuf[local, :, lanes]

        each_half(slot, store)
        return 0

    lax.fori_loop(0, routes[0, 0], put_late, 0)
    late = send(2 * CAP, CAP + 1, 1)
    rest_out = [
        pltpu.make_async_copy(qbuf, queries_hbm, out_sems.at[2]),
        pltpu.make_async_copy(abuf, adapter_hbm, out_sems.at[3]),
    ]
    for copy in rest_out:
        copy.start()
    for copy in [early, late] + rest_out:
        copy.wait()


def core_columns(chip, core):
    return pl.ds(pl.multiple_of((chip * 5 + core * 2) * LANES, LANES), 3 * LANES)


def pack_own_kernel(dims, plan, keys, vals, grad, queries, adapter, feat, *outs):
    groups, blocks, heads, rows, live = dims
    own_outs, feat_out = outs[:heads], outs[heads]
    for chip in range(heads // CORES):
        feat_out[chip] = feat[:, core_columns(chip, 1 - lax.axis_index("core"))]
    extras = live - CAP
    me = lax.axis_index("dp")
    seq = seq_index()
    sources = (keys, vals, queries)

    def put(dest, slot, local):
        @pl.when(slot >= CAP)
        def _():
            extra = slot - CAP
            where = extras * 3 + live + quotient(extra, 2)
            for turn in range(heads):
                columns = lane_tile(seq ^ turn)
                for index, source in enumerate(sources):
                    own_outs[turn][index * extras + extra] = source[local, :, columns]

            def store(lanes):
                for turn in range(heads):
                    own_outs[turn][where, :, lanes] = adapter[local, :, lanes]

            each_half(slot, store)

    each_hit(plan, me, groups, blocks, live, put)
    for turn in range(heads):
        columns = lane_tile(seq ^ turn)
        for position in range(live):
            own_outs[turn][extras * 3 + position] = grad[position, :, columns]


def attend_kernel(dims, plan, seg, up, far_in, *rest):
    groups, blocks, heads, rows, live = dims
    chips = heads // CORES
    own_ins = rest[:heads]
    part_hbm = rest[heads + 1]
    own_parts = rest[heads + 2 : heads + 2 + chips]
    up_out, log_hbm, part_out, log_out, routes, sems, qs, ks, vs, gs, ads, dqs, parts = rest[
        heads + 2 + chips :
    ]
    extras = live - CAP
    me = lax.axis_index("dp")
    seq = seq_index()
    rank = up.shape[0]
    length = seg.shape[1]
    reach = live * LANES
    scaling = 1.0 / math.sqrt(LANES)

    ads[...] = jnp.zeros_like(ads)

    def take(position, group, slot):
        routes[0, position] = group
        routes[1, position] = slot
        far = (group != me) | (slot < CAP)

        @pl.when(far)
        def _():
            for part in range(heads):
                index = part * groups + group
                where = row_tile(position * heads + part, rows)
                ks[where, :] = far_in[index, slot]
                vs[where, :] = far_in[index, CAP + slot]
                qs[where, :] = far_in[index, 2 * CAP + slot]

            def store(lanes):
                for part in range(heads):
                    where = row_tile(position * heads + part, rows)
                    ads[where, lanes] = far_in[part * groups + group, CAP * 3, :, lanes]

            each_half(slot, store)

        @pl.when(jnp.logical_not(far))
        def _():
            extra = slot - CAP
            pair = extras * 3 + live + quotient(extra, 2)
            for turn in range(heads):
                where = row_tile(position * heads + (seq ^ turn), rows)
                ks[where, :] = own_ins[turn][extra]
                vs[where, :] = own_ins[turn][extras + extra]
                qs[where, :] = own_ins[turn][2 * extras + extra]

            def store(lanes):
                for turn in range(heads):
                    where = row_tile(position * heads + (seq ^ turn), rows)
                    ads[where, lanes] = own_ins[turn][pair, :, lanes]

            each_half(slot, store)

    each_block(plan, me, blocks, live, take)
    for turn in range(heads):
        for position in range(live):
            gs[row_tile(position * heads + (seq ^ turn), rows), :] = own_ins[turn][
                extras * 3 + position
            ]

    count = jnp.sum((seg[...] < CLIPS - 1).astype(jnp.float32), axis=1, keepdims=True).astype(
        jnp.int32
    )
    key_rows = ks[...]
    value_rows = vs[...]
    key_columns = key_rows.T
    key_index = lax.broadcasted_iota(jnp.int32, (reach, 1), 0)
    always = length - reach
    up_head = up[:, lane_tile(seq)]
    up_twice = jnp.concatenate([up_head, up_head], axis=0)
    for start in range(0, reach, QUERIES):
        count_here = min(QUERIES, reach - start)
        span = slice(start, start + count_here)
        scores = lax.dot_general(key_rows, qs[span, :], NT, preferred_element_type=jnp.float32)
        scores = jnp.concatenate(
            [
                scores[:always],
                jnp.where(key_index[always:] < count, scores[always:], -1e30),
            ],
            axis=0,
        )
        dprob = lax.dot_general(value_rows, gs[span, :], NT, preferred_element_type=jnp.float32)
        maximum = jnp.max(scores, axis=0, keepdims=True)
        exponent = jnp.exp2((scores - maximum) * (scaling * LOG2E))
        total = jnp.sum(exponent, axis=0, keepdims=True)
        delta = jnp.sum(exponent * dprob, axis=0, keepdims=True) / total
        dscore = (exponent * (dprob - delta)).astype(jnp.bfloat16)
        dquery = jnp.dot(key_columns, dscore, preferred_element_type=jnp.float32)
        query_index = lax.broadcasted_iota(jnp.int32, (1, count_here), 1) + start
        in_clip = query_index < count
        dquery = jnp.where(in_clip, dquery * (scaling / total), 0.0).astype(jnp.bfloat16)
        dqs[:, span] = dquery
        log_out[0, :, span] = jnp.where(in_clip, maximum * scaling + jnp.log(total), 0.0)
    log_out[0, :, reach:] = jnp.zeros((1, length - reach), jnp.float32)
    log_copy = pltpu.make_async_copy(log_out, log_hbm, sems.at[0])
    log_copy.start()
    dquery_all = dqs[...]
    parts[...] = lax.dot_general(
        dquery_all, up_twice, (((0,), (1,)), ((), ())), preferred_element_type=jnp.float32
    ).astype(jnp.bfloat16)

    def put(position, _):
        group, slot = routes[0, position], routes[1, position]
        far = (group != me) | (slot < CAP)

        @pl.when(far)
        def _():
            def store(lanes):
                for part in range(heads):
                    where = row_tile(position * heads + part, rows)
                    part_out[part * groups + group, :, lanes] = parts[where, lanes]

            each_half(slot, store)

        @pl.when(jnp.logical_not(far))
        def _():
            pair = quotient(slot - CAP, 2)

            def store(lanes):
                for turn in range(heads):
                    where = row_tile(position * heads + (seq ^ turn), rows)
                    own_parts[turn // CORES][turn % CORES, pair, :, lanes] = parts[where, lanes]

            each_half(slot, store)

        return 0

    lax.fori_loop(0, live, put, 0)
    part_copy = pltpu.make_async_copy(part_out, part_hbm, sems.at[1])
    part_copy.start()
    up_part = jnp.dot(dquery_all, ads[...], preferred_element_type=jnp.float32)
    up_out[...] = (up_part + swap_halves(up_part)).T[:rank].astype(jnp.bfloat16)
    log_copy.wait()
    part_copy.wait()


def head_sum_kernel(parts, *refs):
    extras, out = refs[:-1], refs[-1]
    pairs = extras[0].shape[1]
    groups = out.shape[0] - CORES * pairs

    def total(terms):
        value = terms[0].astype(jnp.float32)
        for term in terms[1:]:
            value = value + term.astype(jnp.float32)
        return value.astype(jnp.bfloat16)

    for group in range(groups):
        out[group] = total([parts[peer] for peer in range(group, parts.shape[0], groups)])
    for core in range(CORES):
        for pair in range(pairs):
            out[groups + core * pairs + pair] = total([extra[core, pair] for extra in extras])


def product_kernel(dims, plan, feat, feat_other, mine, other, out, sums, grads):
    groups, blocks, heads, rows, live = dims
    me = lax.axis_index("dp")
    core = lax.axis_index("core")
    pairs = sums.shape[1] - groups
    for owner, (tiles, partner) in enumerate(((mine, other), (other, mine))):
        for group in range(groups):
            sums[owner, group] = tiles[group].astype(jnp.float32)
        for index in range(groups, groups + pairs):
            sums[owner, index] = tiles[index].astype(jnp.float32) + partner[index + pairs].astype(
                jnp.float32
            )
    grads[...] = jnp.zeros_like(grads)

    def put(dest, slot, local):
        index = jnp.where(slot < CAP, dest, groups - 1 + quotient(slot, 2))
        for owner in range(CORES):
            grads[owner, local] = split(slot, sums[owner, index])

    each_hit(plan, me, groups, blocks, live, put)
    low = low_lanes(HALF // 2)
    columns = [
        grads[owner].reshape(blocks * rows, LANES).T[:HALF].astype(jnp.bfloat16)
        for owner in range(CORES)
    ]
    even = core == 0
    for chip in range(heads // CORES):
        tiles = jnp.dot(
            columns[0], feat[:, core_columns(chip, core)], preferred_element_type=jnp.float32
        ) + jnp.dot(columns[1], feat_other[chip], preferred_element_type=jnp.float32)
        first, second, third = (
            tiles[:, index * LANES : (index + 1) * LANES] for index in range(3)
        )
        shared = jnp.where(even, third, first)
        upper, lower = shared[: HALF // 2], shared[HALF // 2 :]
        out[chip, :HALF] = jnp.where(even, first, second).astype(jnp.bfloat16)
        out[chip, HALF : 2 * HALF] = jnp.where(even, second, third).astype(jnp.bfloat16)
        out[chip, 2 * HALF :] = jnp.where(
            even,
            jnp.where(low, upper, swap_halves(lower)),
            jnp.where(low, swap_halves(upper), lower),
        ).astype(jnp.bfloat16)


def join_kernel(parts, up_part, out):
    total = parts[0].astype(jnp.float32)
    for head in range(1, parts.shape[0]):
        total = total + parts[head].astype(jnp.float32)
    out[: total.shape[0]] = total.astype(jnp.bfloat16)
    out[total.shape[0] :] = up_part[...]


def total_kernel(grad_norm, *rest):
    groups = len(rest) - 3
    down_out, up_out, held = rest[groups:]
    me = lax.axis_index("dp")
    seq = seq_index()
    for turn in range(groups):
        held[me ^ turn] = rest[turn][...].astype(jnp.float32)
    total = held[0]
    for group in range(1, groups):
        total = total + held[group]
    total = total * grad_norm
    first, second = total[:HALF], total[HALF : 2 * HALF]
    shared = total[2 * HALF : 2 * HALF + HALF // 2]
    up_out[...] = total[2 * HALF + HALF // 2 :]
    swapped = swap_halves(shared)
    low_half = jnp.concatenate([shared, swapped], axis=0)
    high_half = jnp.concatenate([swapped, shared], axis=0)
    even = jnp.concatenate([first, second, low_half], axis=1)
    odd = pltpu.roll(jnp.concatenate([first, second, high_half], axis=1), HALF, 1)
    down = jnp.where(remainder(seq, 2) == 0, even, odd)
    down_out[...] = down[:, : down_out.shape[1]]


def call(kernel, outs, specs, scratch, flops, moved, *args, vmem_mib=32, out_specs=None):
    shapes = [jax.ShapeDtypeStruct(shape, dtype) for shape, dtype in outs]
    return pl.pallas_call(
        kernel,
        out_shape=shapes,
        in_specs=specs,
        out_specs=out_specs or [VMEM] * len(shapes),
        scratch_shapes=scratch,
        compiler_params=pltpu.CompilerParams(vmem_limit_bytes=vmem_mib << 20),
        cost_estimate=pl.CostEstimate(flops=flops, bytes_accessed=moved, transcendentals=0),
    )(*args)


def exchange(value, axis, size, turn):
    return lax.ppermute(value, axis, [(peer, peer ^ turn) for peer in range(size)])


def per_device_tiles(
    features,
    frozen_query_weight,
    source_keys,
    source_values,
    output_gradient,
    adapter_down_weight,
    adapter_up_weight,
    source_block_plan,
    segments,
):
    groups = lax.axis_size("dp")
    chips = lax.axis_size("chip")
    heads = chips * CORES
    _, blocks, rows, width = features.shape
    length = segments.shape[1]
    live = (length // 2 + length // 8) // LANES
    reach = live * LANES
    rank = adapter_up_weight.shape[0]
    extras = live - CAP
    pairs = (extras + 1) // 2
    dims = (groups, blocks, heads, rows, live)
    bf16 = jnp.bfloat16
    f32 = jnp.float32
    peers = groups * heads
    everyone = SEQ + ("dp",)
    flat = features[0].reshape(blocks * rows, width)
    far_shape = (peers, CAP * 3 + 1, rows, LANES)
    own_shape = (extras * 3 + live + pairs, rows, LANES)
    rows_shape = (blocks, rows, heads * LANES)

    far_send, queries, adapter = call(
        functools.partial(pack_far_kernel, dims),
        [(far_shape, bf16), (rows_shape, bf16), ((blocks, rows, LANES), bf16)],
        [ANY] * 7,
        [
            pltpu.SMEM((groups, blocks), jnp.int32),
            pltpu.SMEM((4, blocks), jnp.int32),
            pltpu.VMEM((blocks * rows, width), bf16),
            pltpu.VMEM(rows_shape, bf16),
            pltpu.VMEM(rows_shape, bf16),
            pltpu.VMEM(rows_shape, bf16),
            pltpu.VMEM((rank, width), bf16),
            pltpu.VMEM((rank, heads * LANES), bf16),
            pltpu.VMEM(far_shape, bf16),
            pltpu.VMEM(rows_shape, bf16),
            pltpu.VMEM((blocks, rows, LANES), bf16),
            pltpu.SemaphoreType.DMA((7,)),
            pltpu.SemaphoreType.DMA((4,)),
        ],
        60_000_000,
        4_000_000,
        source_block_plan,
        flat,
        frozen_query_weight[0],
        source_keys[0],
        source_values[0],
        adapter_down_weight.T,
        adapter_up_weight,
        vmem_mib=60,
        out_specs=[ANY] * 3,
    )
    own_send = call(
        functools.partial(pack_own_kernel, dims),
        [(own_shape, bf16)] * heads + [((chips, blocks * rows, 3 * LANES), bf16)],
        [SMEM] + [VMEM] * 6,
        [],
        0,
        1_600_000,
        source_block_plan,
        source_keys[0],
        source_values[0],
        output_gradient[0],
        queries,
        adapter,
        flat,
    )
    feat_other = exchange(own_send[heads], "core", CORES, 1)
    own = [own_send[0]] + [exchange(own_send[turn], SEQ, heads, turn) for turn in range(1, heads)]
    far = lax.all_to_all(far_send, everyone, 0, 0, tiled=True)
    attended = call(
        functools.partial(attend_kernel, dims),
        [((peers, rows, LANES), bf16)]
        + [((CORES, pairs, rows, LANES), bf16)] * (heads // CORES)
        + [((rank, LANES), bf16), ((1, 1, length), f32)],
        [SMEM] + [VMEM] * (3 + heads) + [ANY],
        [
            pltpu.VMEM((peers, rows, LANES), bf16),
            pltpu.VMEM((1, 1, length), f32),
            pltpu.SMEM((2, live), jnp.int32),
            pltpu.SemaphoreType.DMA((2,)),
        ]
        + [pltpu.VMEM((reach, LANES), bf16)] * 5
        + [pltpu.VMEM((LANES, reach), bf16), pltpu.VMEM((reach, LANES), bf16)],
        600_000_000,
        3_000_000,
        source_block_plan,
        segments,
        adapter_up_weight,
        far,
        *own,
        feat_other,
        out_specs=[ANY] + [VMEM] * (chips + 1) + [ANY],
    )
    own_parts = [
        exchange(attended[1 + turn], "chip", chips, turn) for turn in range(chips - 1, 0, -1)
    ]
    part = lax.all_to_all(attended[0], everyone, 0, 0, tiled=True)
    up_part, log_norm = attended[1 + chips :]
    tiles = groups + CORES * pairs
    (mine,) = call(
        head_sum_kernel,
        [((tiles, rows, LANES), bf16)],
        [VMEM] * (1 + chips),
        [],
        0,
        300_000,
        part,
        *own_parts,
        attended[1],
    )
    (shares,) = call(
        functools.partial(product_kernel, dims),
        [((chips, HALF * 5 // 2, LANES), bf16)],
        [SMEM] + [VMEM] * 4,
        [
            pltpu.VMEM((CORES, groups + pairs, rows, LANES), f32),
            pltpu.VMEM((CORES, blocks, rows, LANES), f32),
        ],
        40_000_000,
        2_000_000,
        source_block_plan,
        flat,
        feat_other,
        mine,
        exchange(mine, "core", CORES, 1),
    )
    shares = lax.all_to_all(shares, "chip", 0, 0, tiled=True)
    (joined,) = call(
        join_kernel,
        [((HALF * 5 // 2 + rank, LANES), bf16)],
        [VMEM] * 2,
        [],
        0,
        600_000,
        shares,
        up_part,
    )
    sums = [joined] + [exchange(joined, "dp", groups, turn) for turn in range(1, groups)]
    down, up = call(
        functools.partial(total_kernel, 4.0 / math.sqrt(groups * length)),
        [((rank, width // heads), f32), ((rank, LANES), f32)],
        [VMEM] * groups,
        [pltpu.VMEM((groups,) + joined.shape, f32)],
        0,
        400_000,
        *sums,
    )
    return (down.T, up, log_norm)


def power_of_two(size):
    return size > 1 and size & (size - 1) == 0


def fits_tiles(mesh, features, adapter_up_weight):
    groups, heads = mesh.shape["dp"], mesh.shape["seq"]
    rows = features.shape[2] // heads
    return (
        rows % 16 == 0
        and features.shape[2] == LANES
        and features.shape[3] * 2 == heads * 5 * LANES
        and power_of_two(heads)
        and power_of_two(groups)
        and power_of_two(features.shape[1])
        and adapter_up_weight.shape == (HALF, heads * LANES)
    )


def split_mesh(mesh):
    groups, heads = mesh.shape["dp"], mesh.shape["seq"]
    devices = np.asarray(mesh.devices).reshape(groups, heads // CORES, CORES)
    return Mesh(devices, ("dp",) + SEQ)


def tiles_solution(mesh):
    row_spec = P("dp", None, SEQ, None)
    return jax.shard_map(
        per_device_tiles,
        mesh=split_mesh(mesh),
        in_specs=(row_spec,) * 5 + (P(), P(), P(), P("dp", None)),
        out_specs=(P(SEQ, None), P(None, SEQ), P("dp", SEQ, None)),
        check_vma=False,
    )


def attend_head(query, key_rows, value_rows, cotangent, segment, clip_count, reach_rows):
    length = query.shape[0]
    width = query.shape[1]
    piece_count = 8
    piece_rows = reach_rows // piece_count
    scaling = 1.0 / math.sqrt(width)
    query_padded = jnp.pad(query, ((0, reach_rows), (0, 0)))
    grad_padded = jnp.pad(cotangent, ((0, reach_rows), (0, 0)))
    keys_padded = jnp.pad(key_rows, ((0, reach_rows), (0, 0)))
    values_padded = jnp.pad(value_rows, ((0, reach_rows), (0, 0)))
    segment_padded = jnp.pad(segment, (0, reach_rows), constant_values=-1)
    clip_ids = jnp.arange(clip_count, dtype=jnp.int32)
    starts = jnp.sum((segment[None, :] < clip_ids[:, None]).astype(jnp.int32), axis=1)

    def piece_pass(piece_index):
        clip_slice = piece_index // piece_count
        start = lax.dynamic_index_in_dim(starts, clip_slice, 0, keepdims=False)
        query_start = start + piece_index % piece_count * piece_rows
        query_tile = lax.dynamic_slice_in_dim(query_padded, query_start, piece_rows, 0)
        grad_tile = lax.dynamic_slice_in_dim(grad_padded, query_start, piece_rows, 0)
        seg_tile = lax.dynamic_slice_in_dim(segment_padded, query_start, piece_rows, 0)
        key_tile = lax.dynamic_slice_in_dim(keys_padded, start, reach_rows, 0)
        value_tile = lax.dynamic_slice_in_dim(values_padded, start, reach_rows, 0)
        seg_cols = lax.dynamic_slice_in_dim(segment_padded, start, reach_rows, 0)
        in_clip = seg_tile == clip_slice
        allowed = in_clip[:, None] & (seg_cols == clip_slice)[None, :]
        scores = (
            lax.dot_general(
                query_tile, key_tile, (((1,), (1,)), ((), ())), preferred_element_type=jnp.float32
            )
            * scaling
        )
        scores = jnp.where(allowed, scores, -1e30)
        maximum = jnp.max(scores, axis=1, keepdims=True)
        exponent = jnp.where(allowed, jnp.exp(scores - maximum), 0.0)
        totals = jnp.where(in_clip[:, None], jnp.sum(exponent, axis=1, keepdims=True), 1.0)
        log_norm = jnp.where(in_clip, maximum[:, 0] + jnp.log(totals[:, 0]), 0.0)
        probs = exponent / totals
        weights = probs.astype(jnp.bfloat16)
        attended = jnp.dot(weights, value_tile, preferred_element_type=jnp.float32)
        delta = jnp.sum(grad_tile.astype(jnp.float32) * attended, axis=1, keepdims=True)
        dprob = lax.dot_general(
            grad_tile, value_tile, (((1,), (1,)), ((), ())), preferred_element_type=jnp.float32
        )
        dscore = (probs * (dprob - delta)).astype(jnp.bfloat16)
        query_gradient = (
            jnp.dot(dscore, key_tile, preferred_element_type=jnp.float32) * scaling
        ).astype(jnp.bfloat16)
        query_gradient = jnp.where(in_clip[:, None], query_gradient, jnp.zeros((), jnp.bfloat16))
        return (query_gradient, log_norm, query_start)

    total_pieces = piece_count * (clip_count - 1)
    dquery_pieces, log_pieces, piece_starts = lax.map(
        piece_pass, jnp.arange(total_pieces, dtype=jnp.int32)
    )

    def place(index, carry):
        grad_total, log_total = carry
        where_at = lax.dynamic_index_in_dim(piece_starts, index, 0, keepdims=False)
        grad_piece = lax.dynamic_index_in_dim(dquery_pieces, index, 0, keepdims=False)
        log_piece = lax.dynamic_index_in_dim(log_pieces, index, 0, keepdims=False)
        grad_old = lax.dynamic_slice_in_dim(grad_total, where_at, piece_rows, 0)
        log_old = lax.dynamic_slice_in_dim(log_total, where_at, piece_rows, 0)
        grad_total = lax.dynamic_update_slice_in_dim(grad_total, grad_old + grad_piece, where_at, 0)
        log_total = lax.dynamic_update_slice_in_dim(log_total, log_old + log_piece, where_at, 0)
        return (grad_total, log_total)

    grad_init = jnp.zeros((length + reach_rows, width), jnp.bfloat16)
    log_init = jnp.zeros((length + reach_rows,), jnp.float32)
    grad_total, log_total = lax.fori_loop(0, total_pieces, place, (grad_init, log_init))
    return (grad_total[:length], log_total[:length])


def routing_tables(source_block_plan, group_index, cap_slots):
    group_count, block_count = source_block_plan.shape
    source_group = source_block_plan // block_count
    source_local = source_block_plan % block_count
    dest_groups = jnp.arange(group_count, dtype=jnp.int32)[:, None]
    outgoing = (source_group == group_index) & (dest_groups != group_index)
    out_rank = jnp.cumsum(outgoing.astype(jnp.int32), axis=1) - 1
    slot_ids = jnp.arange(cap_slots, dtype=jnp.int32)
    chosen = outgoing[:, :, None] & (out_rank[:, :, None] == slot_ids[None, None, :])
    send_index = jnp.sum(jnp.where(chosen, source_local[:, :, None], 0), axis=1)
    send_valid = jnp.any(chosen, axis=1)
    own_group = lax.dynamic_index_in_dim(source_group, group_index, 0, keepdims=False)
    own_local = lax.dynamic_index_in_dim(source_local, group_index, 0, keepdims=False)
    incoming = own_group != group_index
    positions = jnp.arange(block_count, dtype=jnp.int32)
    earlier = (own_group[None, :] == own_group[:, None]) & (positions[None, :] < positions[:, None])
    in_rank = jnp.sum(earlier.astype(jnp.int32), axis=1)
    return (send_index, send_valid, incoming, own_group, in_rank, own_local)


def pack_blocks(local, send_index, send_valid):
    picked = jnp.take(local, send_index, axis=0)
    return jnp.where(send_valid[:, :, None, None], picked, jnp.zeros((), local.dtype))


def unpack_blocks(received, local, tables, cap_slots):
    incoming, own_group, in_rank, own_local = tables
    flat = received.reshape((-1,) + received.shape[2:])
    slot_index = jnp.where(incoming, own_group * cap_slots + in_rank, 0)
    remote = jnp.take(flat, slot_index, axis=0)
    staying = jnp.take(local, own_local, axis=0)
    return jnp.where(incoming[:, None, None], remote, staying)


def per_device(
    features,
    frozen_query_weight,
    source_keys,
    source_values,
    output_gradient,
    adapter_down_weight,
    adapter_up_weight,
    source_block_plan,
    segments,
):
    group_count = lax.axis_size("dp")
    group_index = lax.axis_index("dp")
    block_count = features.shape[1]
    feat_local = features[0]
    base_local = frozen_query_weight[0]
    keys_local = source_keys[0]
    values_local = source_values[0]
    send_index, send_valid, incoming, own_group, in_rank, own_local = routing_tables(
        source_block_plan, group_index, CAP
    )
    tables = (incoming, own_group, in_rank, own_local)
    contract_final_axis = (((2,), (0,)), ((), ()))
    shuffled = (
        lax.all_to_all(
            pack_blocks(feat_local, send_index, send_valid),
            "dp",
            split_axis=0,
            concat_axis=0,
            tiled=True,
        ),
        lax.all_to_all(
            pack_blocks(base_local, send_index, send_valid),
            "dp",
            split_axis=0,
            concat_axis=0,
            tiled=True,
        ),
        lax.all_to_all(
            pack_blocks(keys_local, send_index, send_valid),
            "dp",
            split_axis=0,
            concat_axis=0,
            tiled=True,
        ),
        lax.all_to_all(
            pack_blocks(values_local, send_index, send_valid),
            "dp",
            split_axis=0,
            concat_axis=0,
            tiled=True,
        ),
    )
    feature_dest = unpack_blocks(shuffled[0], feat_local, tables, CAP)
    base_query_dest = unpack_blocks(shuffled[1], base_local, tables, CAP)
    keys_dest = unpack_blocks(shuffled[2], keys_local, tables, CAP)
    values_dest = unpack_blocks(shuffled[3], values_local, tables, CAP)
    adapter_params = lax.dot_general(
        feature_dest, adapter_down_weight, contract_final_axis, preferred_element_type=jnp.float32
    ).astype(jnp.bfloat16)
    query_rows = (
        base_query_dest.astype(jnp.float32)
        + lax.dot_general(
            adapter_params,
            adapter_up_weight,
            contract_final_axis,
            preferred_element_type=jnp.float32,
        )
    ).astype(jnp.bfloat16)
    head_query, head_keys, head_values, head_grads = (
        lax.all_to_all(query_rows, "seq", split_axis=2, concat_axis=1, tiled=True),
        lax.all_to_all(keys_dest, "seq", split_axis=2, concat_axis=1, tiled=True),
        lax.all_to_all(values_dest, "seq", split_axis=2, concat_axis=1, tiled=True),
        lax.all_to_all(output_gradient[0], "seq", split_axis=2, concat_axis=1, tiled=True),
    )
    length = head_query.shape[0] * head_query.shape[1]
    reach_rows = length // 2 + length // 8
    head_width = head_query.shape[2]
    segment = segments[0]
    head_query = head_query.reshape(length, head_width)
    head_keys = head_keys.reshape(length, head_width)
    head_values = head_values.reshape(length, head_width)
    head_grads = head_grads.reshape(length, head_width)
    dquery_head, log_head = attend_head(
        head_query, head_keys, head_values, head_grads, segment, CLIPS, reach_rows
    )
    norm_pieces = [log_head]
    log_norm = jnp.stack(norm_pieces, axis=0)
    query_gradient = lax.all_to_all(
        dquery_head.reshape(block_count, length // block_count, head_width),
        "seq",
        split_axis=1,
        concat_axis=2,
        tiled=True,
    )
    adapter_gradient = lax.dot_general(
        query_gradient,
        adapter_up_weight,
        (((2,), (1,)), ((), ())),
        preferred_element_type=jnp.float32,
    ).astype(jnp.bfloat16)
    contract_tokens = (((0, 1), (0, 1)), ((), ()))
    down_part = lax.dot_general(
        feature_dest, adapter_gradient, contract_tokens, preferred_element_type=jnp.float32
    )
    up_part = lax.dot_general(
        adapter_params, query_gradient, contract_tokens, preferred_element_type=jnp.float32
    )
    down_share, up_share = (
        lax.psum_scatter(down_part, "seq", scatter_dimension=0, tiled=True),
        lax.psum_scatter(up_part, "seq", scatter_dimension=1, tiled=True),
    )
    down_total, up_total = lax.psum((down_share, up_share), "dp")
    grad_norm = 4.0 / math.sqrt(group_count * length)
    return (down_total * grad_norm, up_total * grad_norm, log_norm[None])


def solution(mesh):
    in_specs = (
        P("dp", None, "seq", None),
        P("dp", None, "seq", None),
        P("dp", None, "seq", None),
        P("dp", None, "seq", None),
        P("dp", None, "seq", None),
        P(),
        P(),
        P(),
        P("dp", None),
    )
    out_specs = (P("seq", None), P(None, "seq"), P("dp", "seq", None))

    plain = jax.shard_map(
        per_device, mesh=mesh, in_specs=in_specs, out_specs=out_specs, check_vma=False
    )

    def whole(features, *rest):
        fits = fits_tiles(mesh, features, rest[5])
        return (tiles_solution(mesh) if fits else plain)(features, *rest)

    return whole
```

```python
import functools
import math

import jax
import jax.numpy as jnp
import numpy as np
from jax import lax
from jax.experimental import pallas as pl
from jax.experimental.pallas import tpu as pltpu
from jax.sharding import Mesh
from jax.sharding import PartitionSpec as P

CAP = 2
CLIPS = 2
LANES = 128
HALF = 64
CORES = 2
SEQ = ("chip", "core")
QUERIES = 640
LOG2E = math.log2(math.e)
VMEM = pl.BlockSpec(memory_space=pltpu.VMEM)
SMEM = pl.BlockSpec(memory_space=pltpu.SMEM)
ANY = pl.BlockSpec(memory_space=pl.ANY)
NT = (((1,), (1,)), ((), ()))


def low_lanes(rows):
    return lax.broadcasted_iota(jnp.int32, (rows, LANES), 1) < HALF


def swap_halves(tile):
    return pltpu.roll(tile, HALF, 1)


def lane_tile(index):
    return pl.ds(pl.multiple_of(index * LANES, LANES), LANES)


def row_tile(index, rows):
    return pl.ds(pl.multiple_of(index * rows, rows), rows)


def quotient(value, size):
    return lax.shift_right_logical(value, size.bit_length() - 1)


def remainder(value, size):
    return value & (size - 1)


def seq_index():
    return lax.axis_index("chip") * CORES + lax.axis_index("core")


def each_hit(plan, me, groups, blocks, live, put):
    def over_dest(dest, _):
        def over_position(position, slot):
            source = plan[dest, position]
            hit = quotient(source, blocks) == me

            @pl.when(hit)
            def _():
                put(dest, slot, remainder(source, blocks))

            return slot + hit.astype(jnp.int32)

        lax.fori_loop(0, live, over_position, jnp.int32(0))
        return 0

    lax.fori_loop(0, groups, over_dest, 0)


def each_block(plan, me, blocks, live, take):
    def over_position(position, _):
        group = quotient(plan[me, position], blocks)
        slot = jnp.int32(0)
        for other in range(live):
            same = (quotient(plan[me, other], blocks) == group) & (other < position)
            slot = slot + same.astype(jnp.int32)
        take(position, group, slot)
        return 0

    lax.fori_loop(0, live, over_position, 0)


def each_half(slot, store):
    @pl.when(remainder(slot, 2) == 0)
    def _():
        store(slice(0, HALF))

    @pl.when(remainder(slot, 2) == 1)
    def _():
        store(slice(HALF, LANES))


def split(slot, pair):
    pair = pair.astype(jnp.float32)
    return jnp.where(remainder(slot, 2) == 0, pair, swap_halves(pair))


def pack_far_kernel(dims, plan_hbm, feat_hbm, base_hbm, keys_hbm, vals_hbm, down_hbm, up_hbm, *rest):
    groups, blocks, heads, rows, live = dims
    far_hbm, queries_hbm, adapter_hbm = rest[:3]
    plan, routes, feat, base, keys, vals, down, up, far_out, qbuf, abuf, sems, out_sems = rest[3:]
    me = lax.axis_index("dp")
    copies = [
        pltpu.make_async_copy(source, target, sems.at[index])
        for index, (source, target) in enumerate(
            (
                (plan_hbm, plan),
                (keys_hbm, keys),
                (vals_hbm, vals),
                (feat_hbm, feat),
                (down_hbm, down),
                (base_hbm, base),
                (up_hbm, up),
            )
        )
    ]
    for copy in copies:
        copy.start()

    def put_early(dest, slot, local):
        @pl.when(slot < CAP)
        def _():
            index = routes[0, 0]
            routes[0, 0] = index + 1
            for row, value in enumerate((dest, slot, local)):
                routes[row + 1, index] = value
            for head in range(heads):
                columns = slice(head * LANES, (head + 1) * LANES)
                far_out[head * groups + dest, slot] = keys[local, :, columns]
                far_out[head * groups + dest, CAP + slot] = vals[local, :, columns]

    def send(first, count, index):
        tiles = pl.ds(first, count)
        copy = pltpu.make_async_copy(far_out.at[:, tiles], far_hbm.at[:, tiles], out_sems.at[index])
        copy.start()
        return copy

    for copy in copies[:3]:
        copy.wait()
    routes[0, 0] = 0
    each_hit(plan, me, groups, blocks, live, put_early)
    early = send(0, 2 * CAP, 0)
    for copy in copies[3:]:
        copy.wait()
    narrow = lax.dot_general(feat[...], down[...], NT, preferred_element_type=jnp.float32)
    adapter = narrow.astype(jnp.bfloat16)
    lift = jnp.dot(adapter, up[...], preferred_element_type=jnp.float32)
    abuf[...] = jnp.concatenate([narrow, narrow], axis=1).astype(jnp.bfloat16).reshape(abuf.shape)
    qbuf[...] = (base[...].astype(jnp.float32) + lift.reshape(base.shape)).astype(jnp.bfloat16)

    def put_late(index, _):
        dest, slot, local = routes[1, index], routes[2, index], routes[3, index]

        for head in range(heads):
            columns = slice(head * LANES, (head + 1) * LANES)
            far_out[head * groups + dest, 2 * CAP + slot] = qbuf[local, :, columns]
        return 0

    lax.fori_loop(0, routes[0, 0], put_late, 0)
    late = send(2 * CAP, CAP, 1)
    rest_out = [
        pltpu.make_async_copy(qbuf, queries_hbm, out_sems.at[2]),
        pltpu.make_async_copy(abuf, adapter_hbm, out_sems.at[3]),
    ]
    for copy in rest_out:
        copy.start()
    for copy in [early, late] + rest_out:
        copy.wait()


def core_columns(chip, core):
    return pl.ds(pl.multiple_of((chip * 5 + core * 2) * LANES, LANES), 3 * LANES)


def pack_own_kernel(dims, plan, keys, vals, grad, queries, adapter, feat, *outs):
    groups, blocks, heads, rows, live = dims
    own_outs, feat_out, adapter_out = outs[:heads], outs[heads], outs[heads + 1]
    for chip in range(heads // CORES):
        feat_out[chip] = feat[:, core_columns(chip, 1 - lax.axis_index("core"))]
    extras = live - CAP
    me = lax.axis_index("dp")
    seq = seq_index()
    sources = (keys, vals, queries)

    def put(dest, slot, local):
        @pl.when(slot < CAP)
        def _():
            def store(lanes):
                adapter_out[dest, :, lanes] = adapter[local, :, lanes]

            each_half(slot, store)

        @pl.when(slot >= CAP)
        def _():
            extra = slot - CAP
            where = extras * 3 + live + quotient(extra, 2)
            for turn in range(heads):
                columns = lane_tile(seq ^ turn)
                for index, source in enumerate(sources):
                    own_outs[turn][index * extras + extra] = source[local, :, columns]

            def store(lanes):
                for turn in range(heads):
                    own_outs[turn][where, :, lanes] = adapter[local, :, lanes]

            each_half(slot, store)

    each_hit(plan, me, groups, blocks, live, put)
    for turn in range(heads):
        columns = lane_tile(seq ^ turn)
        for position in range(live):
            own_outs[turn][extras * 3 + position] = grad[position, :, columns]


def attend_kernel(dims, plan, seg, up, adapter, far_in, *rest):
    groups, blocks, heads, rows, live = dims
    chips = heads // CORES
    core = lax.axis_index("core")
    own_ins = rest[:heads]
    part_hbm = rest[heads + 1]
    own_parts = rest[heads + 2 : heads + 2 + chips]
    dqs, log_hbm, part_out, log_out, routes, sems, qs, ks, vs, gs, parts = rest[
        heads + 2 + chips :
    ]
    extras = live - CAP
    me = lax.axis_index("dp")
    seq = seq_index()
    length = seg.shape[1]
    reach = live * LANES
    scaling = 1.0 / math.sqrt(LANES)

    def take(position, group, slot):
        routes[0, position] = group
        routes[1, position] = slot
        far = (group != me) | (slot < CAP)

        @pl.when(far)
        def _():
            for part in range(heads):
                index = part * groups + group
                where = row_tile(position * heads + part, rows)
                ks[where, :] = far_in[index, slot]
                vs[where, :] = far_in[index, CAP + slot]
                qs[where, :] = far_in[index, 2 * CAP + slot]

        @pl.when(jnp.logical_not(far))
        def _():
            extra = slot - CAP
            for turn in range(heads):
                where = row_tile(position * heads + (seq ^ turn), rows)
                ks[where, :] = own_ins[turn][extra]
                vs[where, :] = own_ins[turn][extras + extra]
                qs[where, :] = own_ins[turn][2 * extras + extra]

    each_block(plan, me, blocks, live, take)
    for turn in range(heads):
        for position in range(live):
            gs[row_tile(position * heads + (seq ^ turn), rows), :] = own_ins[turn][
                extras * 3 + position
            ]

    count = jnp.sum((seg[...] < CLIPS - 1).astype(jnp.float32), axis=1, keepdims=True).astype(
        jnp.int32
    )
    key_rows = ks[...]
    value_rows = vs[...]
    key_columns = key_rows.T
    key_index = lax.broadcasted_iota(jnp.int32, (reach, 1), 0)
    always = length - reach
    up_head = up[:, lane_tile(seq)]
    up_twice = jnp.concatenate([up_head, up_head], axis=0)
    for start in range(0, reach, QUERIES):
        count_here = min(QUERIES, reach - start)
        span = slice(start, start + count_here)
        scores = lax.dot_general(key_rows, qs[span, :], NT, preferred_element_type=jnp.float32)
        scores = jnp.concatenate(
            [
                scores[:always],
                jnp.where(key_index[always:] < count, scores[always:], -1e30),
            ],
            axis=0,
        )
        dprob = lax.dot_general(value_rows, gs[span, :], NT, preferred_element_type=jnp.float32)
        maximum = jnp.max(scores, axis=0, keepdims=True)
        exponent = jnp.exp2((scores - maximum) * (scaling * LOG2E))
        total = jnp.sum(exponent, axis=0, keepdims=True)
        delta = jnp.sum(exponent * dprob, axis=0, keepdims=True) / total
        dscore = (exponent * (dprob - delta)).astype(jnp.bfloat16)
        dquery = jnp.dot(key_columns, dscore, preferred_element_type=jnp.float32)
        query_index = lax.broadcasted_iota(jnp.int32, (1, count_here), 1) + start
        in_clip = query_index < count
        dquery = jnp.where(in_clip, dquery * (scaling / total), 0.0).astype(jnp.bfloat16)
        dqs[:, span] = dquery
        log_out[0, :, span] = jnp.where(in_clip, maximum * scaling + jnp.log(total), 0.0)
    log_out[0, :, reach:] = jnp.zeros((1, length - reach), jnp.float32)
    log_copy = pltpu.make_async_copy(log_out, log_hbm, sems.at[0])
    log_copy.start()
    dquery_all = dqs[...]
    parts[...] = lax.dot_general(
        dquery_all, up_twice, (((0,), (1,)), ((), ())), preferred_element_type=jnp.float32
    ).astype(jnp.bfloat16)

    def put(position, _):
        group, slot = routes[0, position], routes[1, position]
        far = (group != me) | (slot < CAP)

        @pl.when(far)
        def _():
            def store(lanes):
                for turn in range(heads):
                    chip, side = turn // CORES, turn % CORES
                    where = row_tile(position * heads + chip * CORES + (core ^ side), rows)
                    part_out[chip * groups + group, side, :, lanes] = parts[where, lanes]

            each_half(slot, store)

        @pl.when(jnp.logical_not(far))
        def _():
            pair = quotient(slot - CAP, 2)

            def store(lanes):
                for turn in range(heads):
                    where = row_tile(position * heads + (seq ^ turn), rows)
                    own_parts[turn // CORES][turn % CORES, pair, :, lanes] = parts[where, lanes]

            each_half(slot, store)

        return 0

    lax.fori_loop(0, live, put, 0)
    for chip in range(chips):
        for group in range(groups):
            part_out[chip * groups + group, CORES] = adapter[group]
    part_copy = pltpu.make_async_copy(part_out, part_hbm, sems.at[1])
    part_copy.start()
    log_copy.wait()
    part_copy.wait()


def head_sum_kernel(parts, *refs):
    extras, out = refs[:-1], refs[-1]
    pairs = extras[0].shape[1]
    peers = parts.shape[0]
    tiles = (out.shape[0] - peers) // CORES
    groups = tiles - pairs

    def total(terms):
        value = terms[0].astype(jnp.float32)
        for term in terms[1:]:
            value = value + term.astype(jnp.float32)
        return value.astype(jnp.bfloat16)

    for side in range(CORES):
        for group in range(groups):
            out[side * tiles + group] = total(
                [parts[peer, side] for peer in range(group, peers, groups)]
            )
        for pair in range(pairs):
            out[side * tiles + groups + pair] = total([extra[side, pair] for extra in extras])
    for peer in range(peers):
        out[CORES * tiles + peer] = parts[peer, CORES]


def product_kernel(dims, plan, feat, feat_other, mine, other, dquery, *rest):
    groups, blocks, heads, rows, live = dims
    own_ins = rest[:heads]
    out, up_out, sums, grads, ads = rest[heads:]
    extras = live - CAP
    me = lax.axis_index("dp")
    core = lax.axis_index("core")
    seq = seq_index()
    tiles = sums.shape[1]
    ads[...] = jnp.zeros_like(ads)

    def take(position, group, slot):
        far = (group != me) | (slot < CAP)

        @pl.when(far)
        def _():
            def store(lanes):
                for chip in range(heads // CORES):
                    tile = CORES * tiles + chip * groups + group
                    for source, which in ((mine, core), (other, 1 - core)):
                        where = row_tile(position * heads + chip * CORES + which, rows)
                        ads[where, lanes] = source[tile, :, lanes]

            each_half(slot, store)

        @pl.when(jnp.logical_not(far))
        def _():
            pair = extras * 3 + live + quotient(slot - CAP, 2)

            def store(lanes):
                for turn in range(heads):
                    where = row_tile(position * heads + (seq ^ turn), rows)
                    ads[where, lanes] = own_ins[turn][pair, :, lanes]

            each_half(slot, store)

    each_block(plan, me, blocks, live, take)
    up_part = jnp.dot(dquery[...], ads[...], preferred_element_type=jnp.float32)
    up_out[...] = (up_part + swap_halves(up_part)).T[: up_out.shape[0]].astype(jnp.bfloat16)
    for index in range(tiles):
        sums[0, index] = mine[index].astype(jnp.float32) + other[tiles + index].astype(jnp.float32)
        sums[1, index] = other[index].astype(jnp.float32) + mine[tiles + index].astype(jnp.float32)
    grads[...] = jnp.zeros_like(grads)

    def put(dest, slot, local):
        index = jnp.where(slot < CAP, dest, groups - 1 + quotient(slot, 2))
        for owner in range(CORES):
            grads[owner, local] = split(slot, sums[owner, index])

    each_hit(plan, me, groups, blocks, live, put)
    low = low_lanes(HALF // 2)
    columns = grads[...].reshape(CORES * blocks * rows, LANES).T[:HALF].astype(jnp.bfloat16)
    even = core == 0
    for chip in range(heads // CORES):
        features = jnp.concatenate([feat[:, core_columns(chip, core)], feat_other[chip]], axis=0)
        product = jnp.dot(columns, features, preferred_element_type=jnp.float32)
        first, second, third = (
            product[:, index * LANES : (index + 1) * LANES] for index in range(3)
        )
        shared = jnp.where(even, third, first)
        upper, lower = shared[: HALF // 2], shared[HALF // 2 :]
        out[chip, :HALF] = jnp.where(even, first, second).astype(jnp.bfloat16)
        out[chip, HALF : 2 * HALF] = jnp.where(even, second, third).astype(jnp.bfloat16)
        out[chip, 2 * HALF :] = jnp.where(
            even,
            jnp.where(low, upper, swap_halves(lower)),
            jnp.where(low, swap_halves(upper), lower),
        ).astype(jnp.bfloat16)


def join_kernel(parts, up_part, out):
    total = parts[0].astype(jnp.float32)
    for head in range(1, parts.shape[0]):
        total = total + parts[head].astype(jnp.float32)
    out[: total.shape[0]] = total.astype(jnp.bfloat16)
    out[total.shape[0] :] = up_part[...]


def total_kernel(grad_norm, *rest):
    groups = len(rest) - 3
    down_out, up_out, held = rest[groups:]
    me = lax.axis_index("dp")
    seq = seq_index()
    for turn in range(groups):
        held[me ^ turn] = rest[turn][...].astype(jnp.float32)
    total = held[0]
    for group in range(1, groups):
        total = total + held[group]
    total = total * grad_norm
    first, second = total[:HALF], total[HALF : 2 * HALF]
    shared = total[2 * HALF : 2 * HALF + HALF // 2]
    up_out[...] = total[2 * HALF + HALF // 2 :]
    swapped = swap_halves(shared)
    low_half = jnp.concatenate([shared, swapped], axis=0)
    high_half = jnp.concatenate([swapped, shared], axis=0)
    even = jnp.concatenate([first, second, low_half], axis=1)
    odd = pltpu.roll(jnp.concatenate([first, second, high_half], axis=1), HALF, 1)
    down = jnp.where(remainder(seq, 2) == 0, even, odd)
    down_out[...] = down[:, : down_out.shape[1]]


def call(kernel, outs, specs, scratch, flops, moved, *args, vmem_mib=32, out_specs=None):
    shapes = [jax.ShapeDtypeStruct(shape, dtype) for shape, dtype in outs]
    return pl.pallas_call(
        kernel,
        out_shape=shapes,
        in_specs=specs,
        out_specs=out_specs or [VMEM] * len(shapes),
        scratch_shapes=scratch,
        compiler_params=pltpu.CompilerParams(vmem_limit_bytes=vmem_mib << 20),
        cost_estimate=pl.CostEstimate(flops=flops, bytes_accessed=moved, transcendentals=0),
    )(*args)


def exchange(value, axis, size, turn):
    return lax.ppermute(value, axis, [(peer, peer ^ turn) for peer in range(size)])


def per_device_tiles(
    features,
    frozen_query_weight,
    source_keys,
    source_values,
    output_gradient,
    adapter_down_weight,
    adapter_up_weight,
    source_block_plan,
    segments,
):
    groups = lax.axis_size("dp")
    chips = lax.axis_size("chip")
    heads = chips * CORES
    _, blocks, rows, width = features.shape
    length = segments.shape[1]
    live = (length // 2 + length // 8) // LANES
    reach = live * LANES
    rank = adapter_up_weight.shape[0]
    extras = live - CAP
    pairs = (extras + 1) // 2
    dims = (groups, blocks, heads, rows, live)
    bf16 = jnp.bfloat16
    f32 = jnp.float32
    peers = groups * heads
    everyone = SEQ + ("dp",)
    flat = features[0].reshape(blocks * rows, width)
    far_shape = (peers, CAP * 3, rows, LANES)
    own_shape = (extras * 3 + live + pairs, rows, LANES)
    rows_shape = (blocks, rows, heads * LANES)

    far_send, queries, adapter = call(
        functools.partial(pack_far_kernel, dims),
        [(far_shape, bf16), (rows_shape, bf16), ((blocks, rows, LANES), bf16)],
        [ANY] * 7,
        [
            pltpu.SMEM((groups, blocks), jnp.int32),
            pltpu.SMEM((4, blocks), jnp.int32),
            pltpu.VMEM((blocks * rows, width), bf16),
            pltpu.VMEM(rows_shape, bf16),
            pltpu.VMEM(rows_shape, bf16),
            pltpu.VMEM(rows_shape, bf16),
            pltpu.VMEM((rank, width), bf16),
            pltpu.VMEM((rank, heads * LANES), bf16),
            pltpu.VMEM(far_shape, bf16),
            pltpu.VMEM(rows_shape, bf16),
            pltpu.VMEM((blocks, rows, LANES), bf16),
            pltpu.SemaphoreType.DMA((7,)),
            pltpu.SemaphoreType.DMA((4,)),
        ],
        60_000_000,
        4_000_000,
        source_block_plan,
        flat,
        frozen_query_weight[0],
        source_keys[0],
        source_values[0],
        adapter_down_weight.T,
        adapter_up_weight,
        vmem_mib=60,
        out_specs=[ANY] * 3,
    )
    own_send = call(
        functools.partial(pack_own_kernel, dims),
        [(own_shape, bf16)] * heads
        + [((chips, blocks * rows, 3 * LANES), bf16), ((groups, rows, LANES), bf16)],
        [SMEM] + [VMEM] * 6,
        [],
        0,
        1_600_000,
        source_block_plan,
        source_keys[0],
        source_values[0],
        output_gradient[0],
        queries,
        adapter,
        flat,
    )
    feat_other = exchange(own_send[heads], "core", CORES, 1)
    own = [exchange(own_send[turn], SEQ, heads, turn) for turn in range(heads - 1, 0, -1)]
    own = [own_send[0]] + own[::-1]
    far = lax.all_to_all(far_send, everyone, 0, 0, tiled=True)
    attended = call(
        functools.partial(attend_kernel, dims),
        [((chips * groups, CORES + 1, rows, LANES), bf16)]
        + [((CORES, pairs, rows, LANES), bf16)] * chips
        + [((LANES, reach), bf16), ((1, 1, length), f32)],
        [SMEM] + [VMEM] * (4 + heads) + [ANY],
        [
            pltpu.VMEM((chips * groups, CORES + 1, rows, LANES), bf16),
            pltpu.VMEM((1, 1, length), f32),
            pltpu.SMEM((2, live), jnp.int32),
            pltpu.SemaphoreType.DMA((2,)),
        ]
        + [pltpu.VMEM((reach, LANES), bf16)] * 5,
        600_000_000,
        3_000_000,
        source_block_plan,
        segments,
        adapter_up_weight,
        own_send[heads + 1],
        far,
        *own,
        feat_other,
        out_specs=[ANY] + [VMEM] * (chips + 1) + [ANY],
    )
    own_parts = [
        exchange(attended[1 + turn], "chip", chips, turn) for turn in range(chips - 1, 0, -1)
    ]
    part = lax.all_to_all(attended[0], ("chip", "dp"), 0, 0, tiled=True)
    dquery, log_norm = attended[1 + chips :]
    tiles = groups + pairs
    (mine,) = call(
        head_sum_kernel,
        [((CORES * tiles + chips * groups, rows, LANES), bf16)],
        [VMEM] * (1 + chips),
        [],
        0,
        300_000,
        part,
        *own_parts,
        attended[1],
    )
    shares, up_part = call(
        functools.partial(product_kernel, dims),
        [((chips, HALF * 5 // 2, LANES), bf16), ((rank, LANES), bf16)],
        [SMEM] + [VMEM] * (5 + heads),
        [
            pltpu.VMEM((CORES, tiles, rows, LANES), f32),
            pltpu.VMEM((CORES, blocks, rows, LANES), f32),
            pltpu.VMEM((reach, LANES), bf16),
        ],
        60_000_000,
        2_000_000,
        source_block_plan,
        flat,
        feat_other,
        mine,
        exchange(mine, "core", CORES, 1),
        dquery,
        *own,
    )
    shares = lax.all_to_all(shares, "chip", 0, 0, tiled=True)
    (joined,) = call(
        join_kernel,
        [((HALF * 5 // 2 + rank, LANES), bf16)],
        [VMEM] * 2,
        [],
        0,
        600_000,
        shares,
        up_part,
    )
    sums = [joined] + [exchange(joined, "dp", groups, turn) for turn in range(1, groups)]
    down, up = call(
        functools.partial(total_kernel, 4.0 / math.sqrt(groups * length)),
        [((rank, width // heads), f32), ((rank, LANES), f32)],
        [VMEM] * groups,
        [pltpu.VMEM((groups,) + joined.shape, f32)],
        0,
        400_000,
        *sums,
    )
    return (down.T, up, log_norm)


def power_of_two(size):
    return size > 1 and size & (size - 1) == 0


def fits_tiles(mesh, features, adapter_up_weight):
    groups, heads = mesh.shape["dp"], mesh.shape["seq"]
    rows = features.shape[2] // heads
    return (
        rows % 16 == 0
        and features.shape[2] == LANES
        and features.shape[3] * 2 == heads * 5 * LANES
        and power_of_two(heads)
        and power_of_two(groups)
        and power_of_two(features.shape[1])
        and adapter_up_weight.shape == (HALF, heads * LANES)
    )


def split_mesh(mesh):
    groups, heads = mesh.shape["dp"], mesh.shape["seq"]
    devices = np.asarray(mesh.devices).reshape(groups, heads // CORES, CORES)
    return Mesh(devices, ("dp",) + SEQ)


def tiles_solution(mesh):
    row_spec = P("dp", None, SEQ, None)
    return jax.shard_map(
        per_device_tiles,
        mesh=split_mesh(mesh),
        in_specs=(row_spec,) * 5 + (P(), P(), P(), P("dp", None)),
        out_specs=(P(SEQ, None), P(None, SEQ), P("dp", SEQ, None)),
        check_vma=False,
    )


def attend_head(query, key_rows, value_rows, cotangent, segment, clip_count, reach_rows):
    length = query.shape[0]
    width = query.shape[1]
    piece_count = 8
    piece_rows = reach_rows // piece_count
    scaling = 1.0 / math.sqrt(width)
    query_padded = jnp.pad(query, ((0, reach_rows), (0, 0)))
    grad_padded = jnp.pad(cotangent, ((0, reach_rows), (0, 0)))
    keys_padded = jnp.pad(key_rows, ((0, reach_rows), (0, 0)))
    values_padded = jnp.pad(value_rows, ((0, reach_rows), (0, 0)))
    segment_padded = jnp.pad(segment, (0, reach_rows), constant_values=-1)
    clip_ids = jnp.arange(clip_count, dtype=jnp.int32)
    starts = jnp.sum((segment[None, :] < clip_ids[:, None]).astype(jnp.int32), axis=1)

    def piece_pass(piece_index):
        clip_slice = piece_index // piece_count
        start = lax.dynamic_index_in_dim(starts, clip_slice, 0, keepdims=False)
        query_start = start + piece_index % piece_count * piece_rows
        query_tile = lax.dynamic_slice_in_dim(query_padded, query_start, piece_rows, 0)
        grad_tile = lax.dynamic_slice_in_dim(grad_padded, query_start, piece_rows, 0)
        seg_tile = lax.dynamic_slice_in_dim(segment_padded, query_start, piece_rows, 0)
        key_tile = lax.dynamic_slice_in_dim(keys_padded, start, reach_rows, 0)
        value_tile = lax.dynamic_slice_in_dim(values_padded, start, reach_rows, 0)
        seg_cols = lax.dynamic_slice_in_dim(segment_padded, start, reach_rows, 0)
        in_clip = seg_tile == clip_slice
        allowed = in_clip[:, None] & (seg_cols == clip_slice)[None, :]
        scores = (
            lax.dot_general(
                query_tile, key_tile, (((1,), (1,)), ((), ())), preferred_element_type=jnp.float32
            )
            * scaling
        )
        scores = jnp.where(allowed, scores, -1e30)
        maximum = jnp.max(scores, axis=1, keepdims=True)
        exponent = jnp.where(allowed, jnp.exp(scores - maximum), 0.0)
        totals = jnp.where(in_clip[:, None], jnp.sum(exponent, axis=1, keepdims=True), 1.0)
        log_norm = jnp.where(in_clip, maximum[:, 0] + jnp.log(totals[:, 0]), 0.0)
        probs = exponent / totals
        weights = probs.astype(jnp.bfloat16)
        attended = jnp.dot(weights, value_tile, preferred_element_type=jnp.float32)
        delta = jnp.sum(grad_tile.astype(jnp.float32) * attended, axis=1, keepdims=True)
        dprob = lax.dot_general(
            grad_tile, value_tile, (((1,), (1,)), ((), ())), preferred_element_type=jnp.float32
        )
        dscore = (probs * (dprob - delta)).astype(jnp.bfloat16)
        query_gradient = (
            jnp.dot(dscore, key_tile, preferred_element_type=jnp.float32) * scaling
        ).astype(jnp.bfloat16)
        query_gradient = jnp.where(in_clip[:, None], query_gradient, jnp.zeros((), jnp.bfloat16))
        return (query_gradient, log_norm, query_start)

    total_pieces = piece_count * (clip_count - 1)
    dquery_pieces, log_pieces, piece_starts = lax.map(
        piece_pass, jnp.arange(total_pieces, dtype=jnp.int32)
    )

    def place(index, carry):
        grad_total, log_total = carry
        where_at = lax.dynamic_index_in_dim(piece_starts, index, 0, keepdims=False)
        grad_piece = lax.dynamic_index_in_dim(dquery_pieces, index, 0, keepdims=False)
        log_piece = lax.dynamic_index_in_dim(log_pieces, index, 0, keepdims=False)
        grad_old = lax.dynamic_slice_in_dim(grad_total, where_at, piece_rows, 0)
        log_old = lax.dynamic_slice_in_dim(log_total, where_at, piece_rows, 0)
        grad_total = lax.dynamic_update_slice_in_dim(grad_total, grad_old + grad_piece, where_at, 0)
        log_total = lax.dynamic_update_slice_in_dim(log_total, log_old + log_piece, where_at, 0)
        return (grad_total, log_total)

    grad_init = jnp.zeros((length + reach_rows, width), jnp.bfloat16)
    log_init = jnp.zeros((length + reach_rows,), jnp.float32)
    grad_total, log_total = lax.fori_loop(0, total_pieces, place, (grad_init, log_init))
    return (grad_total[:length], log_total[:length])


def routing_tables(source_block_plan, group_index, cap_slots):
    group_count, block_count = source_block_plan.shape
    source_group = source_block_plan // block_count
    source_local = source_block_plan % block_count
    dest_groups = jnp.arange(group_count, dtype=jnp.int32)[:, None]
    outgoing = (source_group == group_index) & (dest_groups != group_index)
    out_rank = jnp.cumsum(outgoing.astype(jnp.int32), axis=1) - 1
    slot_ids = jnp.arange(cap_slots, dtype=jnp.int32)
    chosen = outgoing[:, :, None] & (out_rank[:, :, None] == slot_ids[None, None, :])
    send_index = jnp.sum(jnp.where(chosen, source_local[:, :, None], 0), axis=1)
    send_valid = jnp.any(chosen, axis=1)
    own_group = lax.dynamic_index_in_dim(source_group, group_index, 0, keepdims=False)
    own_local = lax.dynamic_index_in_dim(source_local, group_index, 0, keepdims=False)
    incoming = own_group != group_index
    positions = jnp.arange(block_count, dtype=jnp.int32)
    earlier = (own_group[None, :] == own_group[:, None]) & (positions[None, :] < positions[:, None])
    in_rank = jnp.sum(earlier.astype(jnp.int32), axis=1)
    return (send_index, send_valid, incoming, own_group, in_rank, own_local)


def pack_blocks(local, send_index, send_valid):
    picked = jnp.take(local, send_index, axis=0)
    return jnp.where(send_valid[:, :, None, None], picked, jnp.zeros((), local.dtype))


def unpack_blocks(received, local, tables, cap_slots):
    incoming, own_group, in_rank, own_local = tables
    flat = received.reshape((-1,) + received.shape[2:])
    slot_index = jnp.where(incoming, own_group * cap_slots + in_rank, 0)
    remote = jnp.take(flat, slot_index, axis=0)
    staying = jnp.take(local, own_local, axis=0)
    return jnp.where(incoming[:, None, None], remote, staying)


def per_device(
    features,
    frozen_query_weight,
    source_keys,
    source_values,
    output_gradient,
    adapter_down_weight,
    adapter_up_weight,
    source_block_plan,
    segments,
):
    group_count = lax.axis_size("dp")
    group_index = lax.axis_index("dp")
    block_count = features.shape[1]
    feat_local = features[0]
    base_local = frozen_query_weight[0]
    keys_local = source_keys[0]
    values_local = source_values[0]
    send_index, send_valid, incoming, own_group, in_rank, own_local = routing_tables(
        source_block_plan, group_index, CAP
    )
    tables = (incoming, own_group, in_rank, own_local)
    contract_final_axis = (((2,), (0,)), ((), ()))
    shuffled = (
        lax.all_to_all(
            pack_blocks(feat_local, send_index, send_valid),
            "dp",
            split_axis=0,
            concat_axis=0,
            tiled=True,
        ),
        lax.all_to_all(
            pack_blocks(base_local, send_index, send_valid),
            "dp",
            split_axis=0,
            concat_axis=0,
            tiled=True,
        ),
        lax.all_to_all(
            pack_blocks(keys_local, send_index, send_valid),
            "dp",
            split_axis=0,
            concat_axis=0,
            tiled=True,
        ),
        lax.all_to_all(
            pack_blocks(values_local, send_index, send_valid),
            "dp",
            split_axis=0,
            concat_axis=0,
            tiled=True,
        ),
    )
    feature_dest = unpack_blocks(shuffled[0], feat_local, tables, CAP)
    base_query_dest = unpack_blocks(shuffled[1], base_local, tables, CAP)
    keys_dest = unpack_blocks(shuffled[2], keys_local, tables, CAP)
    values_dest = unpack_blocks(shuffled[3], values_local, tables, CAP)
    adapter_params = lax.dot_general(
        feature_dest, adapter_down_weight, contract_final_axis, preferred_element_type=jnp.float32
    ).astype(jnp.bfloat16)
    query_rows = (
        base_query_dest.astype(jnp.float32)
        + lax.dot_general(
            adapter_params,
            adapter_up_weight,
            contract_final_axis,
            preferred_element_type=jnp.float32,
        )
    ).astype(jnp.bfloat16)
    head_query, head_keys, head_values, head_grads = (
        lax.all_to_all(query_rows, "seq", split_axis=2, concat_axis=1, tiled=True),
        lax.all_to_all(keys_dest, "seq", split_axis=2, concat_axis=1, tiled=True),
        lax.all_to_all(values_dest, "seq", split_axis=2, concat_axis=1, tiled=True),
        lax.all_to_all(output_gradient[0], "seq", split_axis=2, concat_axis=1, tiled=True),
    )
    length = head_query.shape[0] * head_query.shape[1]
    reach_rows = length // 2 + length // 8
    head_width = head_query.shape[2]
    segment = segments[0]
    head_query = head_query.reshape(length, head_width)
    head_keys = head_keys.reshape(length, head_width)
    head_values = head_values.reshape(length, head_width)
    head_grads = head_grads.reshape(length, head_width)
    dquery_head, log_head = attend_head(
        head_query, head_keys, head_values, head_grads, segment, CLIPS, reach_rows
    )
    norm_pieces = [log_head]
    log_norm = jnp.stack(norm_pieces, axis=0)
    query_gradient = lax.all_to_all(
        dquery_head.reshape(block_count, length // block_count, head_width),
        "seq",
        split_axis=1,
        concat_axis=2,
        tiled=True,
    )
    adapter_gradient = lax.dot_general(
        query_gradient,
        adapter_up_weight,
        (((2,), (1,)), ((), ())),
        preferred_element_type=jnp.float32,
    ).astype(jnp.bfloat16)
    contract_tokens = (((0, 1), (0, 1)), ((), ()))
    down_part = lax.dot_general(
        feature_dest, adapter_gradient, contract_tokens, preferred_element_type=jnp.float32
    )
    up_part = lax.dot_general(
        adapter_params, query_gradient, contract_tokens, preferred_element_type=jnp.float32
    )
    down_share, up_share = (
        lax.psum_scatter(down_part, "seq", scatter_dimension=0, tiled=True),
        lax.psum_scatter(up_part, "seq", scatter_dimension=1, tiled=True),
    )
    down_total, up_total = lax.psum((down_share, up_share), "dp")
    grad_norm = 4.0 / math.sqrt(group_count * length)
    return (down_total * grad_norm, up_total * grad_norm, log_norm[None])


def solution(mesh):
    in_specs = (
        P("dp", None, "seq", None),
        P("dp", None, "seq", None),
        P("dp", None, "seq", None),
        P("dp", None, "seq", None),
        P("dp", None, "seq", None),
        P(),
        P(),
        P(),
        P("dp", None),
    )
    out_specs = (P("seq", None), P(None, "seq"), P("dp", "seq", None))

    plain = jax.shard_map(
        per_device, mesh=mesh, in_specs=in_specs, out_specs=out_specs, check_vma=False
    )

    def whole(features, *rest):
        fits = fits_tiles(mesh, features, rest[5])
        return (tiles_solution(mesh) if fits else plain)(features, *rest)

    return whole
```

```python
import functools
import math

import jax
import jax.numpy as jnp
import numpy as np
from jax import lax
from jax.experimental import pallas as pl
from jax.experimental.pallas import tpu as pltpu
from jax.sharding import Mesh
from jax.sharding import PartitionSpec as P

CAP = 2
CLIPS = 2
LANES = 128
HALF = 64
CORES = 2
SEQ = ("chip", "core")
QUERIES = 640
LOG2E = math.log2(math.e)
VMEM = pl.BlockSpec(memory_space=pltpu.VMEM)
SMEM = pl.BlockSpec(memory_space=pltpu.SMEM)
ANY = pl.BlockSpec(memory_space=pl.ANY)
NT = (((1,), (1,)), ((), ()))


def low_lanes(rows):
    return lax.broadcasted_iota(jnp.int32, (rows, LANES), 1) < HALF


def swap_halves(tile):
    return pltpu.roll(tile, HALF, 1)


def lane_tile(index):
    return pl.ds(pl.multiple_of(index * LANES, LANES), LANES)


def row_tile(index, rows):
    return pl.ds(pl.multiple_of(index * rows, rows), rows)


def quotient(value, size):
    return lax.shift_right_logical(value, size.bit_length() - 1)


def remainder(value, size):
    return value & (size - 1)


def seq_index():
    return lax.axis_index("chip") * CORES + lax.axis_index("core")


def each_hit(plan, me, groups, blocks, live, put):
    def over_dest(dest, _):
        def over_position(position, slot):
            source = plan[dest, position]
            hit = quotient(source, blocks) == me

            @pl.when(hit)
            def _():
                put(dest, slot, remainder(source, blocks))

            return slot + hit.astype(jnp.int32)

        lax.fori_loop(0, live, over_position, jnp.int32(0))
        return 0

    lax.fori_loop(0, groups, over_dest, 0)


def each_block(plan, me, blocks, live, take):
    def over_position(position, _):
        group = quotient(plan[me, position], blocks)
        slot = jnp.int32(0)
        for other in range(live):
            same = (quotient(plan[me, other], blocks) == group) & (other < position)
            slot = slot + same.astype(jnp.int32)
        take(position, group, slot)
        return 0

    lax.fori_loop(0, live, over_position, 0)


def each_half(slot, store):
    @pl.when(remainder(slot, 2) == 0)
    def _():
        store(slice(0, HALF))

    @pl.when(remainder(slot, 2) == 1)
    def _():
        store(slice(HALF, LANES))


def split(slot, pair):
    pair = pair.astype(jnp.float32)
    return jnp.where(remainder(slot, 2) == 0, pair, swap_halves(pair))


def pack_far_kernel(dims, plan_hbm, feat_hbm, base_hbm, keys_hbm, vals_hbm, down_hbm, up_hbm, *rest):
    groups, blocks, heads, rows, live = dims
    far_hbm, queries_hbm, adapter_hbm = rest[:3]
    plan, routes, feat, base, keys, vals, down, up, far_out, qbuf, abuf, sems, out_sems = rest[3:]
    me = lax.axis_index("dp")
    copies = [
        pltpu.make_async_copy(source, target, sems.at[index])
        for index, (source, target) in enumerate(
            (
                (plan_hbm, plan),
                (keys_hbm, keys),
                (vals_hbm, vals),
                (feat_hbm, feat),
                (down_hbm, down),
                (base_hbm, base),
                (up_hbm, up),
            )
        )
    ]
    for copy in copies:
        copy.start()

    def put_early(dest, slot, local):
        @pl.when(slot < CAP)
        def _():
            index = routes[0, 0]
            routes[0, 0] = index + 1
            for row, value in enumerate((dest, slot, local)):
                routes[row + 1, index] = value
            for head in range(heads):
                columns = slice(head * LANES, (head + 1) * LANES)
                far_out[head * groups + dest, slot] = keys[local, :, columns]
                far_out[head * groups + dest, CAP + slot] = vals[local, :, columns]

    def send(first, count, index):
        tiles = pl.ds(first, count)
        copy = pltpu.make_async_copy(far_out.at[:, tiles], far_hbm.at[:, tiles], out_sems.at[index])
        copy.start()
        return copy

    for copy in copies[:3]:
        copy.wait()
    routes[0, 0] = 0
    each_hit(plan, me, groups, blocks, live, put_early)
    early = send(0, 2 * CAP, 0)
    for copy in copies[3:]:
        copy.wait()
    narrow = lax.dot_general(feat[...], down[...], NT, preferred_element_type=jnp.float32)
    adapter = narrow.astype(jnp.bfloat16)
    lift = jnp.dot(adapter, up[...], preferred_element_type=jnp.float32)
    abuf[...] = jnp.concatenate([narrow, narrow], axis=1).astype(jnp.bfloat16).reshape(abuf.shape)
    qbuf[...] = (base[...].astype(jnp.float32) + lift.reshape(base.shape)).astype(jnp.bfloat16)

    def put_late(index, _):
        dest, slot, local = routes[1, index], routes[2, index], routes[3, index]

        for head in range(heads):
            columns = slice(head * LANES, (head + 1) * LANES)
            far_out[head * groups + dest, 2 * CAP + slot] = qbuf[local, :, columns]
        return 0

    lax.fori_loop(0, routes[0, 0], put_late, 0)
    late = send(2 * CAP, CAP, 1)
    rest_out = [
        pltpu.make_async_copy(qbuf, queries_hbm, out_sems.at[2]),
        pltpu.make_async_copy(abuf, adapter_hbm, out_sems.at[3]),
    ]
    for copy in rest_out:
        copy.start()
    for copy in [early, late] + rest_out:
        copy.wait()


def core_columns(chip, core):
    return pl.ds(pl.multiple_of((chip * 5 + core * 2) * LANES, LANES), 3 * LANES)


def pack_own_kernel(dims, plan, keys, vals, grad, queries, adapter, feat, *outs):
    groups, blocks, heads, rows, live = dims
    own_outs, feat_out, adapter_out = outs[:heads], outs[heads], outs[heads + 1]
    for chip in range(heads // CORES):
        feat_out[chip] = feat[:, core_columns(chip, 1 - lax.axis_index("core"))]
    extras = live - CAP
    me = lax.axis_index("dp")
    seq = seq_index()
    sources = (keys, vals, queries)

    def put(dest, slot, local):
        @pl.when(slot < CAP)
        def _():
            def store(lanes):
                adapter_out[dest, :, lanes] = adapter[local, :, lanes]

            each_half(slot, store)

        @pl.when(slot >= CAP)
        def _():
            extra = slot - CAP
            where = extras * 3 + live + quotient(extra, 2)
            for turn in range(heads):
                columns = lane_tile(seq ^ turn)
                for index, source in enumerate(sources):
                    own_outs[turn][index * extras + extra] = source[local, :, columns]

            def store(lanes):
                for turn in range(heads):
                    own_outs[turn][where, :, lanes] = adapter[local, :, lanes]

            each_half(slot, store)

    each_hit(plan, me, groups, blocks, live, put)
    for turn in range(heads):
        columns = lane_tile(seq ^ turn)
        for position in range(live):
            own_outs[turn][extras * 3 + position] = grad[position, :, columns]


def attend_kernel(dims, plan, seg, up, adapter, far_in, *rest):
    groups, blocks, heads, rows, live = dims
    chips = heads // CORES
    core = lax.axis_index("core")
    own_ins = rest[:heads][::-1]
    part_hbm = rest[heads + 1]
    own_parts = rest[heads + 2 : heads + 2 + chips]
    dqs, log_hbm, part_out, log_out, routes, sems, qs, ks, vs, gs, parts = rest[
        heads + 2 + chips :
    ]
    extras = live - CAP
    me = lax.axis_index("dp")
    seq = seq_index()
    length = seg.shape[1]
    reach = live * LANES
    scaling = 1.0 / math.sqrt(LANES)

    def take(position, group, slot):
        routes[0, position] = group
        routes[1, position] = slot
        far = (group != me) | (slot < CAP)

        @pl.when(far)
        def _():
            for part in range(heads):
                index = part * groups + group
                where = row_tile(position * heads + part, rows)
                ks[where, :] = far_in[index, slot]
                vs[where, :] = far_in[index, CAP + slot]
                qs[where, :] = far_in[index, 2 * CAP + slot]

        @pl.when(jnp.logical_not(far))
        def _():
            extra = slot - CAP
            for turn in range(heads):
                where = row_tile(position * heads + (seq ^ turn), rows)
                ks[where, :] = own_ins[turn][extra]
                vs[where, :] = own_ins[turn][extras + extra]
                qs[where, :] = own_ins[turn][2 * extras + extra]

    each_block(plan, me, blocks, live, take)
    for turn in range(heads):
        for position in range(live):
            gs[row_tile(position * heads + (seq ^ turn), rows), :] = own_ins[turn][
                extras * 3 + position
            ]

    count = jnp.sum((seg[...] < CLIPS - 1).astype(jnp.float32), axis=1, keepdims=True).astype(
        jnp.int32
    )
    key_rows = ks[...]
    value_rows = vs[...]
    key_columns = key_rows.T
    key_index = lax.broadcasted_iota(jnp.int32, (reach, 1), 0)
    always = length - reach
    up_head = up[:, lane_tile(seq)]
    up_twice = jnp.concatenate([up_head, up_head], axis=0)
    for start in range(0, reach, QUERIES):
        count_here = min(QUERIES, reach - start)
        span = slice(start, start + count_here)
        scores = lax.dot_general(key_rows, qs[span, :], NT, preferred_element_type=jnp.float32)
        scores = jnp.concatenate(
            [
                scores[:always],
                jnp.where(key_index[always:] < count, scores[always:], -1e30),
            ],
            axis=0,
        )
        dprob = lax.dot_general(value_rows, gs[span, :], NT, preferred_element_type=jnp.float32)
        maximum = jnp.max(scores, axis=0, keepdims=True)
        exponent = jnp.exp2((scores - maximum) * (scaling * LOG2E))
        total = jnp.sum(exponent, axis=0, keepdims=True)
        delta = jnp.sum(exponent * dprob, axis=0, keepdims=True) / total
        dscore = (exponent * (dprob - delta)).astype(jnp.bfloat16)
        dquery = jnp.dot(key_columns, dscore, preferred_element_type=jnp.float32)
        query_index = lax.broadcasted_iota(jnp.int32, (1, count_here), 1) + start
        in_clip = query_index < count
        dquery = jnp.where(in_clip, dquery * (scaling / total), 0.0).astype(jnp.bfloat16)
        dqs[:, span] = dquery
        log_out[0, :, span] = jnp.where(in_clip, maximum * scaling + jnp.log(total), 0.0)
    log_out[0, :, reach:] = jnp.zeros((1, length - reach), jnp.float32)
    log_copy = pltpu.make_async_copy(log_out, log_hbm, sems.at[0])
    log_copy.start()
    dquery_all = dqs[...]
    parts[...] = lax.dot_general(
        dquery_all, up_twice, (((0,), (1,)), ((), ())), preferred_element_type=jnp.float32
    ).astype(jnp.bfloat16)

    def put(position, _):
        group, slot = routes[0, position], routes[1, position]
        far = (group != me) | (slot < CAP)

        @pl.when(far)
        def _():
            def store(lanes):
                for turn in range(heads):
                    chip, side = turn // CORES, turn % CORES
                    where = row_tile(position * heads + chip * CORES + (core ^ side), rows)
                    part_out[chip * groups + group, side, :, lanes] = parts[where, lanes]

            each_half(slot, store)

        @pl.when(jnp.logical_not(far))
        def _():
            pair = quotient(slot - CAP, 2)

            def store(lanes):
                for turn in range(heads):
                    where = row_tile(position * heads + (seq ^ turn), rows)
                    own_parts[turn // CORES][turn % CORES, pair, :, lanes] = parts[where, lanes]

            each_half(slot, store)

        return 0

    lax.fori_loop(0, live, put, 0)
    for chip in range(chips):
        for group in range(groups):
            part_out[chip * groups + group, CORES] = adapter[group]
    part_copy = pltpu.make_async_copy(part_out, part_hbm, sems.at[1])
    part_copy.start()
    log_copy.wait()
    part_copy.wait()


def head_sum_kernel(parts, *refs):
    extras, out = refs[:-1], refs[-1]
    pairs = extras[0].shape[1]
    peers = parts.shape[0]
    tiles = (out.shape[0] - peers) // CORES
    groups = tiles - pairs

    def total(terms):
        value = terms[0].astype(jnp.float32)
        for term in terms[1:]:
            value = value + term.astype(jnp.float32)
        return value.astype(jnp.bfloat16)

    for side in range(CORES):
        for group in range(groups):
            out[side * tiles + group] = total(
                [parts[peer, side] for peer in range(group, peers, groups)]
            )
        for pair in range(pairs):
            out[side * tiles + groups + pair] = total([extra[side, pair] for extra in extras])
    for peer in range(peers):
        out[CORES * tiles + peer] = parts[peer, CORES]


def product_kernel(dims, plan, feat, feat_other, mine, other, dquery, *rest):
    groups, blocks, heads, rows, live = dims
    own_ins = rest[:heads]
    out, up_out, sums, grads, ads = rest[heads:]
    extras = live - CAP
    me = lax.axis_index("dp")
    core = lax.axis_index("core")
    seq = seq_index()
    tiles = sums.shape[1]
    ads[...] = jnp.zeros_like(ads)

    def take(position, group, slot):
        far = (group != me) | (slot < CAP)

        @pl.when(far)
        def _():
            def store(lanes):
                for chip in range(heads // CORES):
                    tile = CORES * tiles + chip * groups + group
                    for source, which in ((mine, core), (other, 1 - core)):
                        where = row_tile(position * heads + chip * CORES + which, rows)
                        ads[where, lanes] = source[tile, :, lanes]

            each_half(slot, store)

        @pl.when(jnp.logical_not(far))
        def _():
            pair = extras * 3 + live + quotient(slot - CAP, 2)

            def store(lanes):
                for turn in range(heads):
                    where = row_tile(position * heads + (seq ^ turn), rows)
                    ads[where, lanes] = own_ins[turn][pair, :, lanes]

            each_half(slot, store)

    each_block(plan, me, blocks, live, take)
    up_part = jnp.dot(dquery[...], ads[...], preferred_element_type=jnp.float32)
    up_out[...] = (up_part + swap_halves(up_part)).T[: up_out.shape[0]].astype(jnp.bfloat16)
    for index in range(tiles):
        sums[0, index] = mine[index].astype(jnp.float32) + other[tiles + index].astype(jnp.float32)
        sums[1, index] = other[index].astype(jnp.float32) + mine[tiles + index].astype(jnp.float32)
    grads[...] = jnp.zeros_like(grads)

    def put(dest, slot, local):
        index = jnp.where(slot < CAP, dest, groups - 1 + quotient(slot, 2))
        for owner in range(CORES):
            grads[owner, local] = split(slot, sums[owner, index])

    each_hit(plan, me, groups, blocks, live, put)
    low = low_lanes(HALF // 2)
    columns = grads[...].reshape(CORES * blocks * rows, LANES).T[:HALF].astype(jnp.bfloat16)
    even = core == 0
    for chip in range(heads // CORES):
        features = jnp.concatenate([feat[:, core_columns(chip, core)], feat_other[chip]], axis=0)
        product = jnp.dot(columns, features, preferred_element_type=jnp.float32)
        first, second, third = (
            product[:, index * LANES : (index + 1) * LANES] for index in range(3)
        )
        shared = jnp.where(even, third, first)
        upper, lower = shared[: HALF // 2], shared[HALF // 2 :]
        out[chip, :HALF] = jnp.where(even, first, second).astype(jnp.bfloat16)
        out[chip, HALF : 2 * HALF] = jnp.where(even, second, third).astype(jnp.bfloat16)
        out[chip, 2 * HALF :] = jnp.where(
            even,
            jnp.where(low, upper, swap_halves(lower)),
            jnp.where(low, swap_halves(upper), lower),
        ).astype(jnp.bfloat16)


def join_kernel(parts, up_part, out):
    total = parts[0].astype(jnp.float32)
    for head in range(1, parts.shape[0]):
        total = total + parts[head].astype(jnp.float32)
    out[: total.shape[0]] = total.astype(jnp.bfloat16)
    out[total.shape[0] :] = up_part[...]


def total_kernel(grad_norm, *rest):
    groups = len(rest) - 3
    down_out, up_out, held = rest[groups:]
    me = lax.axis_index("dp")
    seq = seq_index()
    for turn in range(groups):
        held[me ^ turn] = rest[turn][...].astype(jnp.float32)
    total = held[0]
    for group in range(1, groups):
        total = total + held[group]
    total = total * grad_norm
    first, second = total[:HALF], total[HALF : 2 * HALF]
    shared = total[2 * HALF : 2 * HALF + HALF // 2]
    up_out[...] = total[2 * HALF + HALF // 2 :]
    swapped = swap_halves(shared)
    low_half = jnp.concatenate([shared, swapped], axis=0)
    high_half = jnp.concatenate([swapped, shared], axis=0)
    even = jnp.concatenate([first, second, low_half], axis=1)
    odd = pltpu.roll(jnp.concatenate([first, second, high_half], axis=1), HALF, 1)
    down = jnp.where(remainder(seq, 2) == 0, even, odd)
    down_out[...] = down[:, : down_out.shape[1]]


def call(kernel, outs, specs, scratch, flops, moved, *args, vmem_mib=32, out_specs=None):
    shapes = [jax.ShapeDtypeStruct(shape, dtype) for shape, dtype in outs]
    return pl.pallas_call(
        kernel,
        out_shape=shapes,
        in_specs=specs,
        out_specs=out_specs or [VMEM] * len(shapes),
        scratch_shapes=scratch,
        compiler_params=pltpu.CompilerParams(vmem_limit_bytes=vmem_mib << 20),
        cost_estimate=pl.CostEstimate(flops=flops, bytes_accessed=moved, transcendentals=0),
    )(*args)


def exchange(value, axis, size, turn):
    return lax.ppermute(value, axis, [(peer, peer ^ turn) for peer in range(size)])


def per_device_tiles(
    features,
    frozen_query_weight,
    source_keys,
    source_values,
    output_gradient,
    adapter_down_weight,
    adapter_up_weight,
    source_block_plan,
    segments,
):
    groups = lax.axis_size("dp")
    chips = lax.axis_size("chip")
    heads = chips * CORES
    _, blocks, rows, width = features.shape
    length = segments.shape[1]
    live = (length // 2 + length // 8) // LANES
    reach = live * LANES
    rank = adapter_up_weight.shape[0]
    extras = live - CAP
    pairs = (extras + 1) // 2
    dims = (groups, blocks, heads, rows, live)
    bf16 = jnp.bfloat16
    f32 = jnp.float32
    peers = groups * heads
    everyone = SEQ + ("dp",)
    flat = features[0].reshape(blocks * rows, width)
    far_shape = (peers, CAP * 3, rows, LANES)
    own_shape = (extras * 3 + live + pairs, rows, LANES)
    rows_shape = (blocks, rows, heads * LANES)

    far_send, queries, adapter = call(
        functools.partial(pack_far_kernel, dims),
        [(far_shape, bf16), (rows_shape, bf16), ((blocks, rows, LANES), bf16)],
        [ANY] * 7,
        [
            pltpu.SMEM((groups, blocks), jnp.int32),
            pltpu.SMEM((4, blocks), jnp.int32),
            pltpu.VMEM((blocks * rows, width), bf16),
            pltpu.VMEM(rows_shape, bf16),
            pltpu.VMEM(rows_shape, bf16),
            pltpu.VMEM(rows_shape, bf16),
            pltpu.VMEM((rank, width), bf16),
            pltpu.VMEM((rank, heads * LANES), bf16),
            pltpu.VMEM(far_shape, bf16),
            pltpu.VMEM(rows_shape, bf16),
            pltpu.VMEM((blocks, rows, LANES), bf16),
            pltpu.SemaphoreType.DMA((7,)),
            pltpu.SemaphoreType.DMA((4,)),
        ],
        60_000_000,
        4_000_000,
        source_block_plan,
        flat,
        frozen_query_weight[0],
        source_keys[0],
        source_values[0],
        adapter_down_weight.T,
        adapter_up_weight,
        vmem_mib=60,
        out_specs=[ANY] * 3,
    )
    own_send = call(
        functools.partial(pack_own_kernel, dims),
        [(own_shape, bf16)] * heads
        + [((chips, blocks * rows, 3 * LANES), bf16), ((groups, rows, LANES), bf16)],
        [SMEM] + [VMEM] * 6,
        [],
        0,
        1_600_000,
        source_block_plan,
        source_keys[0],
        source_values[0],
        output_gradient[0],
        queries,
        adapter,
        flat,
    )
    feat_other = exchange(own_send[heads], "core", CORES, 1)
    own = [exchange(own_send[turn], SEQ, heads, turn) for turn in range(heads - 1, 0, -1)]
    own = [own_send[0]] + own[::-1]
    far = lax.all_to_all(far_send, everyone, 0, 0, tiled=True)
    attended = call(
        functools.partial(attend_kernel, dims),
        [((chips * groups, CORES + 1, rows, LANES), bf16)]
        + [((CORES, pairs, rows, LANES), bf16)] * chips
        + [((LANES, reach), bf16), ((1, 1, length), f32)],
        [SMEM] + [VMEM] * (4 + heads) + [ANY],
        [
            pltpu.VMEM((chips * groups, CORES + 1, rows, LANES), bf16),
            pltpu.VMEM((1, 1, length), f32),
            pltpu.SMEM((2, live), jnp.int32),
            pltpu.SemaphoreType.DMA((2,)),
        ]
        + [pltpu.VMEM((reach, LANES), bf16)] * 5,
        600_000_000,
        3_000_000,
        source_block_plan,
        segments,
        adapter_up_weight,
        own_send[heads + 1],
        far,
        *own[::-1],
        feat_other,
        out_specs=[ANY] + [VMEM] * (chips + 1) + [ANY],
    )
    own_parts = [
        exchange(attended[1 + turn], "chip", chips, turn) for turn in range(chips - 1, 0, -1)
    ]
    part = lax.all_to_all(attended[0], ("chip", "dp"), 0, 0, tiled=True)
    dquery, log_norm = attended[1 + chips :]
    tiles = groups + pairs
    (mine,) = call(
        head_sum_kernel,
        [((CORES * tiles + chips * groups, rows, LANES), bf16)],
        [VMEM] * (1 + chips),
        [],
        0,
        300_000,
        part,
        *own_parts,
        attended[1],
    )
    shares, up_part = call(
        functools.partial(product_kernel, dims),
        [((chips, HALF * 5 // 2, LANES), bf16), ((rank, LANES), bf16)],
        [SMEM] + [VMEM] * (5 + heads),
        [
            pltpu.VMEM((CORES, tiles, rows, LANES), f32),
            pltpu.VMEM((CORES, blocks, rows, LANES), f32),
            pltpu.VMEM((reach, LANES), bf16),
        ],
        60_000_000,
        2_000_000,
        source_block_plan,
        flat,
        feat_other,
        mine,
        exchange(mine, "core", CORES, 1),
        dquery,
        *own,
    )
    shares = lax.all_to_all(shares, "chip", 0, 0, tiled=True)
    (joined,) = call(
        join_kernel,
        [((HALF * 5 // 2 + rank, LANES), bf16)],
        [VMEM] * 2,
        [],
        0,
        600_000,
        shares,
        up_part,
    )
    sums = [joined] + [exchange(joined, "dp", groups, turn) for turn in range(1, groups)]
    down, up = call(
        functools.partial(total_kernel, 4.0 / math.sqrt(groups * length)),
        [((rank, width // heads), f32), ((rank, LANES), f32)],
        [VMEM] * groups,
        [pltpu.VMEM((groups,) + joined.shape, f32)],
        0,
        400_000,
        *sums,
    )
    return (down.T, up, log_norm)


def power_of_two(size):
    return size > 1 and size & (size - 1) == 0


def fits_tiles(mesh, features, adapter_up_weight):
    groups, heads = mesh.shape["dp"], mesh.shape["seq"]
    rows = features.shape[2] // heads
    return (
        rows % 16 == 0
        and features.shape[2] == LANES
        and features.shape[3] * 2 == heads * 5 * LANES
        and power_of_two(heads)
        and power_of_two(groups)
        and power_of_two(features.shape[1])
        and adapter_up_weight.shape == (HALF, heads * LANES)
    )


def split_mesh(mesh):
    groups, heads = mesh.shape["dp"], mesh.shape["seq"]
    devices = np.asarray(mesh.devices).reshape(groups, heads // CORES, CORES)
    return Mesh(devices, ("dp",) + SEQ)


def tiles_solution(mesh):
    row_spec = P("dp", None, SEQ, None)
    return jax.shard_map(
        per_device_tiles,
        mesh=split_mesh(mesh),
        in_specs=(row_spec,) * 5 + (P(), P(), P(), P("dp", None)),
        out_specs=(P(SEQ, None), P(None, SEQ), P("dp", SEQ, None)),
        check_vma=False,
    )


def attend_head(query, key_rows, value_rows, cotangent, segment, clip_count, reach_rows):
    length = query.shape[0]
    width = query.shape[1]
    piece_count = 8
    piece_rows = reach_rows // piece_count
    scaling = 1.0 / math.sqrt(width)
    query_padded = jnp.pad(query, ((0, reach_rows), (0, 0)))
    grad_padded = jnp.pad(cotangent, ((0, reach_rows), (0, 0)))
    keys_padded = jnp.pad(key_rows, ((0, reach_rows), (0, 0)))
    values_padded = jnp.pad(value_rows, ((0, reach_rows), (0, 0)))
    segment_padded = jnp.pad(segment, (0, reach_rows), constant_values=-1)
    clip_ids = jnp.arange(clip_count, dtype=jnp.int32)
    starts = jnp.sum((segment[None, :] < clip_ids[:, None]).astype(jnp.int32), axis=1)

    def piece_pass(piece_index):
        clip_slice = piece_index // piece_count
        start = lax.dynamic_index_in_dim(starts, clip_slice, 0, keepdims=False)
        query_start = start + piece_index % piece_count * piece_rows
        query_tile = lax.dynamic_slice_in_dim(query_padded, query_start, piece_rows, 0)
        grad_tile = lax.dynamic_slice_in_dim(grad_padded, query_start, piece_rows, 0)
        seg_tile = lax.dynamic_slice_in_dim(segment_padded, query_start, piece_rows, 0)
        key_tile = lax.dynamic_slice_in_dim(keys_padded, start, reach_rows, 0)
        value_tile = lax.dynamic_slice_in_dim(values_padded, start, reach_rows, 0)
        seg_cols = lax.dynamic_slice_in_dim(segment_padded, start, reach_rows, 0)
        in_clip = seg_tile == clip_slice
        allowed = in_clip[:, None] & (seg_cols == clip_slice)[None, :]
        scores = (
            lax.dot_general(
                query_tile, key_tile, (((1,), (1,)), ((), ())), preferred_element_type=jnp.float32
            )
            * scaling
        )
        scores = jnp.where(allowed, scores, -1e30)
        maximum = jnp.max(scores, axis=1, keepdims=True)
        exponent = jnp.where(allowed, jnp.exp(scores - maximum), 0.0)
        totals = jnp.where(in_clip[:, None], jnp.sum(exponent, axis=1, keepdims=True), 1.0)
        log_norm = jnp.where(in_clip, maximum[:, 0] + jnp.log(totals[:, 0]), 0.0)
        probs = exponent / totals
        weights = probs.astype(jnp.bfloat16)
        attended = jnp.dot(weights, value_tile, preferred_element_type=jnp.float32)
        delta = jnp.sum(grad_tile.astype(jnp.float32) * attended, axis=1, keepdims=True)
        dprob = lax.dot_general(
            grad_tile, value_tile, (((1,), (1,)), ((), ())), preferred_element_type=jnp.float32
        )
        dscore = (probs * (dprob - delta)).astype(jnp.bfloat16)
        query_gradient = (
            jnp.dot(dscore, key_tile, preferred_element_type=jnp.float32) * scaling
        ).astype(jnp.bfloat16)
        query_gradient = jnp.where(in_clip[:, None], query_gradient, jnp.zeros((), jnp.bfloat16))
        return (query_gradient, log_norm, query_start)

    total_pieces = piece_count * (clip_count - 1)
    dquery_pieces, log_pieces, piece_starts = lax.map(
        piece_pass, jnp.arange(total_pieces, dtype=jnp.int32)
    )

    def place(index, carry):
        grad_total, log_total = carry
        where_at = lax.dynamic_index_in_dim(piece_starts, index, 0, keepdims=False)
        grad_piece = lax.dynamic_index_in_dim(dquery_pieces, index, 0, keepdims=False)
        log_piece = lax.dynamic_index_in_dim(log_pieces, index, 0, keepdims=False)
        grad_old = lax.dynamic_slice_in_dim(grad_total, where_at, piece_rows, 0)
        log_old = lax.dynamic_slice_in_dim(log_total, where_at, piece_rows, 0)
        grad_total = lax.dynamic_update_slice_in_dim(grad_total, grad_old + grad_piece, where_at, 0)
        log_total = lax.dynamic_update_slice_in_dim(log_total, log_old + log_piece, where_at, 0)
        return (grad_total, log_total)

    grad_init = jnp.zeros((length + reach_rows, width), jnp.bfloat16)
    log_init = jnp.zeros((length + reach_rows,), jnp.float32)
    grad_total, log_total = lax.fori_loop(0, total_pieces, place, (grad_init, log_init))
    return (grad_total[:length], log_total[:length])


def routing_tables(source_block_plan, group_index, cap_slots):
    group_count, block_count = source_block_plan.shape
    source_group = source_block_plan // block_count
    source_local = source_block_plan % block_count
    dest_groups = jnp.arange(group_count, dtype=jnp.int32)[:, None]
    outgoing = (source_group == group_index) & (dest_groups != group_index)
    out_rank = jnp.cumsum(outgoing.astype(jnp.int32), axis=1) - 1
    slot_ids = jnp.arange(cap_slots, dtype=jnp.int32)
    chosen = outgoing[:, :, None] & (out_rank[:, :, None] == slot_ids[None, None, :])
    send_index = jnp.sum(jnp.where(chosen, source_local[:, :, None], 0), axis=1)
    send_valid = jnp.any(chosen, axis=1)
    own_group = lax.dynamic_index_in_dim(source_group, group_index, 0, keepdims=False)
    own_local = lax.dynamic_index_in_dim(source_local, group_index, 0, keepdims=False)
    incoming = own_group != group_index
    positions = jnp.arange(block_count, dtype=jnp.int32)
    earlier = (own_group[None, :] == own_group[:, None]) & (positions[None, :] < positions[:, None])
    in_rank = jnp.sum(earlier.astype(jnp.int32), axis=1)
    return (send_index, send_valid, incoming, own_group, in_rank, own_local)


def pack_blocks(local, send_index, send_valid):
    picked = jnp.take(local, send_index, axis=0)
    return jnp.where(send_valid[:, :, None, None], picked, jnp.zeros((), local.dtype))


def unpack_blocks(received, local, tables, cap_slots):
    incoming, own_group, in_rank, own_local = tables
    flat = received.reshape((-1,) + received.shape[2:])
    slot_index = jnp.where(incoming, own_group * cap_slots + in_rank, 0)
    remote = jnp.take(flat, slot_index, axis=0)
    staying = jnp.take(local, own_local, axis=0)
    return jnp.where(incoming[:, None, None], remote, staying)


def per_device(
    features,
    frozen_query_weight,
    source_keys,
    source_values,
    output_gradient,
    adapter_down_weight,
    adapter_up_weight,
    source_block_plan,
    segments,
):
    group_count = lax.axis_size("dp")
    group_index = lax.axis_index("dp")
    block_count = features.shape[1]
    feat_local = features[0]
    base_local = frozen_query_weight[0]
    keys_local = source_keys[0]
    values_local = source_values[0]
    send_index, send_valid, incoming, own_group, in_rank, own_local = routing_tables(
        source_block_plan, group_index, CAP
    )
    tables = (incoming, own_group, in_rank, own_local)
    contract_final_axis = (((2,), (0,)), ((), ()))
    shuffled = (
        lax.all_to_all(
            pack_blocks(feat_local, send_index, send_valid),
            "dp",
            split_axis=0,
            concat_axis=0,
            tiled=True,
        ),
        lax.all_to_all(
            pack_blocks(base_local, send_index, send_valid),
            "dp",
            split_axis=0,
            concat_axis=0,
            tiled=True,
        ),
        lax.all_to_all(
            pack_blocks(keys_local, send_index, send_valid),
            "dp",
            split_axis=0,
            concat_axis=0,
            tiled=True,
        ),
        lax.all_to_all(
            pack_blocks(values_local, send_index, send_valid),
            "dp",
            split_axis=0,
            concat_axis=0,
            tiled=True,
        ),
    )
    feature_dest = unpack_blocks(shuffled[0], feat_local, tables, CAP)
    base_query_dest = unpack_blocks(shuffled[1], base_local, tables, CAP)
    keys_dest = unpack_blocks(shuffled[2], keys_local, tables, CAP)
    values_dest = unpack_blocks(shuffled[3], values_local, tables, CAP)
    adapter_params = lax.dot_general(
        feature_dest, adapter_down_weight, contract_final_axis, preferred_element_type=jnp.float32
    ).astype(jnp.bfloat16)
    query_rows = (
        base_query_dest.astype(jnp.float32)
        + lax.dot_general(
            adapter_params,
            adapter_up_weight,
            contract_final_axis,
            preferred_element_type=jnp.float32,
        )
    ).astype(jnp.bfloat16)
    head_query, head_keys, head_values, head_grads = (
        lax.all_to_all(query_rows, "seq", split_axis=2, concat_axis=1, tiled=True),
        lax.all_to_all(keys_dest, "seq", split_axis=2, concat_axis=1, tiled=True),
        lax.all_to_all(values_dest, "seq", split_axis=2, concat_axis=1, tiled=True),
        lax.all_to_all(output_gradient[0], "seq", split_axis=2, concat_axis=1, tiled=True),
    )
    length = head_query.shape[0] * head_query.shape[1]
    reach_rows = length // 2 + length // 8
    head_width = head_query.shape[2]
    segment = segments[0]
    head_query = head_query.reshape(length, head_width)
    head_keys = head_keys.reshape(length, head_width)
    head_values = head_values.reshape(length, head_width)
    head_grads = head_grads.reshape(length, head_width)
    dquery_head, log_head = attend_head(
        head_query, head_keys, head_values, head_grads, segment, CLIPS, reach_rows
    )
    norm_pieces = [log_head]
    log_norm = jnp.stack(norm_pieces, axis=0)
    query_gradient = lax.all_to_all(
        dquery_head.reshape(block_count, length // block_count, head_width),
        "seq",
        split_axis=1,
        concat_axis=2,
        tiled=True,
    )
    adapter_gradient = lax.dot_general(
        query_gradient,
        adapter_up_weight,
        (((2,), (1,)), ((), ())),
        preferred_element_type=jnp.float32,
    ).astype(jnp.bfloat16)
    contract_tokens = (((0, 1), (0, 1)), ((), ()))
    down_part = lax.dot_general(
        feature_dest, adapter_gradient, contract_tokens, preferred_element_type=jnp.float32
    )
    up_part = lax.dot_general(
        adapter_params, query_gradient, contract_tokens, preferred_element_type=jnp.float32
    )
    down_share, up_share = (
        lax.psum_scatter(down_part, "seq", scatter_dimension=0, tiled=True),
        lax.psum_scatter(up_part, "seq", scatter_dimension=1, tiled=True),
    )
    down_total, up_total = lax.psum((down_share, up_share), "dp")
    grad_norm = 4.0 / math.sqrt(group_count * length)
    return (down_total * grad_norm, up_total * grad_norm, log_norm[None])


def solution(mesh):
    in_specs = (
        P("dp", None, "seq", None),
        P("dp", None, "seq", None),
        P("dp", None, "seq", None),
        P("dp", None, "seq", None),
        P("dp", None, "seq", None),
        P(),
        P(),
        P(),
        P("dp", None),
    )
    out_specs = (P("seq", None), P(None, "seq"), P("dp", "seq", None))

    plain = jax.shard_map(
        per_device, mesh=mesh, in_specs=in_specs, out_specs=out_specs, check_vma=False
    )

    def whole(features, *rest):
        fits = fits_tiles(mesh, features, rest[5])
        return (tiles_solution(mesh) if fits else plain)(features, *rest)

    return whole
```

```python
import functools
import math

import jax
import jax.numpy as jnp
import numpy as np
from jax import lax
from jax.experimental import pallas as pl
from jax.experimental.pallas import tpu as pltpu
from jax.sharding import Mesh
from jax.sharding import PartitionSpec as P

CAP = 2
CLIPS = 2
LANES = 128
HALF = 64
CORES = 2
SEQ = ("chip", "core")
QUERIES = 640
LOG2E = math.log2(math.e)
VMEM = pl.BlockSpec(memory_space=pltpu.VMEM)
SMEM = pl.BlockSpec(memory_space=pltpu.SMEM)
ANY = pl.BlockSpec(memory_space=pl.ANY)
NT = (((1,), (1,)), ((), ()))


def low_lanes(rows):
    return lax.broadcasted_iota(jnp.int32, (rows, LANES), 1) < HALF


def swap_halves(tile):
    return pltpu.roll(tile, HALF, 1)


def lane_tile(index):
    return pl.ds(pl.multiple_of(index * LANES, LANES), LANES)


def row_tile(index, rows):
    return pl.ds(pl.multiple_of(index * rows, rows), rows)


def quotient(value, size):
    return lax.shift_right_logical(value, size.bit_length() - 1)


def remainder(value, size):
    return value & (size - 1)


def seq_index():
    return lax.axis_index("chip") * CORES + lax.axis_index("core")


def each_hit(plan, me, groups, blocks, live, put):
    def over_dest(dest, _):
        def over_position(position, slot):
            source = plan[dest, position]
            hit = quotient(source, blocks) == me

            @pl.when(hit)
            def _():
                put(dest, slot, remainder(source, blocks))

            return slot + hit.astype(jnp.int32)

        lax.fori_loop(0, live, over_position, jnp.int32(0))
        return 0

    lax.fori_loop(0, groups, over_dest, 0)


def each_block(plan, me, blocks, live, take):
    groups_of = [quotient(plan[me, position], blocks) for position in range(live)]
    for position, group in enumerate(groups_of):
        slot = jnp.int32(0)
        for earlier in groups_of[:position]:
            slot = slot + (earlier == group).astype(jnp.int32)
        take(position, group, slot)


def each_half(slot, store):
    @pl.when(remainder(slot, 2) == 0)
    def _():
        store(slice(0, HALF))

    @pl.when(remainder(slot, 2) == 1)
    def _():
        store(slice(HALF, LANES))


def split(slot, pair):
    pair = pair.astype(jnp.float32)
    return jnp.where(remainder(slot, 2) == 0, pair, swap_halves(pair))


def pack_far_kernel(dims, plan_hbm, feat_hbm, base_hbm, keys_hbm, vals_hbm, down_hbm, up_hbm, *rest):
    groups, blocks, heads, rows, live = dims
    far_hbm, queries_hbm, adapter_hbm = rest[:3]
    plan, routes, feat, base, keys, vals, down, up, far_out, qbuf, abuf, sems, out_sems = rest[3:]
    me = lax.axis_index("dp")
    copies = [
        pltpu.make_async_copy(source, target, sems.at[index])
        for index, (source, target) in enumerate(
            (
                (plan_hbm, plan),
                (keys_hbm, keys),
                (vals_hbm, vals),
                (feat_hbm, feat),
                (down_hbm, down),
                (base_hbm, base),
                (up_hbm, up),
            )
        )
    ]
    for copy in copies:
        copy.start()

    def put_early(dest, slot, local):
        @pl.when(slot < CAP)
        def _():
            index = routes[0, 0]
            routes[0, 0] = index + 1
            for row, value in enumerate((dest, slot, local)):
                routes[row + 1, index] = value
            for head in range(heads):
                columns = slice(head * LANES, (head + 1) * LANES)
                far_out[head * groups + dest, slot] = keys[local, :, columns]
                far_out[head * groups + dest, CAP + slot] = vals[local, :, columns]

    def send(first, count, index):
        tiles = pl.ds(first, count)
        copy = pltpu.make_async_copy(far_out.at[:, tiles], far_hbm.at[:, tiles], out_sems.at[index])
        copy.start()
        return copy

    for copy in copies[:3]:
        copy.wait()
    routes[0, 0] = 0
    each_hit(plan, me, groups, blocks, live, put_early)
    early = send(0, 2 * CAP, 0)
    for copy in copies[3:]:
        copy.wait()
    narrow = lax.dot_general(feat[...], down[...], NT, preferred_element_type=jnp.float32)
    adapter = narrow.astype(jnp.bfloat16)
    lift = jnp.dot(adapter, up[...], preferred_element_type=jnp.float32)
    abuf[...] = jnp.concatenate([narrow, narrow], axis=1).astype(jnp.bfloat16).reshape(abuf.shape)
    qbuf[...] = (base[...].astype(jnp.float32) + lift.reshape(base.shape)).astype(jnp.bfloat16)

    def put_late(index, _):
        dest, slot, local = routes[1, index], routes[2, index], routes[3, index]

        for head in range(heads):
            columns = slice(head * LANES, (head + 1) * LANES)
            far_out[head * groups + dest, 2 * CAP + slot] = qbuf[local, :, columns]
        return 0

    lax.fori_loop(0, routes[0, 0], put_late, 0)
    late = send(2 * CAP, CAP, 1)
    rest_out = [
        pltpu.make_async_copy(qbuf, queries_hbm, out_sems.at[2]),
        pltpu.make_async_copy(abuf, adapter_hbm, out_sems.at[3]),
    ]
    for copy in rest_out:
        copy.start()
    for copy in [early, late] + rest_out:
        copy.wait()


def core_columns(chip, core):
    return pl.ds(pl.multiple_of((chip * 5 + core * 2) * LANES, LANES), 3 * LANES)


def pack_own_kernel(dims, plan, keys, vals, grad, queries, adapter, feat, *outs):
    groups, blocks, heads, rows, live = dims
    own_outs, feat_out, adapter_out = outs[:heads], outs[heads], outs[heads + 1]
    for chip in range(heads // CORES):
        feat_out[chip] = feat[:, core_columns(chip, 1 - lax.axis_index("core"))]
    extras = live - CAP
    me = lax.axis_index("dp")
    seq = seq_index()
    sources = (keys, vals, queries)

    def put(dest, slot, local):
        @pl.when(slot < CAP)
        def _():
            def store(lanes):
                adapter_out[dest, :, lanes] = adapter[local, :, lanes]

            each_half(slot, store)

        @pl.when(slot >= CAP)
        def _():
            extra = slot - CAP
            where = extras * 3 + live + quotient(extra, 2)
            for turn in range(heads):
                columns = lane_tile(seq ^ turn)
                for index, source in enumerate(sources):
                    own_outs[turn][index * extras + extra] = source[local, :, columns]

            def store(lanes):
                for turn in range(heads):
                    own_outs[turn][where, :, lanes] = adapter[local, :, lanes]

            each_half(slot, store)

    each_hit(plan, me, groups, blocks, live, put)
    for turn in range(heads):
        columns = lane_tile(seq ^ turn)
        for position in range(live):
            own_outs[turn][extras * 3 + position] = grad[position, :, columns]


def attend_kernel(dims, plan, seg, up, adapter, far_in, *rest):
    groups, blocks, heads, rows, live = dims
    chips = heads // CORES
    core = lax.axis_index("core")
    own_ins = rest[:heads]
    part_hbm = rest[heads + 1]
    own_parts = rest[heads + 2 : heads + 2 + chips]
    dqs, log_hbm, part_out, log_out, routes, sems, qs, ks, vs, gs, parts = rest[
        heads + 2 + chips :
    ]
    extras = live - CAP
    me = lax.axis_index("dp")
    seq = seq_index()
    length = seg.shape[1]
    reach = live * LANES
    scaling = 1.0 / math.sqrt(LANES)

    def take(position, group, slot):
        routes[0, position] = group
        routes[1, position] = slot
        far = (group != me) | (slot < CAP)

        @pl.when(far)
        def _():
            for part in range(heads):
                index = part * groups + group
                where = row_tile(position * heads + part, rows)
                ks[where, :] = far_in[index, slot]
                vs[where, :] = far_in[index, CAP + slot]
                qs[where, :] = far_in[index, 2 * CAP + slot]

        @pl.when(jnp.logical_not(far))
        def _():
            extra = slot - CAP
            for turn in range(heads):
                where = row_tile(position * heads + (seq ^ turn), rows)
                ks[where, :] = own_ins[turn][extra]
                vs[where, :] = own_ins[turn][extras + extra]
                qs[where, :] = own_ins[turn][2 * extras + extra]

    each_block(plan, me, blocks, live, take)
    for turn in range(heads):
        for position in range(live):
            gs[row_tile(position * heads + (seq ^ turn), rows), :] = own_ins[turn][
                extras * 3 + position
            ]

    count = jnp.sum((seg[...] < CLIPS - 1).astype(jnp.float32), axis=1, keepdims=True).astype(
        jnp.int32
    )
    key_rows = ks[...]
    value_rows = vs[...]
    key_columns = key_rows.T
    key_index = lax.broadcasted_iota(jnp.int32, (reach, 1), 0)
    always = length - reach
    up_head = up[:, lane_tile(seq)]
    up_twice = jnp.concatenate([up_head, up_head], axis=0)
    for start in range(0, reach, QUERIES):
        count_here = min(QUERIES, reach - start)
        span = slice(start, start + count_here)
        scores = lax.dot_general(key_rows, qs[span, :], NT, preferred_element_type=jnp.float32)
        scores = jnp.concatenate(
            [
                scores[:always],
                jnp.where(key_index[always:] < count, scores[always:], -1e30),
            ],
            axis=0,
        )
        dprob = lax.dot_general(value_rows, gs[span, :], NT, preferred_element_type=jnp.float32)
        maximum = jnp.max(scores, axis=0, keepdims=True)
        exponent = jnp.exp2((scores - maximum) * (scaling * LOG2E))
        total = jnp.sum(exponent, axis=0, keepdims=True)
        delta = jnp.sum(exponent * dprob, axis=0, keepdims=True) / total
        dscore = (exponent * (dprob - delta)).astype(jnp.bfloat16)
        dquery = jnp.dot(key_columns, dscore, preferred_element_type=jnp.float32)
        query_index = lax.broadcasted_iota(jnp.int32, (1, count_here), 1) + start
        in_clip = query_index < count
        dquery = jnp.where(in_clip, dquery * (scaling / total), 0.0).astype(jnp.bfloat16)
        dqs[:, span] = dquery
        log_out[0, :, span] = jnp.where(in_clip, maximum * scaling + jnp.log(total), 0.0)
    log_out[0, :, reach:] = jnp.zeros((1, length - reach), jnp.float32)
    log_copy = pltpu.make_async_copy(log_out, log_hbm, sems.at[0])
    log_copy.start()
    dquery_all = dqs[...]
    parts[...] = lax.dot_general(
        dquery_all, up_twice, (((0,), (1,)), ((), ())), preferred_element_type=jnp.float32
    ).astype(jnp.bfloat16)

    def put(position):
        group, slot = routes[0, position], routes[1, position]
        far = (group != me) | (slot < CAP)

        @pl.when(far)
        def _():
            def store(lanes):
                for turn in range(heads):
                    chip, side = turn // CORES, turn % CORES
                    where = row_tile(position * heads + chip * CORES + (core ^ side), rows)
                    part_out[chip * groups + group, side, :, lanes] = parts[where, lanes]

            each_half(slot, store)

        @pl.when(jnp.logical_not(far))
        def _():
            pair = quotient(slot - CAP, 2)

            def store(lanes):
                for turn in range(heads):
                    where = row_tile(position * heads + (seq ^ turn), rows)
                    own_parts[turn // CORES][turn % CORES, pair, :, lanes] = parts[where, lanes]

            each_half(slot, store)

    for position in range(live):
        put(position)
    for chip in range(chips):
        for group in range(groups):
            part_out[chip * groups + group, CORES] = adapter[group]
    part_copy = pltpu.make_async_copy(part_out, part_hbm, sems.at[1])
    part_copy.start()
    log_copy.wait()
    part_copy.wait()


def head_sum_kernel(parts, *refs):
    extras, out = refs[:-1], refs[-1]
    pairs = extras[0].shape[1]
    peers = parts.shape[0]
    tiles = (out.shape[0] - peers) // CORES
    groups = tiles - pairs

    def total(terms):
        value = terms[0].astype(jnp.float32)
        for term in terms[1:]:
            value = value + term.astype(jnp.float32)
        return value.astype(jnp.bfloat16)

    for side in range(CORES):
        for group in range(groups):
            out[side * tiles + group] = total(
                [parts[peer, side] for peer in range(group, peers, groups)]
            )
        for pair in range(pairs):
            out[side * tiles + groups + pair] = total([extra[side, pair] for extra in extras])
    for peer in range(peers):
        out[CORES * tiles + peer] = parts[peer, CORES]


def product_kernel(dims, plan, feat, feat_other, mine, other, dquery, *rest):
    groups, blocks, heads, rows, live = dims
    own_ins = rest[:heads]
    out, up_out, sums, grads, ads = rest[heads:]
    extras = live - CAP
    me = lax.axis_index("dp")
    core = lax.axis_index("core")
    seq = seq_index()
    tiles = sums.shape[1]
    ads[...] = jnp.zeros_like(ads)

    def take(position, group, slot):
        far = (group != me) | (slot < CAP)

        @pl.when(far)
        def _():
            def store(lanes):
                for chip in range(heads // CORES):
                    tile = CORES * tiles + chip * groups + group
                    for source, which in ((mine, core), (other, 1 - core)):
                        where = row_tile(position * heads + chip * CORES + which, rows)
                        ads[where, lanes] = source[tile, :, lanes]

            each_half(slot, store)

        @pl.when(jnp.logical_not(far))
        def _():
            pair = extras * 3 + live + quotient(slot - CAP, 2)

            def store(lanes):
                for turn in range(heads):
                    where = row_tile(position * heads + (seq ^ turn), rows)
                    ads[where, lanes] = own_ins[turn][pair, :, lanes]

            each_half(slot, store)

    each_block(plan, me, blocks, live, take)
    up_part = jnp.dot(dquery[...], ads[...], preferred_element_type=jnp.float32)
    up_out[...] = (up_part + swap_halves(up_part)).T[: up_out.shape[0]].astype(jnp.bfloat16)
    for index in range(tiles):
        sums[0, index] = mine[index].astype(jnp.float32) + other[tiles + index].astype(jnp.float32)
        sums[1, index] = other[index].astype(jnp.float32) + mine[tiles + index].astype(jnp.float32)
    grads[...] = jnp.zeros_like(grads)

    def put(dest, slot, local):
        index = jnp.where(slot < CAP, dest, groups - 1 + quotient(slot, 2))
        for owner in range(CORES):
            grads[owner, local] = split(slot, sums[owner, index])

    each_hit(plan, me, groups, blocks, live, put)
    low = low_lanes(HALF // 2)
    columns = grads[...].reshape(CORES * blocks * rows, LANES).T[:HALF].astype(jnp.bfloat16)
    even = core == 0
    for chip in range(heads // CORES):
        features = jnp.concatenate([feat[:, core_columns(chip, core)], feat_other[chip]], axis=0)
        product = jnp.dot(columns, features, preferred_element_type=jnp.float32)
        first, second, third = (
            product[:, index * LANES : (index + 1) * LANES] for index in range(3)
        )
        shared = jnp.where(even, third, first)
        upper, lower = shared[: HALF // 2], shared[HALF // 2 :]
        out[chip, :HALF] = jnp.where(even, first, second).astype(jnp.bfloat16)
        out[chip, HALF : 2 * HALF] = jnp.where(even, second, third).astype(jnp.bfloat16)
        out[chip, 2 * HALF :] = jnp.where(
            even,
            jnp.where(low, upper, swap_halves(lower)),
            jnp.where(low, swap_halves(upper), lower),
        ).astype(jnp.bfloat16)


def join_kernel(parts, up_part, out):
    total = parts[0].astype(jnp.float32)
    for head in range(1, parts.shape[0]):
        total = total + parts[head].astype(jnp.float32)
    out[: total.shape[0]] = total.astype(jnp.bfloat16)
    out[total.shape[0] :] = up_part[...]


def total_kernel(grad_norm, *rest):
    groups = len(rest) - 3
    down_out, up_out, held = rest[groups:]
    me = lax.axis_index("dp")
    seq = seq_index()
    for turn in range(groups):
        held[me ^ turn] = rest[turn][...].astype(jnp.float32)
    total = held[0]
    for group in range(1, groups):
        total = total + held[group]
    total = total * grad_norm
    first, second = total[:HALF], total[HALF : 2 * HALF]
    shared = total[2 * HALF : 2 * HALF + HALF // 2]
    up_out[...] = total[2 * HALF + HALF // 2 :]
    swapped = swap_halves(shared)
    low_half = jnp.concatenate([shared, swapped], axis=0)
    high_half = jnp.concatenate([swapped, shared], axis=0)
    even = jnp.concatenate([first, second, low_half], axis=1)
    odd = pltpu.roll(jnp.concatenate([first, second, high_half], axis=1), HALF, 1)
    down = jnp.where(remainder(seq, 2) == 0, even, odd)
    down_out[...] = down[:, : down_out.shape[1]]


def call(kernel, outs, specs, scratch, flops, moved, *args, vmem_mib=32, out_specs=None):
    shapes = [jax.ShapeDtypeStruct(shape, dtype) for shape, dtype in outs]
    return pl.pallas_call(
        kernel,
        out_shape=shapes,
        in_specs=specs,
        out_specs=out_specs or [VMEM] * len(shapes),
        scratch_shapes=scratch,
        compiler_params=pltpu.CompilerParams(vmem_limit_bytes=vmem_mib << 20),
        cost_estimate=pl.CostEstimate(flops=flops, bytes_accessed=moved, transcendentals=0),
    )(*args)


def exchange(value, axis, size, turn):
    return lax.ppermute(value, axis, [(peer, peer ^ turn) for peer in range(size)])


def per_device_tiles(
    features,
    frozen_query_weight,
    source_keys,
    source_values,
    output_gradient,
    adapter_down_weight,
    adapter_up_weight,
    source_block_plan,
    segments,
):
    groups = lax.axis_size("dp")
    chips = lax.axis_size("chip")
    heads = chips * CORES
    _, blocks, rows, width = features.shape
    length = segments.shape[1]
    live = (length // 2 + length // 8) // LANES
    reach = live * LANES
    rank = adapter_up_weight.shape[0]
    extras = live - CAP
    pairs = (extras + 1) // 2
    dims = (groups, blocks, heads, rows, live)
    bf16 = jnp.bfloat16
    f32 = jnp.float32
    peers = groups * heads
    everyone = SEQ + ("dp",)
    flat = features[0].reshape(blocks * rows, width)
    far_shape = (peers, CAP * 3, rows, LANES)
    own_shape = (extras * 3 + live + pairs, rows, LANES)
    rows_shape = (blocks, rows, heads * LANES)

    far_send, queries, adapter = call(
        functools.partial(pack_far_kernel, dims),
        [(far_shape, bf16), (rows_shape, bf16), ((blocks, rows, LANES), bf16)],
        [ANY] * 7,
        [
            pltpu.SMEM((groups, blocks), jnp.int32),
            pltpu.SMEM((4, blocks), jnp.int32),
            pltpu.VMEM((blocks * rows, width), bf16),
            pltpu.VMEM(rows_shape, bf16),
            pltpu.VMEM(rows_shape, bf16),
            pltpu.VMEM(rows_shape, bf16),
            pltpu.VMEM((rank, width), bf16),
            pltpu.VMEM((rank, heads * LANES), bf16),
            pltpu.VMEM(far_shape, bf16),
            pltpu.VMEM(rows_shape, bf16),
            pltpu.VMEM((blocks, rows, LANES), bf16),
            pltpu.SemaphoreType.DMA((7,)),
            pltpu.SemaphoreType.DMA((4,)),
        ],
        60_000_000,
        4_000_000,
        source_block_plan,
        flat,
        frozen_query_weight[0],
        source_keys[0],
        source_values[0],
        adapter_down_weight.T,
        adapter_up_weight,
        vmem_mib=60,
        out_specs=[ANY] * 3,
    )
    own_send = call(
        functools.partial(pack_own_kernel, dims),
        [(own_shape, bf16)] * heads
        + [((chips, blocks * rows, 3 * LANES), bf16), ((groups, rows, LANES), bf16)],
        [SMEM] + [VMEM] * 6,
        [],
        0,
        1_600_000,
        source_block_plan,
        source_keys[0],
        source_values[0],
        output_gradient[0],
        queries,
        adapter,
        flat,
    )
    feat_other = exchange(own_send[heads], "core", CORES, 1)
    own = [exchange(own_send[turn], SEQ, heads, turn) for turn in range(heads - 1, 0, -1)]
    own = [own_send[0]] + own[::-1]
    far = lax.all_to_all(far_send, everyone, 0, 0, tiled=True)
    attended = call(
        functools.partial(attend_kernel, dims),
        [((chips * groups, CORES + 1, rows, LANES), bf16)]
        + [((CORES, pairs, rows, LANES), bf16)] * chips
        + [((LANES, reach), bf16), ((1, 1, length), f32)],
        [SMEM] + [VMEM] * (4 + heads) + [ANY],
        [
            pltpu.VMEM((chips * groups, CORES + 1, rows, LANES), bf16),
            pltpu.VMEM((1, 1, length), f32),
            pltpu.SMEM((2, live), jnp.int32),
            pltpu.SemaphoreType.DMA((2,)),
        ]
        + [pltpu.VMEM((reach, LANES), bf16)] * 5,
        600_000_000,
        3_000_000,
        source_block_plan,
        segments,
        adapter_up_weight,
        own_send[heads + 1],
        far,
        *own,
        feat_other,
        out_specs=[ANY] + [VMEM] * (chips + 1) + [ANY],
    )
    own_parts = [
        exchange(attended[1 + turn], "chip", chips, turn) for turn in range(chips - 1, 0, -1)
    ]
    part = lax.all_to_all(attended[0], ("chip", "dp"), 0, 0, tiled=True)
    dquery, log_norm = attended[1 + chips :]
    tiles = groups + pairs
    (mine,) = call(
        head_sum_kernel,
        [((CORES * tiles + chips * groups, rows, LANES), bf16)],
        [VMEM] * (1 + chips),
        [],
        0,
        300_000,
        part,
        *own_parts,
        attended[1],
    )
    shares, up_part = call(
        functools.partial(product_kernel, dims),
        [((chips, HALF * 5 // 2, LANES), bf16), ((rank, LANES), bf16)],
        [SMEM] + [VMEM] * (5 + heads),
        [
            pltpu.VMEM((CORES, tiles, rows, LANES), f32),
            pltpu.VMEM((CORES, blocks, rows, LANES), f32),
            pltpu.VMEM((reach, LANES), bf16),
        ],
        60_000_000,
        2_000_000,
        source_block_plan,
        flat,
        feat_other,
        mine,
        exchange(mine, "core", CORES, 1),
        dquery,
        *own,
    )
    shares = lax.all_to_all(shares, "chip", 0, 0, tiled=True)
    (joined,) = call(
        join_kernel,
        [((HALF * 5 // 2 + rank, LANES), bf16)],
        [VMEM] * 2,
        [],
        0,
        600_000,
        shares,
        up_part,
    )
    sums = [joined] + [exchange(joined, "dp", groups, turn) for turn in range(1, groups)]
    down, up = call(
        functools.partial(total_kernel, 4.0 / math.sqrt(groups * length)),
        [((rank, width // heads), f32), ((rank, LANES), f32)],
        [VMEM] * groups,
        [pltpu.VMEM((groups,) + joined.shape, f32)],
        0,
        400_000,
        *sums,
    )
    return (down.T, up, log_norm)


def power_of_two(size):
    return size > 1 and size & (size - 1) == 0


def fits_tiles(mesh, features, adapter_up_weight):
    groups, heads = mesh.shape["dp"], mesh.shape["seq"]
    rows = features.shape[2] // heads
    return (
        rows % 16 == 0
        and features.shape[2] == LANES
        and features.shape[3] * 2 == heads * 5 * LANES
        and power_of_two(heads)
        and power_of_two(groups)
        and power_of_two(features.shape[1])
        and adapter_up_weight.shape == (HALF, heads * LANES)
    )


def split_mesh(mesh):
    groups, heads = mesh.shape["dp"], mesh.shape["seq"]
    devices = np.asarray(mesh.devices).reshape(groups, heads // CORES, CORES)
    return Mesh(devices, ("dp",) + SEQ)


def tiles_solution(mesh):
    row_spec = P("dp", None, SEQ, None)
    return jax.shard_map(
        per_device_tiles,
        mesh=split_mesh(mesh),
        in_specs=(row_spec,) * 5 + (P(), P(), P(), P("dp", None)),
        out_specs=(P(SEQ, None), P(None, SEQ), P("dp", SEQ, None)),
        check_vma=False,
    )


def attend_head(query, key_rows, value_rows, cotangent, segment, clip_count, reach_rows):
    length = query.shape[0]
    width = query.shape[1]
    piece_count = 8
    piece_rows = reach_rows // piece_count
    scaling = 1.0 / math.sqrt(width)
    query_padded = jnp.pad(query, ((0, reach_rows), (0, 0)))
    grad_padded = jnp.pad(cotangent, ((0, reach_rows), (0, 0)))
    keys_padded = jnp.pad(key_rows, ((0, reach_rows), (0, 0)))
    values_padded = jnp.pad(value_rows, ((0, reach_rows), (0, 0)))
    segment_padded = jnp.pad(segment, (0, reach_rows), constant_values=-1)
    clip_ids = jnp.arange(clip_count, dtype=jnp.int32)
    starts = jnp.sum((segment[None, :] < clip_ids[:, None]).astype(jnp.int32), axis=1)

    def piece_pass(piece_index):
        clip_slice = piece_index // piece_count
        start = lax.dynamic_index_in_dim(starts, clip_slice, 0, keepdims=False)
        query_start = start + piece_index % piece_count * piece_rows
        query_tile = lax.dynamic_slice_in_dim(query_padded, query_start, piece_rows, 0)
        grad_tile = lax.dynamic_slice_in_dim(grad_padded, query_start, piece_rows, 0)
        seg_tile = lax.dynamic_slice_in_dim(segment_padded, query_start, piece_rows, 0)
        key_tile = lax.dynamic_slice_in_dim(keys_padded, start, reach_rows, 0)
        value_tile = lax.dynamic_slice_in_dim(values_padded, start, reach_rows, 0)
        seg_cols = lax.dynamic_slice_in_dim(segment_padded, start, reach_rows, 0)
        in_clip = seg_tile == clip_slice
        allowed = in_clip[:, None] & (seg_cols == clip_slice)[None, :]
        scores = (
            lax.dot_general(
                query_tile, key_tile, (((1,), (1,)), ((), ())), preferred_element_type=jnp.float32
            )
            * scaling
        )
        scores = jnp.where(allowed, scores, -1e30)
        maximum = jnp.max(scores, axis=1, keepdims=True)
        exponent = jnp.where(allowed, jnp.exp(scores - maximum), 0.0)
        totals = jnp.where(in_clip[:, None], jnp.sum(exponent, axis=1, keepdims=True), 1.0)
        log_norm = jnp.where(in_clip, maximum[:, 0] + jnp.log(totals[:, 0]), 0.0)
        probs = exponent / totals
        weights = probs.astype(jnp.bfloat16)
        attended = jnp.dot(weights, value_tile, preferred_element_type=jnp.float32)
        delta = jnp.sum(grad_tile.astype(jnp.float32) * attended, axis=1, keepdims=True)
        dprob = lax.dot_general(
            grad_tile, value_tile, (((1,), (1,)), ((), ())), preferred_element_type=jnp.float32
        )
        dscore = (probs * (dprob - delta)).astype(jnp.bfloat16)
        query_gradient = (
            jnp.dot(dscore, key_tile, preferred_element_type=jnp.float32) * scaling
        ).astype(jnp.bfloat16)
        query_gradient = jnp.where(in_clip[:, None], query_gradient, jnp.zeros((), jnp.bfloat16))
        return (query_gradient, log_norm, query_start)

    total_pieces = piece_count * (clip_count - 1)
    dquery_pieces, log_pieces, piece_starts = lax.map(
        piece_pass, jnp.arange(total_pieces, dtype=jnp.int32)
    )

    def place(index, carry):
        grad_total, log_total = carry
        where_at = lax.dynamic_index_in_dim(piece_starts, index, 0, keepdims=False)
        grad_piece = lax.dynamic_index_in_dim(dquery_pieces, index, 0, keepdims=False)
        log_piece = lax.dynamic_index_in_dim(log_pieces, index, 0, keepdims=False)
        grad_old = lax.dynamic_slice_in_dim(grad_total, where_at, piece_rows, 0)
        log_old = lax.dynamic_slice_in_dim(log_total, where_at, piece_rows, 0)
        grad_total = lax.dynamic_update_slice_in_dim(grad_total, grad_old + grad_piece, where_at, 0)
        log_total = lax.dynamic_update_slice_in_dim(log_total, log_old + log_piece, where_at, 0)
        return (grad_total, log_total)

    grad_init = jnp.zeros((length + reach_rows, width), jnp.bfloat16)
    log_init = jnp.zeros((length + reach_rows,), jnp.float32)
    grad_total, log_total = lax.fori_loop(0, total_pieces, place, (grad_init, log_init))
    return (grad_total[:length], log_total[:length])


def routing_tables(source_block_plan, group_index, cap_slots):
    group_count, block_count = source_block_plan.shape
    source_group = source_block_plan // block_count
    source_local = source_block_plan % block_count
    dest_groups = jnp.arange(group_count, dtype=jnp.int32)[:, None]
    outgoing = (source_group == group_index) & (dest_groups != group_index)
    out_rank = jnp.cumsum(outgoing.astype(jnp.int32), axis=1) - 1
    slot_ids = jnp.arange(cap_slots, dtype=jnp.int32)
    chosen = outgoing[:, :, None] & (out_rank[:, :, None] == slot_ids[None, None, :])
    send_index = jnp.sum(jnp.where(chosen, source_local[:, :, None], 0), axis=1)
    send_valid = jnp.any(chosen, axis=1)
    own_group = lax.dynamic_index_in_dim(source_group, group_index, 0, keepdims=False)
    own_local = lax.dynamic_index_in_dim(source_local, group_index, 0, keepdims=False)
    incoming = own_group != group_index
    positions = jnp.arange(block_count, dtype=jnp.int32)
    earlier = (own_group[None, :] == own_group[:, None]) & (positions[None, :] < positions[:, None])
    in_rank = jnp.sum(earlier.astype(jnp.int32), axis=1)
    return (send_index, send_valid, incoming, own_group, in_rank, own_local)


def pack_blocks(local, send_index, send_valid):
    picked = jnp.take(local, send_index, axis=0)
    return jnp.where(send_valid[:, :, None, None], picked, jnp.zeros((), local.dtype))


def unpack_blocks(received, local, tables, cap_slots):
    incoming, own_group, in_rank, own_local = tables
    flat = received.reshape((-1,) + received.shape[2:])
    slot_index = jnp.where(incoming, own_group * cap_slots + in_rank, 0)
    remote = jnp.take(flat, slot_index, axis=0)
    staying = jnp.take(local, own_local, axis=0)
    return jnp.where(incoming[:, None, None], remote, staying)


def per_device(
    features,
    frozen_query_weight,
    source_keys,
    source_values,
    output_gradient,
    adapter_down_weight,
    adapter_up_weight,
    source_block_plan,
    segments,
):
    group_count = lax.axis_size("dp")
    group_index = lax.axis_index("dp")
    block_count = features.shape[1]
    feat_local = features[0]
    base_local = frozen_query_weight[0]
    keys_local = source_keys[0]
    values_local = source_values[0]
    send_index, send_valid, incoming, own_group, in_rank, own_local = routing_tables(
        source_block_plan, group_index, CAP
    )
    tables = (incoming, own_group, in_rank, own_local)
    contract_final_axis = (((2,), (0,)), ((), ()))
    shuffled = (
        lax.all_to_all(
            pack_blocks(feat_local, send_index, send_valid),
            "dp",
            split_axis=0,
            concat_axis=0,
            tiled=True,
        ),
        lax.all_to_all(
            pack_blocks(base_local, send_index, send_valid),
            "dp",
            split_axis=0,
            concat_axis=0,
            tiled=True,
        ),
        lax.all_to_all(
            pack_blocks(keys_local, send_index, send_valid),
            "dp",
            split_axis=0,
            concat_axis=0,
            tiled=True,
        ),
        lax.all_to_all(
            pack_blocks(values_local, send_index, send_valid),
            "dp",
            split_axis=0,
            concat_axis=0,
            tiled=True,
        ),
    )
    feature_dest = unpack_blocks(shuffled[0], feat_local, tables, CAP)
    base_query_dest = unpack_blocks(shuffled[1], base_local, tables, CAP)
    keys_dest = unpack_blocks(shuffled[2], keys_local, tables, CAP)
    values_dest = unpack_blocks(shuffled[3], values_local, tables, CAP)
    adapter_params = lax.dot_general(
        feature_dest, adapter_down_weight, contract_final_axis, preferred_element_type=jnp.float32
    ).astype(jnp.bfloat16)
    query_rows = (
        base_query_dest.astype(jnp.float32)
        + lax.dot_general(
            adapter_params,
            adapter_up_weight,
            contract_final_axis,
            preferred_element_type=jnp.float32,
        )
    ).astype(jnp.bfloat16)
    head_query, head_keys, head_values, head_grads = (
        lax.all_to_all(query_rows, "seq", split_axis=2, concat_axis=1, tiled=True),
        lax.all_to_all(keys_dest, "seq", split_axis=2, concat_axis=1, tiled=True),
        lax.all_to_all(values_dest, "seq", split_axis=2, concat_axis=1, tiled=True),
        lax.all_to_all(output_gradient[0], "seq", split_axis=2, concat_axis=1, tiled=True),
    )
    length = head_query.shape[0] * head_query.shape[1]
    reach_rows = length // 2 + length // 8
    head_width = head_query.shape[2]
    segment = segments[0]
    head_query = head_query.reshape(length, head_width)
    head_keys = head_keys.reshape(length, head_width)
    head_values = head_values.reshape(length, head_width)
    head_grads = head_grads.reshape(length, head_width)
    dquery_head, log_head = attend_head(
        head_query, head_keys, head_values, head_grads, segment, CLIPS, reach_rows
    )
    norm_pieces = [log_head]
    log_norm = jnp.stack(norm_pieces, axis=0)
    query_gradient = lax.all_to_all(
        dquery_head.reshape(block_count, length // block_count, head_width),
        "seq",
        split_axis=1,
        concat_axis=2,
        tiled=True,
    )
    adapter_gradient = lax.dot_general(
        query_gradient,
        adapter_up_weight,
        (((2,), (1,)), ((), ())),
        preferred_element_type=jnp.float32,
    ).astype(jnp.bfloat16)
    contract_tokens = (((0, 1), (0, 1)), ((), ()))
    down_part = lax.dot_general(
        feature_dest, adapter_gradient, contract_tokens, preferred_element_type=jnp.float32
    )
    up_part = lax.dot_general(
        adapter_params, query_gradient, contract_tokens, preferred_element_type=jnp.float32
    )
    down_share, up_share = (
        lax.psum_scatter(down_part, "seq", scatter_dimension=0, tiled=True),
        lax.psum_scatter(up_part, "seq", scatter_dimension=1, tiled=True),
    )
    down_total, up_total = lax.psum((down_share, up_share), "dp")
    grad_norm = 4.0 / math.sqrt(group_count * length)
    return (down_total * grad_norm, up_total * grad_norm, log_norm[None])


def solution(mesh):
    in_specs = (
        P("dp", None, "seq", None),
        P("dp", None, "seq", None),
        P("dp", None, "seq", None),
        P("dp", None, "seq", None),
        P("dp", None, "seq", None),
        P(),
        P(),
        P(),
        P("dp", None),
    )
    out_specs = (P("seq", None), P(None, "seq"), P("dp", "seq", None))

    plain = jax.shard_map(
        per_device, mesh=mesh, in_specs=in_specs, out_specs=out_specs, check_vma=False
    )

    def whole(features, *rest):
        fits = fits_tiles(mesh, features, rest[5])
        return (tiles_solution(mesh) if fits else plain)(features, *rest)

    return whole
```

```python
import functools
import math

import jax
import jax.numpy as jnp
import numpy as np
from jax import lax
from jax.experimental import pallas as pl
from jax.experimental.pallas import tpu as pltpu
from jax.sharding import Mesh
from jax.sharding import PartitionSpec as P

CAP = 2
CLIPS = 2
LANES = 128
HALF = 64
CORES = 2
SEQ = ("chip", "core")
QUERIES = 640
LOG2E = math.log2(math.e)
VMEM = pl.BlockSpec(memory_space=pltpu.VMEM)
SMEM = pl.BlockSpec(memory_space=pltpu.SMEM)
ANY = pl.BlockSpec(memory_space=pl.ANY)
NT = (((1,), (1,)), ((), ()))


def low_lanes(rows):
    return lax.broadcasted_iota(jnp.int32, (rows, LANES), 1) < HALF


def swap_halves(tile):
    return pltpu.roll(tile, HALF, 1)


def lane_tile(index):
    return pl.ds(pl.multiple_of(index * LANES, LANES), LANES)


def row_tile(index, rows):
    return pl.ds(pl.multiple_of(index * rows, rows), rows)


def quotient(value, size):
    return lax.shift_right_logical(value, size.bit_length() - 1)


def remainder(value, size):
    return value & (size - 1)


def seq_index():
    return lax.axis_index("chip") * CORES + lax.axis_index("core")


def each_hit(plan, me, groups, blocks, live, put):
    def over_dest(dest, _):
        def over_position(position, slot):
            source = plan[dest, position]
            hit = quotient(source, blocks) == me

            @pl.when(hit)
            def _():
                put(dest, slot, remainder(source, blocks))

            return slot + hit.astype(jnp.int32)

        lax.fori_loop(0, live, over_position, jnp.int32(0))
        return 0

    lax.fori_loop(0, groups, over_dest, 0)


def each_block(plan, me, blocks, live, take):
    groups_of = [quotient(plan[me, position], blocks) for position in range(live)]
    for position, group in enumerate(groups_of):
        slot = jnp.int32(0)
        for earlier in groups_of[:position]:
            slot = slot + (earlier == group).astype(jnp.int32)
        take(position, group, slot)


def each_half(slot, store):
    @pl.when(remainder(slot, 2) == 0)
    def _():
        store(slice(0, HALF))

    @pl.when(remainder(slot, 2) == 1)
    def _():
        store(slice(HALF, LANES))


def split(slot, pair):
    pair = pair.astype(jnp.float32)
    return jnp.where(remainder(slot, 2) == 0, pair, swap_halves(pair))


def pack_far_kernel(dims, plan_hbm, feat_hbm, base_hbm, keys_hbm, vals_hbm, down_hbm, up_hbm, *rest):
    groups, blocks, heads, rows, live = dims
    far_hbm, queries_hbm, adapter_hbm = rest[:3]
    plan, routes, feat, base, keys, vals, down, up, far_out, qbuf, abuf, sems, out_sems = rest[3:]
    me = lax.axis_index("dp")
    copies = [
        pltpu.make_async_copy(source, target, sems.at[index])
        for index, (source, target) in enumerate(
            (
                (plan_hbm, plan),
                (keys_hbm, keys),
                (vals_hbm, vals),
                (feat_hbm, feat),
                (down_hbm, down),
                (base_hbm, base),
                (up_hbm, up),
            )
        )
    ]
    for copy in copies:
        copy.start()

    def put_early(dest, slot, local):
        @pl.when(slot < CAP)
        def _():
            index = routes[0, 0]
            routes[0, 0] = index + 1
            for row, value in enumerate((dest, slot, local)):
                routes[row + 1, index] = value
            for head in range(heads):
                columns = slice(head * LANES, (head + 1) * LANES)
                far_out[head * groups + dest, slot] = keys[local, :, columns]
                far_out[head * groups + dest, CAP + slot] = vals[local, :, columns]

    def send(first, count, index):
        tiles = pl.ds(first, count)
        copy = pltpu.make_async_copy(far_out.at[:, tiles], far_hbm.at[:, tiles], out_sems.at[index])
        copy.start()
        return copy

    for copy in copies[:3]:
        copy.wait()
    routes[0, 0] = 0
    each_hit(plan, me, groups, blocks, live, put_early)
    early = send(0, 2 * CAP, 0)
    for copy in copies[3:5]:
        copy.wait()
    narrow = lax.dot_general(feat[...], down[...], NT, preferred_element_type=jnp.float32)
    adapter = narrow.astype(jnp.bfloat16)
    for copy in copies[5:]:
        copy.wait()
    lift = jnp.dot(adapter, up[...], preferred_element_type=jnp.float32)
    abuf[...] = jnp.concatenate([narrow, narrow], axis=1).astype(jnp.bfloat16).reshape(abuf.shape)
    qbuf[...] = (base[...].astype(jnp.float32) + lift.reshape(base.shape)).astype(jnp.bfloat16)

    rest_out = [
        pltpu.make_async_copy(qbuf, queries_hbm, out_sems.at[2]),
        pltpu.make_async_copy(abuf, adapter_hbm, out_sems.at[3]),
    ]
    for copy in rest_out:
        copy.start()

    def put_late(index, _):
        dest, slot, local = routes[1, index], routes[2, index], routes[3, index]

        for head in range(heads):
            columns = slice(head * LANES, (head + 1) * LANES)
            far_out[head * groups + dest, 2 * CAP + slot] = qbuf[local, :, columns]
        return 0

    lax.fori_loop(0, routes[0, 0], put_late, 0)
    late = send(2 * CAP, CAP, 1)
    for copy in [early, late] + rest_out:
        copy.wait()


def core_columns(chip, core):
    return pl.ds(pl.multiple_of((chip * 5 + core * 2) * LANES, LANES), 3 * LANES)


def pack_own_kernel(dims, plan, keys, vals, grad, queries, adapter, feat, *outs):
    groups, blocks, heads, rows, live = dims
    own_outs, feat_out, adapter_out = outs[:heads], outs[heads], outs[heads + 1]
    for chip in range(heads // CORES):
        feat_out[chip] = feat[:, core_columns(chip, 1 - lax.axis_index("core"))]
    extras = live - CAP
    me = lax.axis_index("dp")
    seq = seq_index()
    sources = (keys, vals, queries)

    def put(dest, slot, local):
        @pl.when(slot < CAP)
        def _():
            def store(lanes):
                adapter_out[dest, :, lanes] = adapter[local, :, lanes]

            each_half(slot, store)

        @pl.when(slot >= CAP)
        def _():
            extra = slot - CAP
            where = extras * 3 + live + quotient(extra, 2)
            for turn in range(heads):
                columns = lane_tile(seq ^ turn)
                for index, source in enumerate(sources):
                    own_outs[turn][index * extras + extra] = source[local, :, columns]

            def store(lanes):
                for turn in range(heads):
                    own_outs[turn][where, :, lanes] = adapter[local, :, lanes]

            each_half(slot, store)

    each_hit(plan, me, groups, blocks, live, put)
    for turn in range(heads):
        columns = lane_tile(seq ^ turn)
        for position in range(live):
            own_outs[turn][extras * 3 + position] = grad[position, :, columns]


def attend_kernel(dims, plan, seg, up, adapter, far_in, *rest):
    groups, blocks, heads, rows, live = dims
    chips = heads // CORES
    core = lax.axis_index("core")
    own_ins = rest[:heads]
    part_hbm = rest[heads + 1]
    own_parts = rest[heads + 2 : heads + 2 + chips]
    dqs, log_hbm, part_out, log_out, routes, sems, qs, ks, vs, gs, parts = rest[
        heads + 2 + chips :
    ]
    extras = live - CAP
    me = lax.axis_index("dp")
    seq = seq_index()
    length = seg.shape[1]
    reach = live * LANES
    scaling = 1.0 / math.sqrt(LANES)

    def take(position, group, slot):
        routes[0, position] = group
        routes[1, position] = slot
        far = (group != me) | (slot < CAP)

        @pl.when(far)
        def _():
            for part in range(heads):
                index = part * groups + group
                where = row_tile(position * heads + part, rows)
                ks[where, :] = far_in[index, slot]
                vs[where, :] = far_in[index, CAP + slot]
                qs[where, :] = far_in[index, 2 * CAP + slot]

        @pl.when(jnp.logical_not(far))
        def _():
            extra = slot - CAP
            for turn in range(heads):
                where = row_tile(position * heads + (seq ^ turn), rows)
                ks[where, :] = own_ins[turn][extra]
                vs[where, :] = own_ins[turn][extras + extra]
                qs[where, :] = own_ins[turn][2 * extras + extra]

    each_block(plan, me, blocks, live, take)
    for turn in range(heads):
        for position in range(live):
            gs[row_tile(position * heads + (seq ^ turn), rows), :] = own_ins[turn][
                extras * 3 + position
            ]

    count = jnp.sum((seg[...] < CLIPS - 1).astype(jnp.float32), axis=1, keepdims=True).astype(
        jnp.int32
    )
    key_rows = ks[...]
    value_rows = vs[...]
    key_columns = key_rows.T
    key_index = lax.broadcasted_iota(jnp.int32, (reach, 1), 0)
    always = length - reach
    up_head = up[:, lane_tile(seq)]
    up_twice = jnp.concatenate([up_head, up_head], axis=0)
    for start in range(0, reach, QUERIES):
        count_here = min(QUERIES, reach - start)
        span = slice(start, start + count_here)
        scores = lax.dot_general(key_rows, qs[span, :], NT, preferred_element_type=jnp.float32)
        scores = jnp.concatenate(
            [
                scores[:always],
                jnp.where(key_index[always:] < count, scores[always:], -1e30),
            ],
            axis=0,
        )
        dprob = lax.dot_general(value_rows, gs[span, :], NT, preferred_element_type=jnp.float32)
        maximum = jnp.max(scores, axis=0, keepdims=True)
        exponent = jnp.exp2((scores - maximum) * (scaling * LOG2E))
        total = jnp.sum(exponent, axis=0, keepdims=True)
        delta = jnp.sum(exponent * dprob, axis=0, keepdims=True) / total
        dscore = (exponent * (dprob - delta)).astype(jnp.bfloat16)
        dquery = jnp.dot(key_columns, dscore, preferred_element_type=jnp.float32)
        query_index = lax.broadcasted_iota(jnp.int32, (1, count_here), 1) + start
        in_clip = query_index < count
        dquery = jnp.where(in_clip, dquery * (scaling / total), 0.0).astype(jnp.bfloat16)
        dqs[:, span] = dquery
        log_out[0, :, span] = jnp.where(in_clip, maximum * scaling + jnp.log(total), 0.0)
    log_out[0, :, reach:] = jnp.zeros((1, length - reach), jnp.float32)
    log_copy = pltpu.make_async_copy(log_out, log_hbm, sems.at[0])
    log_copy.start()
    dquery_all = dqs[...]
    parts[...] = lax.dot_general(
        dquery_all, up_twice, (((0,), (1,)), ((), ())), preferred_element_type=jnp.float32
    ).astype(jnp.bfloat16)

    def put(position):
        group, slot = routes[0, position], routes[1, position]
        far = (group != me) | (slot < CAP)

        @pl.when(far)
        def _():
            def store(lanes):
                for turn in range(heads):
                    chip, side = turn // CORES, turn % CORES
                    where = row_tile(position * heads + chip * CORES + (core ^ side), rows)
                    part_out[chip * groups + group, side, :, lanes] = parts[where, lanes]

            each_half(slot, store)

        @pl.when(jnp.logical_not(far))
        def _():
            pair = quotient(slot - CAP, 2)

            def store(lanes):
                for turn in range(heads):
                    where = row_tile(position * heads + (seq ^ turn), rows)
                    own_parts[turn // CORES][turn % CORES, pair, :, lanes] = parts[where, lanes]

            each_half(slot, store)

    for position in range(live):
        put(position)
    for chip in range(chips):
        for group in range(groups):
            part_out[chip * groups + group, CORES] = adapter[group]
    part_copy = pltpu.make_async_copy(part_out, part_hbm, sems.at[1])
    part_copy.start()
    log_copy.wait()
    part_copy.wait()


def head_sum_kernel(parts, *refs):
    extras, out = refs[:-1], refs[-1]
    pairs = extras[0].shape[1]
    peers = parts.shape[0]
    tiles = (out.shape[0] - peers) // CORES
    groups = tiles - pairs

    def total(terms):
        value = terms[0].astype(jnp.float32)
        for term in terms[1:]:
            value = value + term.astype(jnp.float32)
        return value.astype(jnp.bfloat16)

    for side in range(CORES):
        for group in range(groups):
            out[side * tiles + group] = total(
                [parts[peer, side] for peer in range(group, peers, groups)]
            )
        for pair in range(pairs):
            out[side * tiles + groups + pair] = total([extra[side, pair] for extra in extras])
    for peer in range(peers):
        out[CORES * tiles + peer] = parts[peer, CORES]


def product_kernel(dims, plan, feat, feat_other, mine, other, dquery, *rest):
    groups, blocks, heads, rows, live = dims
    own_ins = rest[:heads]
    out, up_out, sums, grads, ads = rest[heads:]
    extras = live - CAP
    me = lax.axis_index("dp")
    core = lax.axis_index("core")
    seq = seq_index()
    tiles = sums.shape[1]
    ads[...] = jnp.zeros_like(ads)

    def take(position, group, slot):
        far = (group != me) | (slot < CAP)

        @pl.when(far)
        def _():
            def store(lanes):
                for chip in range(heads // CORES):
                    tile = CORES * tiles + chip * groups + group
                    for source, which in ((mine, core), (other, 1 - core)):
                        where = row_tile(position * heads + chip * CORES + which, rows)
                        ads[where, lanes] = source[tile, :, lanes]

            each_half(slot, store)

        @pl.when(jnp.logical_not(far))
        def _():
            pair = extras * 3 + live + quotient(slot - CAP, 2)

            def store(lanes):
                for turn in range(heads):
                    where = row_tile(position * heads + (seq ^ turn), rows)
                    ads[where, lanes] = own_ins[turn][pair, :, lanes]

            each_half(slot, store)

    each_block(plan, me, blocks, live, take)
    up_part = jnp.dot(dquery[...], ads[...], preferred_element_type=jnp.float32)
    up_out[...] = (up_part + swap_halves(up_part)).T[: up_out.shape[0]].astype(jnp.bfloat16)
    for index in range(tiles):
        sums[0, index] = mine[index].astype(jnp.float32) + other[tiles + index].astype(jnp.float32)
        sums[1, index] = other[index].astype(jnp.float32) + mine[tiles + index].astype(jnp.float32)
    grads[...] = jnp.zeros_like(grads)

    def put(dest, slot, local):
        index = jnp.where(slot < CAP, dest, groups - 1 + quotient(slot, 2))
        for owner in range(CORES):
            grads[owner, local] = split(slot, sums[owner, index])

    each_hit(plan, me, groups, blocks, live, put)
    low = low_lanes(HALF // 2)
    columns = grads[...].reshape(CORES * blocks * rows, LANES).T[:HALF].astype(jnp.bfloat16)
    even = core == 0
    for chip in range(heads // CORES):
        features = jnp.concatenate([feat[:, core_columns(chip, core)], feat_other[chip]], axis=0)
        product = jnp.dot(columns, features, preferred_element_type=jnp.float32)
        first, second, third = (
            product[:, index * LANES : (index + 1) * LANES] for index in range(3)
        )
        shared = jnp.where(even, third, first)
        upper, lower = shared[: HALF // 2], shared[HALF // 2 :]
        out[chip, :HALF] = jnp.where(even, first, second).astype(jnp.bfloat16)
        out[chip, HALF : 2 * HALF] = jnp.where(even, second, third).astype(jnp.bfloat16)
        out[chip, 2 * HALF :] = jnp.where(
            even,
            jnp.where(low, upper, swap_halves(lower)),
            jnp.where(low, swap_halves(upper), lower),
        ).astype(jnp.bfloat16)


def join_kernel(parts, up_part, out):
    total = parts[0].astype(jnp.float32)
    for head in range(1, parts.shape[0]):
        total = total + parts[head].astype(jnp.float32)
    out[: total.shape[0]] = total.astype(jnp.bfloat16)
    out[total.shape[0] :] = up_part[...]


def total_kernel(grad_norm, *rest):
    groups = len(rest) - 3
    down_out, up_out, held = rest[groups:]
    me = lax.axis_index("dp")
    seq = seq_index()
    for turn in range(groups):
        held[me ^ turn] = rest[turn][...].astype(jnp.float32)
    total = held[0]
    for group in range(1, groups):
        total = total + held[group]
    total = total * grad_norm
    first, second = total[:HALF], total[HALF : 2 * HALF]
    shared = total[2 * HALF : 2 * HALF + HALF // 2]
    up_out[...] = total[2 * HALF + HALF // 2 :]
    swapped = swap_halves(shared)
    low_half = jnp.concatenate([shared, swapped], axis=0)
    high_half = jnp.concatenate([swapped, shared], axis=0)
    even = jnp.concatenate([first, second, low_half], axis=1)
    odd = pltpu.roll(jnp.concatenate([first, second, high_half], axis=1), HALF, 1)
    down = jnp.where(remainder(seq, 2) == 0, even, odd)
    down_out[...] = down[:, : down_out.shape[1]]


def call(kernel, outs, specs, scratch, flops, moved, *args, vmem_mib=32, out_specs=None):
    shapes = [jax.ShapeDtypeStruct(shape, dtype) for shape, dtype in outs]
    return pl.pallas_call(
        kernel,
        out_shape=shapes,
        in_specs=specs,
        out_specs=out_specs or [VMEM] * len(shapes),
        scratch_shapes=scratch,
        compiler_params=pltpu.CompilerParams(vmem_limit_bytes=vmem_mib << 20),
        cost_estimate=pl.CostEstimate(flops=flops, bytes_accessed=moved, transcendentals=0),
    )(*args)


def exchange(value, axis, size, turn):
    return lax.ppermute(value, axis, [(peer, peer ^ turn) for peer in range(size)])


def per_device_tiles(
    features,
    frozen_query_weight,
    source_keys,
    source_values,
    output_gradient,
    adapter_down_weight,
    adapter_up_weight,
    source_block_plan,
    segments,
):
    groups = lax.axis_size("dp")
    chips = lax.axis_size("chip")
    heads = chips * CORES
    _, blocks, rows, width = features.shape
    length = segments.shape[1]
    live = (length // 2 + length // 8) // LANES
    reach = live * LANES
    rank = adapter_up_weight.shape[0]
    extras = live - CAP
    pairs = (extras + 1) // 2
    dims = (groups, blocks, heads, rows, live)
    bf16 = jnp.bfloat16
    f32 = jnp.float32
    peers = groups * heads
    everyone = SEQ + ("dp",)
    flat = features[0].reshape(blocks * rows, width)
    far_shape = (peers, CAP * 3, rows, LANES)
    own_shape = (extras * 3 + live + pairs, rows, LANES)
    rows_shape = (blocks, rows, heads * LANES)

    far_send, queries, adapter = call(
        functools.partial(pack_far_kernel, dims),
        [(far_shape, bf16), (rows_shape, bf16), ((blocks, rows, LANES), bf16)],
        [ANY] * 7,
        [
            pltpu.SMEM((groups, blocks), jnp.int32),
            pltpu.SMEM((4, blocks), jnp.int32),
            pltpu.VMEM((blocks * rows, width), bf16),
            pltpu.VMEM(rows_shape, bf16),
            pltpu.VMEM(rows_shape, bf16),
            pltpu.VMEM(rows_shape, bf16),
            pltpu.VMEM((rank, width), bf16),
            pltpu.VMEM((rank, heads * LANES), bf16),
            pltpu.VMEM(far_shape, bf16),
            pltpu.VMEM(rows_shape, bf16),
            pltpu.VMEM((blocks, rows, LANES), bf16),
            pltpu.SemaphoreType.DMA((7,)),
            pltpu.SemaphoreType.DMA((4,)),
        ],
        60_000_000,
        4_000_000,
        source_block_plan,
        flat,
        frozen_query_weight[0],
        source_keys[0],
        source_values[0],
        adapter_down_weight.T,
        adapter_up_weight,
        vmem_mib=60,
        out_specs=[ANY] * 3,
    )
    own_send = call(
        functools.partial(pack_own_kernel, dims),
        [(own_shape, bf16)] * heads
        + [((chips, blocks * rows, 3 * LANES), bf16), ((groups, rows, LANES), bf16)],
        [SMEM] + [VMEM] * 6,
        [],
        0,
        1_600_000,
        source_block_plan,
        source_keys[0],
        source_values[0],
        output_gradient[0],
        queries,
        adapter,
        flat,
    )
    feat_other = exchange(own_send[heads], "core", CORES, 1)
    own = [exchange(own_send[turn], SEQ, heads, turn) for turn in range(heads - 1, 0, -1)]
    own = [own_send[0]] + own[::-1]
    far = lax.all_to_all(far_send, everyone, 0, 0, tiled=True)
    attended = call(
        functools.partial(attend_kernel, dims),
        [((chips * groups, CORES + 1, rows, LANES), bf16)]
        + [((CORES, pairs, rows, LANES), bf16)] * chips
        + [((LANES, reach), bf16), ((1, 1, length), f32)],
        [SMEM] + [VMEM] * (4 + heads) + [ANY],
        [
            pltpu.VMEM((chips * groups, CORES + 1, rows, LANES), bf16),
            pltpu.VMEM((1, 1, length), f32),
            pltpu.SMEM((2, live), jnp.int32),
            pltpu.SemaphoreType.DMA((2,)),
        ]
        + [pltpu.VMEM((reach, LANES), bf16)] * 5,
        600_000_000,
        3_000_000,
        source_block_plan,
        segments,
        adapter_up_weight,
        own_send[heads + 1],
        far,
        *own,
        feat_other,
        out_specs=[ANY] + [VMEM] * (chips + 1) + [ANY],
    )
    own_parts = [
        exchange(attended[1 + turn], "chip", chips, turn) for turn in range(chips - 1, 0, -1)
    ]
    part = lax.all_to_all(attended[0], ("chip", "dp"), 0, 0, tiled=True)
    dquery, log_norm = attended[1 + chips :]
    tiles = groups + pairs
    (mine,) = call(
        head_sum_kernel,
        [((CORES * tiles + chips * groups, rows, LANES), bf16)],
        [VMEM] * (1 + chips),
        [],
        0,
        300_000,
        part,
        *own_parts,
        attended[1],
    )
    shares, up_part = call(
        functools.partial(product_kernel, dims),
        [((chips, HALF * 5 // 2, LANES), bf16), ((rank, LANES), bf16)],
        [SMEM] + [VMEM] * (5 + heads),
        [
            pltpu.VMEM((CORES, tiles, rows, LANES), f32),
            pltpu.VMEM((CORES, blocks, rows, LANES), f32),
            pltpu.VMEM((reach, LANES), bf16),
        ],
        60_000_000,
        2_000_000,
        source_block_plan,
        flat,
        feat_other,
        mine,
        exchange(mine, "core", CORES, 1),
        dquery,
        *own,
    )
    shares = lax.all_to_all(shares, "chip", 0, 0, tiled=True)
    (joined,) = call(
        join_kernel,
        [((HALF * 5 // 2 + rank, LANES), bf16)],
        [VMEM] * 2,
        [],
        0,
        600_000,
        shares,
        up_part,
    )
    sums = [joined] + [exchange(joined, "dp", groups, turn) for turn in range(1, groups)]
    down, up = call(
        functools.partial(total_kernel, 4.0 / math.sqrt(groups * length)),
        [((rank, width // heads), f32), ((rank, LANES), f32)],
        [VMEM] * groups,
        [pltpu.VMEM((groups,) + joined.shape, f32)],
        0,
        400_000,
        *sums,
    )
    return (down.T, up, log_norm)


def power_of_two(size):
    return size > 1 and size & (size - 1) == 0


def fits_tiles(mesh, features, adapter_up_weight):
    groups, heads = mesh.shape["dp"], mesh.shape["seq"]
    rows = features.shape[2] // heads
    return (
        rows % 16 == 0
        and features.shape[2] == LANES
        and features.shape[3] * 2 == heads * 5 * LANES
        and power_of_two(heads)
        and power_of_two(groups)
        and power_of_two(features.shape[1])
        and adapter_up_weight.shape == (HALF, heads * LANES)
    )


def split_mesh(mesh):
    groups, heads = mesh.shape["dp"], mesh.shape["seq"]
    devices = np.asarray(mesh.devices).reshape(groups, heads // CORES, CORES)
    return Mesh(devices, ("dp",) + SEQ)


def tiles_solution(mesh):
    row_spec = P("dp", None, SEQ, None)
    return jax.shard_map(
        per_device_tiles,
        mesh=split_mesh(mesh),
        in_specs=(row_spec,) * 5 + (P(), P(), P(), P("dp", None)),
        out_specs=(P(SEQ, None), P(None, SEQ), P("dp", SEQ, None)),
        check_vma=False,
    )


def attend_head(query, key_rows, value_rows, cotangent, segment, clip_count, reach_rows):
    length = query.shape[0]
    width = query.shape[1]
    piece_count = 8
    piece_rows = reach_rows // piece_count
    scaling = 1.0 / math.sqrt(width)
    query_padded = jnp.pad(query, ((0, reach_rows), (0, 0)))
    grad_padded = jnp.pad(cotangent, ((0, reach_rows), (0, 0)))
    keys_padded = jnp.pad(key_rows, ((0, reach_rows), (0, 0)))
    values_padded = jnp.pad(value_rows, ((0, reach_rows), (0, 0)))
    segment_padded = jnp.pad(segment, (0, reach_rows), constant_values=-1)
    clip_ids = jnp.arange(clip_count, dtype=jnp.int32)
    starts = jnp.sum((segment[None, :] < clip_ids[:, None]).astype(jnp.int32), axis=1)

    def piece_pass(piece_index):
        clip_slice = piece_index // piece_count
        start = lax.dynamic_index_in_dim(starts, clip_slice, 0, keepdims=False)
        query_start = start + piece_index % piece_count * piece_rows
        query_tile = lax.dynamic_slice_in_dim(query_padded, query_start, piece_rows, 0)
        grad_tile = lax.dynamic_slice_in_dim(grad_padded, query_start, piece_rows, 0)
        seg_tile = lax.dynamic_slice_in_dim(segment_padded, query_start, piece_rows, 0)
        key_tile = lax.dynamic_slice_in_dim(keys_padded, start, reach_rows, 0)
        value_tile = lax.dynamic_slice_in_dim(values_padded, start, reach_rows, 0)
        seg_cols = lax.dynamic_slice_in_dim(segment_padded, start, reach_rows, 0)
        in_clip = seg_tile == clip_slice
        allowed = in_clip[:, None] & (seg_cols == clip_slice)[None, :]
        scores = (
            lax.dot_general(
                query_tile, key_tile, (((1,), (1,)), ((), ())), preferred_element_type=jnp.float32
            )
            * scaling
        )
        scores = jnp.where(allowed, scores, -1e30)
        maximum = jnp.max(scores, axis=1, keepdims=True)
        exponent = jnp.where(allowed, jnp.exp(scores - maximum), 0.0)
        totals = jnp.where(in_clip[:, None], jnp.sum(exponent, axis=1, keepdims=True), 1.0)
        log_norm = jnp.where(in_clip, maximum[:, 0] + jnp.log(totals[:, 0]), 0.0)
        probs = exponent / totals
        weights = probs.astype(jnp.bfloat16)
        attended = jnp.dot(weights, value_tile, preferred_element_type=jnp.float32)
        delta = jnp.sum(grad_tile.astype(jnp.float32) * attended, axis=1, keepdims=True)
        dprob = lax.dot_general(
            grad_tile, value_tile, (((1,), (1,)), ((), ())), preferred_element_type=jnp.float32
        )
        dscore = (probs * (dprob - delta)).astype(jnp.bfloat16)
        query_gradient = (
            jnp.dot(dscore, key_tile, preferred_element_type=jnp.float32) * scaling
        ).astype(jnp.bfloat16)
        query_gradient = jnp.where(in_clip[:, None], query_gradient, jnp.zeros((), jnp.bfloat16))
        return (query_gradient, log_norm, query_start)

    total_pieces = piece_count * (clip_count - 1)
    dquery_pieces, log_pieces, piece_starts = lax.map(
        piece_pass, jnp.arange(total_pieces, dtype=jnp.int32)
    )

    def place(index, carry):
        grad_total, log_total = carry
        where_at = lax.dynamic_index_in_dim(piece_starts, index, 0, keepdims=False)
        grad_piece = lax.dynamic_index_in_dim(dquery_pieces, index, 0, keepdims=False)
        log_piece = lax.dynamic_index_in_dim(log_pieces, index, 0, keepdims=False)
        grad_old = lax.dynamic_slice_in_dim(grad_total, where_at, piece_rows, 0)
        log_old = lax.dynamic_slice_in_dim(log_total, where_at, piece_rows, 0)
        grad_total = lax.dynamic_update_slice_in_dim(grad_total, grad_old + grad_piece, where_at, 0)
        log_total = lax.dynamic_update_slice_in_dim(log_total, log_old + log_piece, where_at, 0)
        return (grad_total, log_total)

    grad_init = jnp.zeros((length + reach_rows, width), jnp.bfloat16)
    log_init = jnp.zeros((length + reach_rows,), jnp.float32)
    grad_total, log_total = lax.fori_loop(0, total_pieces, place, (grad_init, log_init))
    return (grad_total[:length], log_total[:length])


def routing_tables(source_block_plan, group_index, cap_slots):
    group_count, block_count = source_block_plan.shape
    source_group = source_block_plan // block_count
    source_local = source_block_plan % block_count
    dest_groups = jnp.arange(group_count, dtype=jnp.int32)[:, None]
    outgoing = (source_group == group_index) & (dest_groups != group_index)
    out_rank = jnp.cumsum(outgoing.astype(jnp.int32), axis=1) - 1
    slot_ids = jnp.arange(cap_slots, dtype=jnp.int32)
    chosen = outgoing[:, :, None] & (out_rank[:, :, None] == slot_ids[None, None, :])
    send_index = jnp.sum(jnp.where(chosen, source_local[:, :, None], 0), axis=1)
    send_valid = jnp.any(chosen, axis=1)
    own_group = lax.dynamic_index_in_dim(source_group, group_index, 0, keepdims=False)
    own_local = lax.dynamic_index_in_dim(source_local, group_index, 0, keepdims=False)
    incoming = own_group != group_index
    positions = jnp.arange(block_count, dtype=jnp.int32)
    earlier = (own_group[None, :] == own_group[:, None]) & (positions[None, :] < positions[:, None])
    in_rank = jnp.sum(earlier.astype(jnp.int32), axis=1)
    return (send_index, send_valid, incoming, own_group, in_rank, own_local)


def pack_blocks(local, send_index, send_valid):
    picked = jnp.take(local, send_index, axis=0)
    return jnp.where(send_valid[:, :, None, None], picked, jnp.zeros((), local.dtype))


def unpack_blocks(received, local, tables, cap_slots):
    incoming, own_group, in_rank, own_local = tables
    flat = received.reshape((-1,) + received.shape[2:])
    slot_index = jnp.where(incoming, own_group * cap_slots + in_rank, 0)
    remote = jnp.take(flat, slot_index, axis=0)
    staying = jnp.take(local, own_local, axis=0)
    return jnp.where(incoming[:, None, None], remote, staying)


def per_device(
    features,
    frozen_query_weight,
    source_keys,
    source_values,
    output_gradient,
    adapter_down_weight,
    adapter_up_weight,
    source_block_plan,
    segments,
):
    group_count = lax.axis_size("dp")
    group_index = lax.axis_index("dp")
    block_count = features.shape[1]
    feat_local = features[0]
    base_local = frozen_query_weight[0]
    keys_local = source_keys[0]
    values_local = source_values[0]
    send_index, send_valid, incoming, own_group, in_rank, own_local = routing_tables(
        source_block_plan, group_index, CAP
    )
    tables = (incoming, own_group, in_rank, own_local)
    contract_final_axis = (((2,), (0,)), ((), ()))
    shuffled = (
        lax.all_to_all(
            pack_blocks(feat_local, send_index, send_valid),
            "dp",
            split_axis=0,
            concat_axis=0,
            tiled=True,
        ),
        lax.all_to_all(
            pack_blocks(base_local, send_index, send_valid),
            "dp",
            split_axis=0,
            concat_axis=0,
            tiled=True,
        ),
        lax.all_to_all(
            pack_blocks(keys_local, send_index, send_valid),
            "dp",
            split_axis=0,
            concat_axis=0,
            tiled=True,
        ),
        lax.all_to_all(
            pack_blocks(values_local, send_index, send_valid),
            "dp",
            split_axis=0,
            concat_axis=0,
            tiled=True,
        ),
    )
    feature_dest = unpack_blocks(shuffled[0], feat_local, tables, CAP)
    base_query_dest = unpack_blocks(shuffled[1], base_local, tables, CAP)
    keys_dest = unpack_blocks(shuffled[2], keys_local, tables, CAP)
    values_dest = unpack_blocks(shuffled[3], values_local, tables, CAP)
    adapter_params = lax.dot_general(
        feature_dest, adapter_down_weight, contract_final_axis, preferred_element_type=jnp.float32
    ).astype(jnp.bfloat16)
    query_rows = (
        base_query_dest.astype(jnp.float32)
        + lax.dot_general(
            adapter_params,
            adapter_up_weight,
            contract_final_axis,
            preferred_element_type=jnp.float32,
        )
    ).astype(jnp.bfloat16)
    head_query, head_keys, head_values, head_grads = (
        lax.all_to_all(query_rows, "seq", split_axis=2, concat_axis=1, tiled=True),
        lax.all_to_all(keys_dest, "seq", split_axis=2, concat_axis=1, tiled=True),
        lax.all_to_all(values_dest, "seq", split_axis=2, concat_axis=1, tiled=True),
        lax.all_to_all(output_gradient[0], "seq", split_axis=2, concat_axis=1, tiled=True),
    )
    length = head_query.shape[0] * head_query.shape[1]
    reach_rows = length // 2 + length // 8
    head_width = head_query.shape[2]
    segment = segments[0]
    head_query = head_query.reshape(length, head_width)
    head_keys = head_keys.reshape(length, head_width)
    head_values = head_values.reshape(length, head_width)
    head_grads = head_grads.reshape(length, head_width)
    dquery_head, log_head = attend_head(
        head_query, head_keys, head_values, head_grads, segment, CLIPS, reach_rows
    )
    norm_pieces = [log_head]
    log_norm = jnp.stack(norm_pieces, axis=0)
    query_gradient = lax.all_to_all(
        dquery_head.reshape(block_count, length // block_count, head_width),
        "seq",
        split_axis=1,
        concat_axis=2,
        tiled=True,
    )
    adapter_gradient = lax.dot_general(
        query_gradient,
        adapter_up_weight,
        (((2,), (1,)), ((), ())),
        preferred_element_type=jnp.float32,
    ).astype(jnp.bfloat16)
    contract_tokens = (((0, 1), (0, 1)), ((), ()))
    down_part = lax.dot_general(
        feature_dest, adapter_gradient, contract_tokens, preferred_element_type=jnp.float32
    )
    up_part = lax.dot_general(
        adapter_params, query_gradient, contract_tokens, preferred_element_type=jnp.float32
    )
    down_share, up_share = (
        lax.psum_scatter(down_part, "seq", scatter_dimension=0, tiled=True),
        lax.psum_scatter(up_part, "seq", scatter_dimension=1, tiled=True),
    )
    down_total, up_total = lax.psum((down_share, up_share), "dp")
    grad_norm = 4.0 / math.sqrt(group_count * length)
    return (down_total * grad_norm, up_total * grad_norm, log_norm[None])


def solution(mesh):
    in_specs = (
        P("dp", None, "seq", None),
        P("dp", None, "seq", None),
        P("dp", None, "seq", None),
        P("dp", None, "seq", None),
        P("dp", None, "seq", None),
        P(),
        P(),
        P(),
        P("dp", None),
    )
    out_specs = (P("seq", None), P(None, "seq"), P("dp", "seq", None))

    plain = jax.shard_map(
        per_device, mesh=mesh, in_specs=in_specs, out_specs=out_specs, check_vma=False
    )

    def whole(features, *rest):
        fits = fits_tiles(mesh, features, rest[5])
        return (tiles_solution(mesh) if fits else plain)(features, *rest)

    return whole
```

```python
import functools
import math

import jax
import jax.numpy as jnp
import numpy as np
from jax import lax
from jax.experimental import pallas as pl
from jax.experimental.pallas import tpu as pltpu
from jax.sharding import Mesh
from jax.sharding import PartitionSpec as P

CAP = 2
CLIPS = 2
LANES = 128
HALF = 64
CORES = 2
SEQ = ("chip", "core")
QUERIES = 640
LOG2E = math.log2(math.e)
VMEM = pl.BlockSpec(memory_space=pltpu.VMEM)
SMEM = pl.BlockSpec(memory_space=pltpu.SMEM)
ANY = pl.BlockSpec(memory_space=pl.ANY)
NT = (((1,), (1,)), ((), ()))


def low_lanes(rows):
    return lax.broadcasted_iota(jnp.int32, (rows, LANES), 1) < HALF


def swap_halves(tile):
    return pltpu.roll(tile, HALF, 1)


def lane_tile(index):
    return pl.ds(pl.multiple_of(index * LANES, LANES), LANES)


def row_tile(index, rows):
    return pl.ds(pl.multiple_of(index * rows, rows), rows)


def quotient(value, size):
    return lax.shift_right_logical(value, size.bit_length() - 1)


def remainder(value, size):
    return value & (size - 1)


def seq_index():
    return lax.axis_index("chip") * CORES + lax.axis_index("core")


def each_hit(plan, me, groups, blocks, live, put):
    def over_dest(dest, _):
        def over_position(position, slot):
            source = plan[dest, position]
            hit = quotient(source, blocks) == me

            @pl.when(hit)
            def _():
                put(dest, slot, remainder(source, blocks))

            return slot + hit.astype(jnp.int32)

        lax.fori_loop(0, live, over_position, jnp.int32(0), unroll=True)
        return 0

    lax.fori_loop(0, groups, over_dest, 0)


def each_block(plan, me, blocks, live, take):
    groups_of = [quotient(plan[me, position], blocks) for position in range(live)]
    for position, group in enumerate(groups_of):
        slot = jnp.int32(0)
        for earlier in groups_of[:position]:
            slot = slot + (earlier == group).astype(jnp.int32)
        take(position, group, slot)


def each_half(slot, store):
    @pl.when(remainder(slot, 2) == 0)
    def _():
        store(slice(0, HALF))

    @pl.when(remainder(slot, 2) == 1)
    def _():
        store(slice(HALF, LANES))


def split(slot, pair):
    pair = pair.astype(jnp.float32)
    return jnp.where(remainder(slot, 2) == 0, pair, swap_halves(pair))


def pack_far_kernel(dims, plan_hbm, feat_hbm, base_hbm, keys_hbm, vals_hbm, down_hbm, up_hbm, *rest):
    groups, blocks, heads, rows, live = dims
    far_hbm, queries_hbm, adapter_hbm = rest[:3]
    plan, routes, feat, base, keys, vals, down, up, far_out, qbuf, abuf, sems, out_sems = rest[3:]
    me = lax.axis_index("dp")
    copies = [
        pltpu.make_async_copy(source, target, sems.at[index])
        for index, (source, target) in enumerate(
            (
                (plan_hbm, plan),
                (keys_hbm, keys),
                (vals_hbm, vals),
                (feat_hbm, feat),
                (down_hbm, down),
                (base_hbm, base),
                (up_hbm, up),
            )
        )
    ]
    for copy in copies:
        copy.start()

    def put_early(dest, slot, local):
        @pl.when(slot < CAP)
        def _():
            index = routes[0, 0]
            routes[0, 0] = index + 1
            for row, value in enumerate((dest, slot, local)):
                routes[row + 1, index] = value
            for head in range(heads):
                columns = slice(head * LANES, (head + 1) * LANES)
                far_out[head * groups + dest, slot] = keys[local, :, columns]
                far_out[head * groups + dest, CAP + slot] = vals[local, :, columns]

    def send(first, count, index):
        tiles = pl.ds(first, count)
        copy = pltpu.make_async_copy(far_out.at[:, tiles], far_hbm.at[:, tiles], out_sems.at[index])
        copy.start()
        return copy

    for copy in copies[:3]:
        copy.wait()
    routes[0, 0] = 0
    each_hit(plan, me, groups, blocks, live, put_early)
    early = send(0, 2 * CAP, 0)
    for copy in copies[3:5]:
        copy.wait()
    narrow = lax.dot_general(feat[...], down[...], NT, preferred_element_type=jnp.float32)
    adapter = narrow.astype(jnp.bfloat16)
    for copy in copies[5:]:
        copy.wait()
    lift = jnp.dot(adapter, up[...], preferred_element_type=jnp.float32)
    abuf[...] = jnp.concatenate([narrow, narrow], axis=1).astype(jnp.bfloat16).reshape(abuf.shape)
    qbuf[...] = (base[...].astype(jnp.float32) + lift.reshape(base.shape)).astype(jnp.bfloat16)

    rest_out = [
        pltpu.make_async_copy(qbuf, queries_hbm, out_sems.at[2]),
        pltpu.make_async_copy(abuf, adapter_hbm, out_sems.at[3]),
    ]
    for copy in rest_out:
        copy.start()

    def put_late(index, _):
        dest, slot, local = routes[1, index], routes[2, index], routes[3, index]

        for head in range(heads):
            columns = slice(head * LANES, (head + 1) * LANES)
            far_out[head * groups + dest, 2 * CAP + slot] = qbuf[local, :, columns]
        return 0

    lax.fori_loop(0, routes[0, 0], put_late, 0)
    late = send(2 * CAP, CAP, 1)
    for copy in [early, late] + rest_out:
        copy.wait()


def core_columns(chip, core):
    return pl.ds(pl.multiple_of((chip * 5 + core * 2) * LANES, LANES), 3 * LANES)


def pack_own_kernel(dims, plan, keys, vals, grad, queries, adapter, feat, *outs):
    groups, blocks, heads, rows, live = dims
    own_outs, feat_out, adapter_out = outs[:heads], outs[heads], outs[heads + 1]
    for chip in range(heads // CORES):
        feat_out[chip] = feat[:, core_columns(chip, 1 - lax.axis_index("core"))]
    extras = live - CAP
    me = lax.axis_index("dp")
    seq = seq_index()
    sources = (keys, vals, queries)

    def put(dest, slot, local):
        @pl.when(slot < CAP)
        def _():
            def store(lanes):
                adapter_out[dest, :, lanes] = adapter[local, :, lanes]

            each_half(slot, store)

        @pl.when(slot >= CAP)
        def _():
            extra = slot - CAP
            where = extras * 3 + live + quotient(extra, 2)
            for turn in range(heads):
                columns = lane_tile(seq ^ turn)
                for index, source in enumerate(sources):
                    own_outs[turn][index * extras + extra] = source[local, :, columns]

            def store(lanes):
                for turn in range(heads):
                    own_outs[turn][where, :, lanes] = adapter[local, :, lanes]

            each_half(slot, store)

    each_hit(plan, me, groups, blocks, live, put)
    for turn in range(heads):
        columns = lane_tile(seq ^ turn)
        for position in range(live):
            own_outs[turn][extras * 3 + position] = grad[position, :, columns]


def attend_kernel(dims, plan, seg, up, adapter, far_in, *rest):
    groups, blocks, heads, rows, live = dims
    chips = heads // CORES
    core = lax.axis_index("core")
    own_ins = rest[:heads]
    part_hbm = rest[heads + 1]
    own_parts = rest[heads + 2 : heads + 2 + chips]
    dqs, log_hbm, part_out, log_out, routes, sems, qs, ks, vs, gs, parts = rest[
        heads + 2 + chips :
    ]
    extras = live - CAP
    me = lax.axis_index("dp")
    seq = seq_index()
    length = seg.shape[1]
    reach = live * LANES
    scaling = 1.0 / math.sqrt(LANES)

    def take(position, group, slot):
        routes[0, position] = group
        routes[1, position] = slot
        far = (group != me) | (slot < CAP)

        @pl.when(far)
        def _():
            for part in range(heads):
                index = part * groups + group
                where = row_tile(position * heads + part, rows)
                ks[where, :] = far_in[index, slot]
                vs[where, :] = far_in[index, CAP + slot]
                qs[where, :] = far_in[index, 2 * CAP + slot]

        @pl.when(jnp.logical_not(far))
        def _():
            extra = slot - CAP
            for turn in range(heads):
                where = row_tile(position * heads + (seq ^ turn), rows)
                ks[where, :] = own_ins[turn][extra]
                vs[where, :] = own_ins[turn][extras + extra]
                qs[where, :] = own_ins[turn][2 * extras + extra]

    each_block(plan, me, blocks, live, take)
    for turn in range(heads):
        for position in range(live):
            gs[row_tile(position * heads + (seq ^ turn), rows), :] = own_ins[turn][
                extras * 3 + position
            ]

    count = jnp.sum((seg[...] < CLIPS - 1).astype(jnp.float32), axis=1, keepdims=True).astype(
        jnp.int32
    )
    key_rows = ks[...]
    value_rows = vs[...]
    key_columns = key_rows.T
    key_index = lax.broadcasted_iota(jnp.int32, (reach, 1), 0)
    always = length - reach
    up_head = up[:, lane_tile(seq)]
    up_twice = jnp.concatenate([up_head, up_head], axis=0)
    for start in range(0, reach, QUERIES):
        count_here = min(QUERIES, reach - start)
        span = slice(start, start + count_here)
        scores = lax.dot_general(key_rows, qs[span, :], NT, preferred_element_type=jnp.float32)
        scores = jnp.concatenate(
            [
                scores[:always],
                jnp.where(key_index[always:] < count, scores[always:], -1e30),
            ],
            axis=0,
        )
        dprob = lax.dot_general(value_rows, gs[span, :], NT, preferred_element_type=jnp.float32)
        maximum = jnp.max(scores, axis=0, keepdims=True)
        exponent = jnp.exp2((scores - maximum) * (scaling * LOG2E))
        total = jnp.sum(exponent, axis=0, keepdims=True)
        delta = jnp.sum(exponent * dprob, axis=0, keepdims=True) / total
        dscore = (exponent * (dprob - delta)).astype(jnp.bfloat16)
        dquery = jnp.dot(key_columns, dscore, preferred_element_type=jnp.float32)
        query_index = lax.broadcasted_iota(jnp.int32, (1, count_here), 1) + start
        in_clip = query_index < count
        dquery = jnp.where(in_clip, dquery * (scaling / total), 0.0).astype(jnp.bfloat16)
        dqs[:, span] = dquery
        log_out[0, :, span] = jnp.where(in_clip, maximum * scaling + jnp.log(total), 0.0)
    log_out[0, :, reach:] = jnp.zeros((1, length - reach), jnp.float32)
    log_copy = pltpu.make_async_copy(log_out, log_hbm, sems.at[0])
    log_copy.start()
    dquery_all = dqs[...]
    parts[...] = lax.dot_general(
        dquery_all, up_twice, (((0,), (1,)), ((), ())), preferred_element_type=jnp.float32
    ).astype(jnp.bfloat16)

    def put(position):
        group, slot = routes[0, position], routes[1, position]
        far = (group != me) | (slot < CAP)

        @pl.when(far)
        def _():
            def store(lanes):
                for turn in range(heads):
                    chip, side = turn // CORES, turn % CORES
                    where = row_tile(position * heads + chip * CORES + (core ^ side), rows)
                    part_out[chip * groups + group, side, :, lanes] = parts[where, lanes]

            each_half(slot, store)

        @pl.when(jnp.logical_not(far))
        def _():
            pair = quotient(slot - CAP, 2)

            def store(lanes):
                for turn in range(heads):
                    where = row_tile(position * heads + (seq ^ turn), rows)
                    own_parts[turn // CORES][turn % CORES, pair, :, lanes] = parts[where, lanes]

            each_half(slot, store)

    for position in range(live):
        put(position)
    for chip in range(chips):
        for group in range(groups):
            part_out[chip * groups + group, CORES] = adapter[group]
    part_copy = pltpu.make_async_copy(part_out, part_hbm, sems.at[1])
    part_copy.start()
    log_copy.wait()
    part_copy.wait()


def head_sum_kernel(parts, *refs):
    extras, out = refs[:-1], refs[-1]
    pairs = extras[0].shape[1]
    peers = parts.shape[0]
    tiles = (out.shape[0] - peers) // CORES
    groups = tiles - pairs

    def total(terms):
        value = terms[0].astype(jnp.float32)
        for term in terms[1:]:
            value = value + term.astype(jnp.float32)
        return value.astype(jnp.bfloat16)

    for side in range(CORES):
        for group in range(groups):
            out[side * tiles + group] = total(
                [parts[peer, side] for peer in range(group, peers, groups)]
            )
        for pair in range(pairs):
            out[side * tiles + groups + pair] = total([extra[side, pair] for extra in extras])
    for peer in range(peers):
        out[CORES * tiles + peer] = parts[peer, CORES]


def product_kernel(dims, plan, feat, feat_other, mine, other, dquery, *rest):
    groups, blocks, heads, rows, live = dims
    own_ins = rest[:heads]
    out, up_out, sums, grads, ads = rest[heads:]
    extras = live - CAP
    me = lax.axis_index("dp")
    core = lax.axis_index("core")
    seq = seq_index()
    tiles = sums.shape[1]
    ads[...] = jnp.zeros_like(ads)

    def take(position, group, slot):
        far = (group != me) | (slot < CAP)

        @pl.when(far)
        def _():
            def store(lanes):
                for chip in range(heads // CORES):
                    tile = CORES * tiles + chip * groups + group
                    for source, which in ((mine, core), (other, 1 - core)):
                        where = row_tile(position * heads + chip * CORES + which, rows)
                        ads[where, lanes] = source[tile, :, lanes]

            each_half(slot, store)

        @pl.when(jnp.logical_not(far))
        def _():
            pair = extras * 3 + live + quotient(slot - CAP, 2)

            def store(lanes):
                for turn in range(heads):
                    where = row_tile(position * heads + (seq ^ turn), rows)
                    ads[where, lanes] = own_ins[turn][pair, :, lanes]

            each_half(slot, store)

    each_block(plan, me, blocks, live, take)
    up_part = jnp.dot(dquery[...], ads[...], preferred_element_type=jnp.float32)
    up_out[...] = (up_part + swap_halves(up_part)).T[: up_out.shape[0]].astype(jnp.bfloat16)
    for index in range(tiles):
        sums[0, index] = mine[index].astype(jnp.float32) + other[tiles + index].astype(jnp.float32)
        sums[1, index] = other[index].astype(jnp.float32) + mine[tiles + index].astype(jnp.float32)
    grads[...] = jnp.zeros_like(grads)

    def put(dest, slot, local):
        index = jnp.where(slot < CAP, dest, groups - 1 + quotient(slot, 2))
        for owner in range(CORES):
            grads[owner, local] = split(slot, sums[owner, index])

    each_hit(plan, me, groups, blocks, live, put)
    low = low_lanes(HALF // 2)
    columns = grads[...].reshape(CORES * blocks * rows, LANES).T[:HALF].astype(jnp.bfloat16)
    even = core == 0
    for chip in range(heads // CORES):
        features = jnp.concatenate([feat[:, core_columns(chip, core)], feat_other[chip]], axis=0)
        product = jnp.dot(columns, features, preferred_element_type=jnp.float32)
        first, second, third = (
            product[:, index * LANES : (index + 1) * LANES] for index in range(3)
        )
        shared = jnp.where(even, third, first)
        upper, lower = shared[: HALF // 2], shared[HALF // 2 :]
        out[chip, :HALF] = jnp.where(even, first, second).astype(jnp.bfloat16)
        out[chip, HALF : 2 * HALF] = jnp.where(even, second, third).astype(jnp.bfloat16)
        out[chip, 2 * HALF :] = jnp.where(
            even,
            jnp.where(low, upper, swap_halves(lower)),
            jnp.where(low, swap_halves(upper), lower),
        ).astype(jnp.bfloat16)


def join_kernel(parts, up_part, out):
    total = parts[0].astype(jnp.float32)
    for head in range(1, parts.shape[0]):
        total = total + parts[head].astype(jnp.float32)
    out[: total.shape[0]] = total.astype(jnp.bfloat16)
    out[total.shape[0] :] = up_part[...]


def total_kernel(grad_norm, *rest):
    groups = len(rest) - 3
    down_out, up_out, held = rest[groups:]
    me = lax.axis_index("dp")
    seq = seq_index()
    for turn in range(groups):
        held[me ^ turn] = rest[turn][...].astype(jnp.float32)
    total = held[0]
    for group in range(1, groups):
        total = total + held[group]
    total = total * grad_norm
    first, second = total[:HALF], total[HALF : 2 * HALF]
    shared = total[2 * HALF : 2 * HALF + HALF // 2]
    up_out[...] = total[2 * HALF + HALF // 2 :]
    swapped = swap_halves(shared)
    low_half = jnp.concatenate([shared, swapped], axis=0)
    high_half = jnp.concatenate([swapped, shared], axis=0)
    even = jnp.concatenate([first, second, low_half], axis=1)
    odd = pltpu.roll(jnp.concatenate([first, second, high_half], axis=1), HALF, 1)
    down = jnp.where(remainder(seq, 2) == 0, even, odd)
    down_out[...] = down[:, : down_out.shape[1]]


def call(kernel, outs, specs, scratch, flops, moved, *args, vmem_mib=32, out_specs=None):
    shapes = [jax.ShapeDtypeStruct(shape, dtype) for shape, dtype in outs]
    return pl.pallas_call(
        kernel,
        out_shape=shapes,
        in_specs=specs,
        out_specs=out_specs or [VMEM] * len(shapes),
        scratch_shapes=scratch,
        compiler_params=pltpu.CompilerParams(vmem_limit_bytes=vmem_mib << 20),
        cost_estimate=pl.CostEstimate(flops=flops, bytes_accessed=moved, transcendentals=0),
    )(*args)


def exchange(value, axis, size, turn):
    return lax.ppermute(value, axis, [(peer, peer ^ turn) for peer in range(size)])


def per_device_tiles(
    features,
    frozen_query_weight,
    source_keys,
    source_values,
    output_gradient,
    adapter_down_weight,
    adapter_up_weight,
    source_block_plan,
    segments,
):
    groups = lax.axis_size("dp")
    chips = lax.axis_size("chip")
    heads = chips * CORES
    _, blocks, rows, width = features.shape
    length = segments.shape[1]
    live = (length // 2 + length // 8) // LANES
    reach = live * LANES
    rank = adapter_up_weight.shape[0]
    extras = live - CAP
    pairs = (extras + 1) // 2
    dims = (groups, blocks, heads, rows, live)
    bf16 = jnp.bfloat16
    f32 = jnp.float32
    peers = groups * heads
    everyone = SEQ + ("dp",)
    flat = features[0].reshape(blocks * rows, width)
    far_shape = (peers, CAP * 3, rows, LANES)
    own_shape = (extras * 3 + live + pairs, rows, LANES)
    rows_shape = (blocks, rows, heads * LANES)

    far_send, queries, adapter = call(
        functools.partial(pack_far_kernel, dims),
        [(far_shape, bf16), (rows_shape, bf16), ((blocks, rows, LANES), bf16)],
        [ANY] * 7,
        [
            pltpu.SMEM((groups, blocks), jnp.int32),
            pltpu.SMEM((4, blocks), jnp.int32),
            pltpu.VMEM((blocks * rows, width), bf16),
            pltpu.VMEM(rows_shape, bf16),
            pltpu.VMEM(rows_shape, bf16),
            pltpu.VMEM(rows_shape, bf16),
            pltpu.VMEM((rank, width), bf16),
            pltpu.VMEM((rank, heads * LANES), bf16),
            pltpu.VMEM(far_shape, bf16),
            pltpu.VMEM(rows_shape, bf16),
            pltpu.VMEM((blocks, rows, LANES), bf16),
            pltpu.SemaphoreType.DMA((7,)),
            pltpu.SemaphoreType.DMA((4,)),
        ],
        60_000_000,
        4_000_000,
        source_block_plan,
        flat,
        frozen_query_weight[0],
        source_keys[0],
        source_values[0],
        adapter_down_weight.T,
        adapter_up_weight,
        vmem_mib=60,
        out_specs=[ANY] * 3,
    )
    own_send = call(
        functools.partial(pack_own_kernel, dims),
        [(own_shape, bf16)] * heads
        + [((chips, blocks * rows, 3 * LANES), bf16), ((groups, rows, LANES), bf16)],
        [SMEM] + [VMEM] * 6,
        [],
        0,
        1_600_000,
        source_block_plan,
        source_keys[0],
        source_values[0],
        output_gradient[0],
        queries,
        adapter,
        flat,
    )
    feat_other = exchange(own_send[heads], "core", CORES, 1)
    own = [exchange(own_send[turn], SEQ, heads, turn) for turn in range(heads - 1, 0, -1)]
    own = [own_send[0]] + own[::-1]
    far = lax.all_to_all(far_send, everyone, 0, 0, tiled=True)
    attended = call(
        functools.partial(attend_kernel, dims),
        [((chips * groups, CORES + 1, rows, LANES), bf16)]
        + [((CORES, pairs, rows, LANES), bf16)] * chips
        + [((LANES, reach), bf16), ((1, 1, length), f32)],
        [SMEM] + [VMEM] * (4 + heads) + [ANY],
        [
            pltpu.VMEM((chips * groups, CORES + 1, rows, LANES), bf16),
            pltpu.VMEM((1, 1, length), f32),
            pltpu.SMEM((2, live), jnp.int32),
            pltpu.SemaphoreType.DMA((2,)),
        ]
        + [pltpu.VMEM((reach, LANES), bf16)] * 5,
        600_000_000,
        3_000_000,
        source_block_plan,
        segments,
        adapter_up_weight,
        own_send[heads + 1],
        far,
        *own,
        feat_other,
        out_specs=[ANY] + [VMEM] * (chips + 1) + [ANY],
    )
    own_parts = [
        exchange(attended[1 + turn], "chip", chips, turn) for turn in range(chips - 1, 0, -1)
    ]
    part = lax.all_to_all(attended[0], ("chip", "dp"), 0, 0, tiled=True)
    dquery, log_norm = attended[1 + chips :]
    tiles = groups + pairs
    (mine,) = call(
        head_sum_kernel,
        [((CORES * tiles + chips * groups, rows, LANES), bf16)],
        [VMEM] * (1 + chips),
        [],
        0,
        300_000,
        part,
        *own_parts,
        attended[1],
    )
    shares, up_part = call(
        functools.partial(product_kernel, dims),
        [((chips, HALF * 5 // 2, LANES), bf16), ((rank, LANES), bf16)],
        [SMEM] + [VMEM] * (5 + heads),
        [
            pltpu.VMEM((CORES, tiles, rows, LANES), f32),
            pltpu.VMEM((CORES, blocks, rows, LANES), f32),
            pltpu.VMEM((reach, LANES), bf16),
        ],
        60_000_000,
        2_000_000,
        source_block_plan,
        flat,
        feat_other,
        mine,
        exchange(mine, "core", CORES, 1),
        dquery,
        *own,
    )
    shares = lax.all_to_all(shares, "chip", 0, 0, tiled=True)
    (joined,) = call(
        join_kernel,
        [((HALF * 5 // 2 + rank, LANES), bf16)],
        [VMEM] * 2,
        [],
        0,
        600_000,
        shares,
        up_part,
    )
    sums = [joined] + [exchange(joined, "dp", groups, turn) for turn in range(1, groups)]
    down, up = call(
        functools.partial(total_kernel, 4.0 / math.sqrt(groups * length)),
        [((rank, width // heads), f32), ((rank, LANES), f32)],
        [VMEM] * groups,
        [pltpu.VMEM((groups,) + joined.shape, f32)],
        0,
        400_000,
        *sums,
    )
    return (down.T, up, log_norm)


def power_of_two(size):
    return size > 1 and size & (size - 1) == 0


def fits_tiles(mesh, features, adapter_up_weight):
    groups, heads = mesh.shape["dp"], mesh.shape["seq"]
    rows = features.shape[2] // heads
    return (
        rows % 16 == 0
        and features.shape[2] == LANES
        and features.shape[3] * 2 == heads * 5 * LANES
        and power_of_two(heads)
        and power_of_two(groups)
        and power_of_two(features.shape[1])
        and adapter_up_weight.shape == (HALF, heads * LANES)
    )


def split_mesh(mesh):
    groups, heads = mesh.shape["dp"], mesh.shape["seq"]
    devices = np.asarray(mesh.devices).reshape(groups, heads // CORES, CORES)
    return Mesh(devices, ("dp",) + SEQ)


def tiles_solution(mesh):
    row_spec = P("dp", None, SEQ, None)
    return jax.shard_map(
        per_device_tiles,
        mesh=split_mesh(mesh),
        in_specs=(row_spec,) * 5 + (P(), P(), P(), P("dp", None)),
        out_specs=(P(SEQ, None), P(None, SEQ), P("dp", SEQ, None)),
        check_vma=False,
    )


def attend_head(query, key_rows, value_rows, cotangent, segment, clip_count, reach_rows):
    length = query.shape[0]
    width = query.shape[1]
    piece_count = 8
    piece_rows = reach_rows // piece_count
    scaling = 1.0 / math.sqrt(width)
    query_padded = jnp.pad(query, ((0, reach_rows), (0, 0)))
    grad_padded = jnp.pad(cotangent, ((0, reach_rows), (0, 0)))
    keys_padded = jnp.pad(key_rows, ((0, reach_rows), (0, 0)))
    values_padded = jnp.pad(value_rows, ((0, reach_rows), (0, 0)))
    segment_padded = jnp.pad(segment, (0, reach_rows), constant_values=-1)
    clip_ids = jnp.arange(clip_count, dtype=jnp.int32)
    starts = jnp.sum((segment[None, :] < clip_ids[:, None]).astype(jnp.int32), axis=1)

    def piece_pass(piece_index):
        clip_slice = piece_index // piece_count
        start = lax.dynamic_index_in_dim(starts, clip_slice, 0, keepdims=False)
        query_start = start + piece_index % piece_count * piece_rows
        query_tile = lax.dynamic_slice_in_dim(query_padded, query_start, piece_rows, 0)
        grad_tile = lax.dynamic_slice_in_dim(grad_padded, query_start, piece_rows, 0)
        seg_tile = lax.dynamic_slice_in_dim(segment_padded, query_start, piece_rows, 0)
        key_tile = lax.dynamic_slice_in_dim(keys_padded, start, reach_rows, 0)
        value_tile = lax.dynamic_slice_in_dim(values_padded, start, reach_rows, 0)
        seg_cols = lax.dynamic_slice_in_dim(segment_padded, start, reach_rows, 0)
        in_clip = seg_tile == clip_slice
        allowed = in_clip[:, None] & (seg_cols == clip_slice)[None, :]
        scores = (
            lax.dot_general(
                query_tile, key_tile, (((1,), (1,)), ((), ())), preferred_element_type=jnp.float32
            )
            * scaling
        )
        scores = jnp.where(allowed, scores, -1e30)
        maximum = jnp.max(scores, axis=1, keepdims=True)
        exponent = jnp.where(allowed, jnp.exp(scores - maximum), 0.0)
        totals = jnp.where(in_clip[:, None], jnp.sum(exponent, axis=1, keepdims=True), 1.0)
        log_norm = jnp.where(in_clip, maximum[:, 0] + jnp.log(totals[:, 0]), 0.0)
        probs = exponent / totals
        weights = probs.astype(jnp.bfloat16)
        attended = jnp.dot(weights, value_tile, preferred_element_type=jnp.float32)
        delta = jnp.sum(grad_tile.astype(jnp.float32) * attended, axis=1, keepdims=True)
        dprob = lax.dot_general(
            grad_tile, value_tile, (((1,), (1,)), ((), ())), preferred_element_type=jnp.float32
        )
        dscore = (probs * (dprob - delta)).astype(jnp.bfloat16)
        query_gradient = (
            jnp.dot(dscore, key_tile, preferred_element_type=jnp.float32) * scaling
        ).astype(jnp.bfloat16)
        query_gradient = jnp.where(in_clip[:, None], query_gradient, jnp.zeros((), jnp.bfloat16))
        return (query_gradient, log_norm, query_start)

    total_pieces = piece_count * (clip_count - 1)
    dquery_pieces, log_pieces, piece_starts = lax.map(
        piece_pass, jnp.arange(total_pieces, dtype=jnp.int32)
    )

    def place(index, carry):
        grad_total, log_total = carry
        where_at = lax.dynamic_index_in_dim(piece_starts, index, 0, keepdims=False)
        grad_piece = lax.dynamic_index_in_dim(dquery_pieces, index, 0, keepdims=False)
        log_piece = lax.dynamic_index_in_dim(log_pieces, index, 0, keepdims=False)
        grad_old = lax.dynamic_slice_in_dim(grad_total, where_at, piece_rows, 0)
        log_old = lax.dynamic_slice_in_dim(log_total, where_at, piece_rows, 0)
        grad_total = lax.dynamic_update_slice_in_dim(grad_total, grad_old + grad_piece, where_at, 0)
        log_total = lax.dynamic_update_slice_in_dim(log_total, log_old + log_piece, where_at, 0)
        return (grad_total, log_total)

    grad_init = jnp.zeros((length + reach_rows, width), jnp.bfloat16)
    log_init = jnp.zeros((length + reach_rows,), jnp.float32)
    grad_total, log_total = lax.fori_loop(0, total_pieces, place, (grad_init, log_init))
    return (grad_total[:length], log_total[:length])


def routing_tables(source_block_plan, group_index, cap_slots):
    group_count, block_count = source_block_plan.shape
    source_group = source_block_plan // block_count
    source_local = source_block_plan % block_count
    dest_groups = jnp.arange(group_count, dtype=jnp.int32)[:, None]
    outgoing = (source_group == group_index) & (dest_groups != group_index)
    out_rank = jnp.cumsum(outgoing.astype(jnp.int32), axis=1) - 1
    slot_ids = jnp.arange(cap_slots, dtype=jnp.int32)
    chosen = outgoing[:, :, None] & (out_rank[:, :, None] == slot_ids[None, None, :])
    send_index = jnp.sum(jnp.where(chosen, source_local[:, :, None], 0), axis=1)
    send_valid = jnp.any(chosen, axis=1)
    own_group = lax.dynamic_index_in_dim(source_group, group_index, 0, keepdims=False)
    own_local = lax.dynamic_index_in_dim(source_local, group_index, 0, keepdims=False)
    incoming = own_group != group_index
    positions = jnp.arange(block_count, dtype=jnp.int32)
    earlier = (own_group[None, :] == own_group[:, None]) & (positions[None, :] < positions[:, None])
    in_rank = jnp.sum(earlier.astype(jnp.int32), axis=1)
    return (send_index, send_valid, incoming, own_group, in_rank, own_local)


def pack_blocks(local, send_index, send_valid):
    picked = jnp.take(local, send_index, axis=0)
    return jnp.where(send_valid[:, :, None, None], picked, jnp.zeros((), local.dtype))


def unpack_blocks(received, local, tables, cap_slots):
    incoming, own_group, in_rank, own_local = tables
    flat = received.reshape((-1,) + received.shape[2:])
    slot_index = jnp.where(incoming, own_group * cap_slots + in_rank, 0)
    remote = jnp.take(flat, slot_index, axis=0)
    staying = jnp.take(local, own_local, axis=0)
    return jnp.where(incoming[:, None, None], remote, staying)


def per_device(
    features,
    frozen_query_weight,
    source_keys,
    source_values,
    output_gradient,
    adapter_down_weight,
    adapter_up_weight,
    source_block_plan,
    segments,
):
    group_count = lax.axis_size("dp")
    group_index = lax.axis_index("dp")
    block_count = features.shape[1]
    feat_local = features[0]
    base_local = frozen_query_weight[0]
    keys_local = source_keys[0]
    values_local = source_values[0]
    send_index, send_valid, incoming, own_group, in_rank, own_local = routing_tables(
        source_block_plan, group_index, CAP
    )
    tables = (incoming, own_group, in_rank, own_local)
    contract_final_axis = (((2,), (0,)), ((), ()))
    shuffled = (
        lax.all_to_all(
            pack_blocks(feat_local, send_index, send_valid),
            "dp",
            split_axis=0,
            concat_axis=0,
            tiled=True,
        ),
        lax.all_to_all(
            pack_blocks(base_local, send_index, send_valid),
            "dp",
            split_axis=0,
            concat_axis=0,
            tiled=True,
        ),
        lax.all_to_all(
            pack_blocks(keys_local, send_index, send_valid),
            "dp",
            split_axis=0,
            concat_axis=0,
            tiled=True,
        ),
        lax.all_to_all(
            pack_blocks(values_local, send_index, send_valid),
            "dp",
            split_axis=0,
            concat_axis=0,
            tiled=True,
        ),
    )
    feature_dest = unpack_blocks(shuffled[0], feat_local, tables, CAP)
    base_query_dest = unpack_blocks(shuffled[1], base_local, tables, CAP)
    keys_dest = unpack_blocks(shuffled[2], keys_local, tables, CAP)
    values_dest = unpack_blocks(shuffled[3], values_local, tables, CAP)
    adapter_params = lax.dot_general(
        feature_dest, adapter_down_weight, contract_final_axis, preferred_element_type=jnp.float32
    ).astype(jnp.bfloat16)
    query_rows = (
        base_query_dest.astype(jnp.float32)
        + lax.dot_general(
            adapter_params,
            adapter_up_weight,
            contract_final_axis,
            preferred_element_type=jnp.float32,
        )
    ).astype(jnp.bfloat16)
    head_query, head_keys, head_values, head_grads = (
        lax.all_to_all(query_rows, "seq", split_axis=2, concat_axis=1, tiled=True),
        lax.all_to_all(keys_dest, "seq", split_axis=2, concat_axis=1, tiled=True),
        lax.all_to_all(values_dest, "seq", split_axis=2, concat_axis=1, tiled=True),
        lax.all_to_all(output_gradient[0], "seq", split_axis=2, concat_axis=1, tiled=True),
    )
    length = head_query.shape[0] * head_query.shape[1]
    reach_rows = length // 2 + length // 8
    head_width = head_query.shape[2]
    segment = segments[0]
    head_query = head_query.reshape(length, head_width)
    head_keys = head_keys.reshape(length, head_width)
    head_values = head_values.reshape(length, head_width)
    head_grads = head_grads.reshape(length, head_width)
    dquery_head, log_head = attend_head(
        head_query, head_keys, head_values, head_grads, segment, CLIPS, reach_rows
    )
    norm_pieces = [log_head]
    log_norm = jnp.stack(norm_pieces, axis=0)
    query_gradient = lax.all_to_all(
        dquery_head.reshape(block_count, length // block_count, head_width),
        "seq",
        split_axis=1,
        concat_axis=2,
        tiled=True,
    )
    adapter_gradient = lax.dot_general(
        query_gradient,
        adapter_up_weight,
        (((2,), (1,)), ((), ())),
        preferred_element_type=jnp.float32,
    ).astype(jnp.bfloat16)
    contract_tokens = (((0, 1), (0, 1)), ((), ()))
    down_part = lax.dot_general(
        feature_dest, adapter_gradient, contract_tokens, preferred_element_type=jnp.float32
    )
    up_part = lax.dot_general(
        adapter_params, query_gradient, contract_tokens, preferred_element_type=jnp.float32
    )
    down_share, up_share = (
        lax.psum_scatter(down_part, "seq", scatter_dimension=0, tiled=True),
        lax.psum_scatter(up_part, "seq", scatter_dimension=1, tiled=True),
    )
    down_total, up_total = lax.psum((down_share, up_share), "dp")
    grad_norm = 4.0 / math.sqrt(group_count * length)
    return (down_total * grad_norm, up_total * grad_norm, log_norm[None])


def solution(mesh):
    in_specs = (
        P("dp", None, "seq", None),
        P("dp", None, "seq", None),
        P("dp", None, "seq", None),
        P("dp", None, "seq", None),
        P("dp", None, "seq", None),
        P(),
        P(),
        P(),
        P("dp", None),
    )
    out_specs = (P("seq", None), P(None, "seq"), P("dp", "seq", None))

    plain = jax.shard_map(
        per_device, mesh=mesh, in_specs=in_specs, out_specs=out_specs, check_vma=False
    )

    def whole(features, *rest):
        fits = fits_tiles(mesh, features, rest[5])
        return (tiles_solution(mesh) if fits else plain)(features, *rest)

    return whole
```
